256 devices in a mesh: band: 16 (over y, x), head: 16 (over z, core).
Axes of the slice: x: 4, y: 4, z: 8, core: 2. Of those that a mesh axis runs over, the one named last changes fastest.
Arguments:
- grid_latent: bfloat16 [65536, 1024], P('band'), may hold values from -6 to 6
- node_latent: bfloat16 [8192, 1024], P(('band', 'head')), may hold values from -6 to 6
- src_index: int32 [8192, 32], P('band'), may hold values from 0 to 65535, as said below
- in_degree: int32 [8192], P('band'), may hold values from 4 to 32, as said below
- node_order: int32 [8192], P('band'), may hold values from 0 to 8191, as said below
- norm_gains: float32 [6, 1024], replicated, may hold values from 0.1 to 1.9
- enc_wq: bfloat16 [1024, 1024], P(None, 'head'), may hold values from -0.1875 to 0.1875
- enc_wkv: bfloat16 [2, 1024, 1024], P(None, None, 'head'), may hold values from -0.1875 to 0.1875
- enc_wo: bfloat16 [1024, 1024], P('head'), may hold values from -0.1875 to 0.1875
- proc_wqkv: bfloat16 [2, 3, 1024, 1024], P(None, None, None, 'head'), may hold values from -0.1875 to 0.1875
- proc_wo: bfloat16 [2, 1024, 1024], P(None, 'head'), may hold values from -0.1875 to 0.1875
- w_up: bfloat16 [2, 1024, 4096], P(None, None, 'head'), may hold values from -0.1875 to 0.1875
- w_down: bfloat16 [2, 4096, 1024], P(None, 'head'), may hold values from -0.09375 to 0.09375
Outputs:
- processed: bfloat16 [8192, 1024], P(('band', 'head'))
The draws below stay inside these ranges and needn't reach their ends.
Inputs may be any that keep to these rules, and one draw needn't show every extreme that they name: `src_index`: for node t of band b = t // 512, every source lies in rows b * 4096 - 1440 to (b + 1) * 4096 + 1439; sources cluster around the node's latitude. `in_degree`: nodes near the poles have more incoming edges than nodes near the equator. `node_order`: the 512 entries of band b hold each of the numbers b * 512 to (b + 1) * 512 - 1 once.
All inputs are finite; a program needn't handle non-finite values.
Results may differ from the reference program's by a relative error of at most 0.035.
Values may be sent and summed in bfloat16 or wider, within the bound.
No kernel may reach another device: no remote copies, remote signals or barrier semaphores. Data moves between devices by JAX's collectives and lax.ppermute only.
A program may use at most 128 MiB of HBM per device.

```python
import math
import jax
import jax.numpy as jnp
from jax import lax

D = 1024
HEADS = 16
FF = 4096
HEAD_DIM = 64
G_DEV = 4096
NODE_DEV = 512
K_MAX = 32
RIM = 1440
HALF_WIN = 512
LAYERS = 2
GRID = 65536
NODES = 8192


def draw_src_index(key, part):
    key = jax.random.fold_in(key, 11)
    node_ids = jnp.arange(NODES, dtype=jnp.int32)
    band_ids = node_ids // NODE_DEV
    local_ids = node_ids % NODE_DEV
    centre_row = band_ids * G_DEV + local_ids * G_DEV // NODE_DEV
    offsets = jax.random.randint(key, (NODES, K_MAX), -RIM, RIM + 1, dtype=jnp.int32)
    sources = jnp.clip(centre_row[:, None] + offsets, 0, GRID - 1)
    lower_end = jnp.maximum(band_ids * G_DEV - RIM, 0)
    upper_end = jnp.minimum((band_ids + 1) * G_DEV + RIM - 1, GRID - 1)
    first_slot = jnp.where(local_ids == 0, lower_end, jnp.where(local_ids == NODE_DEV - 1, upper_end, sources[:, 0]))
    return jnp.concatenate([first_slot[:, None], sources[:, 1:]], axis=1).astype(jnp.int32)


def draw_in_degree(key, part):
    key = jax.random.fold_in(key, 23)
    node_ids = jnp.arange(NODES, dtype=jnp.int32)
    distance = jnp.abs(2 * node_ids + 1 - NODES)
    ceiling = K_MAX // 4 + (K_MAX - K_MAX // 4) * distance // NODES
    lowest = jnp.maximum(ceiling // 2, 1)
    degrees = jax.random.randint(key, (NODES,), lowest, ceiling + 1, dtype=jnp.int32)
    degrees = jnp.where(node_ids == 0, K_MAX, degrees)
    degrees = jnp.where(node_ids == NODES // 2, max(1, K_MAX // 8), degrees)
    return degrees.astype(jnp.int32)


def shuffle_band(band_key):
    return jax.random.permutation(band_key, NODE_DEV).astype(jnp.int32)


def draw_node_order(key, part):
    key = jax.random.fold_in(key, 37)
    band_keys = jax.random.split(key, NODES // NODE_DEV)
    shuffled = jax.vmap(shuffle_band)(band_keys)
    offsets_base = (jnp.arange(NODES // NODE_DEV, dtype=jnp.int32) * NODE_DEV)[:, None]
    return (shuffled + offsets_base).reshape(NODES).astype(jnp.int32)


def block_scale(stream_key, extent, cuts, smallest, high):
    def one(dim, shards_of):
        steps = jax.random.uniform(jax.random.fold_in(jax.random.fold_in(stream_key, 6), dim), (shards_of,), jnp.float32, smallest / len(cuts), high / len(cuts))
        return jnp.repeat(jnp.exp(steps), extent[dim] // shards_of).reshape((-1,) + (1,) * (len(extent) - dim - 1))

    level = one(*cuts[0])
    for cut in cuts[1:]:
        level = level * one(*cut)
    return level


def gaussian(key, extent, width, bound, shards=(), kind=jnp.bfloat16):
    level = block_scale(key, extent, shards, -0.22, 0.18) if shards else 1.0
    entries = jax.random.normal(key, extent, jnp.float32) * width * level
    return jnp.minimum(jnp.maximum(entries, -bound), bound).astype(kind)


def setup_inputs(seed: int = 0) -> dict:
    seeds = jax.random.split(jax.random.key(seed), 14)
    grid_latent = gaussian(seeds[0], (GRID, D), 1.0, 6.0, ((0, 16),))
    node_latent = gaussian(seeds[1], (NODES, D), 1.0, 6.0, ((0, 256),))
    src_index = draw_src_index(jax.random.fold_in(seeds[13], 71), 0)
    in_degree = draw_in_degree(jax.random.fold_in(seeds[13], 71), 0)
    node_order = draw_node_order(jax.random.fold_in(seeds[13], 71), 0)
    norm_gains = jnp.clip(1.0 + 0.18 * jax.random.normal(seeds[5], (2 + 2 * LAYERS, D), jnp.float32), 0.1, 1.9)
    enc_wq = gaussian(seeds[6], (D, D), D ** -0.5, 0.1875, ((1, 16),))
    enc_wkv = gaussian(seeds[7], (2, D, D), D ** -0.5, 0.1875, ((2, 16),))
    enc_wo = gaussian(seeds[8], (D, D), D ** -0.5, 0.1875, ((0, 16),))
    proc_wqkv = gaussian(seeds[9], (LAYERS, 3, D, D), D ** -0.5, 0.1875, ((3, 16),))
    proc_wo = gaussian(seeds[10], (LAYERS, D, D), D ** -0.5, 0.1875, ((1, 16),))
    w_up = gaussian(seeds[11], (LAYERS, D, FF), D ** -0.5, 0.1875, ((2, 16),))
    w_down = gaussian(seeds[12], (LAYERS, FF, D), FF ** -0.5, 0.09375, ((1, 16),))
    return {"grid_latent": grid_latent, "node_latent": node_latent, "src_index": src_index, "in_degree": in_degree, "node_order": node_order, "norm_gains": norm_gains, "enc_wq": enc_wq, "enc_wkv": enc_wkv, "enc_wo": enc_wo, "proc_wqkv": proc_wqkv, "proc_wo": proc_wo, "w_up": w_up, "w_down": w_down}


def layer_norm(row_data, gain_row):
    values = row_data.astype(jnp.float32)
    row_mean = lax.optimization_barrier(jnp.mean(values, axis=-1, keepdims=True))
    centred = values - row_mean
    variance = lax.optimization_barrier(jnp.mean(centred * centred, axis=-1, keepdims=True))
    return centred * lax.rsqrt(variance + 1e-05) * gain_row.astype(jnp.float32)

def window_heads(queries, keys_pad, values_pad, total_nodes):
    n_rows = queries.shape[0]
    head_size = HEAD_DIM
    query_block = min(512, n_rows)
    key_span = query_block + 2 * HALF_WIN
    score_scale = 1.0 / math.sqrt(head_size)

    def one_block(block_start):
        query_rows = lax.dynamic_slice_in_dim(queries, block_start, query_block, 0)
        key_rows = lax.dynamic_slice_in_dim(keys_pad, block_start, key_span, 0)
        value_rows = lax.dynamic_slice_in_dim(values_pad, block_start, key_span, 0)
        query_rows = query_rows.reshape(query_block, HEADS, head_size).astype(jnp.float32)
        key_rows = key_rows.reshape(key_span, HEADS, head_size).astype(jnp.float32)
        value_rows = value_rows.reshape(key_span, HEADS, head_size).astype(jnp.float32)
        scores = jnp.einsum('qhd,khd->hqk', query_rows, key_rows, precision=lax.Precision.HIGHEST) * score_scale
        offset_grid = jnp.arange(key_span, dtype=jnp.int32)[None, :] - jnp.arange(query_block, dtype=jnp.int32)[:, None]
        key_position = block_start - HALF_WIN + jnp.arange(key_span, dtype=jnp.int32)
        in_window = (offset_grid >= 0) & (offset_grid < 2 * HALF_WIN) & (key_position >= 0)[None, :] & (key_position < total_nodes)[None, :]
        exp_scores = jnp.where(in_window[None], jnp.exp(scores), jnp.float32(0.0))
        weights = (exp_scores / lax.optimization_barrier(jnp.sum(exp_scores, axis=-1, keepdims=True))).astype(jnp.bfloat16)
        attended = jnp.einsum('hqk,khd->qhd', weights.astype(jnp.float32), value_rows, precision=lax.Precision.HIGHEST)
        return attended.astype(jnp.bfloat16).reshape(query_block, HEADS * head_size)
    block_starts = jnp.arange(n_rows // query_block, dtype=jnp.int32) * query_block
    return lax.map(one_block, block_starts).reshape(n_rows, HEADS * head_size)

def reference(grid_latent, node_latent, src_index, in_degree, node_order, norm_gains, enc_wq, enc_wkv, enc_wo, proc_wqkv, proc_wo, w_up, w_down):
    score_scale = 1.0 / math.sqrt(HEAD_DIM)
    grid_normed = layer_norm(grid_latent, norm_gains[0]).astype(jnp.bfloat16)
    grid_keys = jnp.dot(grid_normed, enc_wkv[0], preferred_element_type=jnp.float32).astype(jnp.bfloat16)
    grid_values = jnp.dot(grid_normed, enc_wkv[1], preferred_element_type=jnp.float32).astype(jnp.bfloat16)
    node_normed = layer_norm(node_latent, norm_gains[1]).astype(jnp.bfloat16)
    enc_query = jnp.dot(node_normed, enc_wq, preferred_element_type=jnp.float32).astype(jnp.bfloat16)

    def encode(block_index):
        first_row = (block_index * NODE_DEV).astype(jnp.int32)
        sources = lax.dynamic_slice_in_dim(src_index, first_row, NODE_DEV, 0)
        degrees = lax.dynamic_slice_in_dim(in_degree, first_row, NODE_DEV, 0)
        query_rows = lax.dynamic_slice_in_dim(enc_query, first_row, NODE_DEV, 0)
        query_rows = query_rows.reshape(NODE_DEV, HEADS, HEAD_DIM).astype(jnp.float32)
        key_rows = jnp.take(grid_keys, sources, axis=0).reshape(NODE_DEV, K_MAX, HEADS, HEAD_DIM).astype(jnp.float32)
        value_rows = jnp.take(grid_values, sources, axis=0).reshape(NODE_DEV, K_MAX, HEADS, HEAD_DIM).astype(jnp.float32)
        scores = jnp.einsum('nhd,nkhd->nhk', query_rows, key_rows, precision=lax.Precision.HIGHEST) * score_scale
        used = jnp.arange(K_MAX, dtype=jnp.int32)[None, None, :] < degrees[:, None, None]
        exp_scores = jnp.where(used, jnp.exp(scores), jnp.float32(0.0))
        weights = (exp_scores / lax.optimization_barrier(jnp.sum(exp_scores, axis=-1, keepdims=True))).astype(jnp.bfloat16)
        attended = jnp.einsum('nhk,nkhd->nhd', weights.astype(jnp.float32), value_rows, precision=lax.Precision.HIGHEST)
        return attended.astype(jnp.bfloat16).reshape(NODE_DEV, D)
    enc_heads = lax.map(encode, jnp.arange(NODES // NODE_DEV, dtype=jnp.int32)).reshape(NODES, D)
    mapped = (node_latent.astype(jnp.float32) + jnp.dot(enc_heads, enc_wo, preferred_element_type=jnp.float32)).astype(jnp.bfloat16)
    stream = jnp.take(mapped, node_order, axis=0)
    for layer_index in range(LAYERS):
        normed = layer_norm(stream, norm_gains[2 + 2 * layer_index]).astype(jnp.bfloat16)
        queries = jnp.dot(normed, proc_wqkv[layer_index, 0], preferred_element_type=jnp.float32).astype(jnp.bfloat16)
        keys_all = jnp.dot(normed, proc_wqkv[layer_index, 1], preferred_element_type=jnp.float32).astype(jnp.bfloat16)
        values_all = jnp.dot(normed, proc_wqkv[layer_index, 2], preferred_element_type=jnp.float32).astype(jnp.bfloat16)
        keys_pad = jnp.pad(keys_all, ((HALF_WIN, HALF_WIN), (0, 0)))
        values_pad = jnp.pad(values_all, ((HALF_WIN, HALF_WIN), (0, 0)))
        win_heads = window_heads(queries, keys_pad, values_pad, NODES)
        stream = (stream.astype(jnp.float32) + jnp.dot(win_heads, proc_wo[layer_index], preferred_element_type=jnp.float32)).astype(jnp.bfloat16)
        normed_two = layer_norm(stream, norm_gains[3 + 2 * layer_index]).astype(jnp.bfloat16)
        hidden = jax.nn.gelu(jnp.dot(normed_two, w_up[layer_index], preferred_element_type=jnp.float32)).astype(jnp.bfloat16)
        stream = (stream.astype(jnp.float32) + jnp.dot(hidden, w_down[layer_index], preferred_element_type=jnp.float32)).astype(jnp.bfloat16)
    return stream
```

```python
import functools
import math

import jax
import jax.numpy as jnp
from jax import lax
from jax.experimental import pallas as pl
from jax.experimental.pallas import tpu as pltpu
from jax.sharding import PartitionSpec as P

HEAD_DIM = 64
K_MAX = 32
HALF_WIN = 512
LAYERS = 2
EDGE = 1536
KV_BLOCK = 512
BLOCK = 32
GROUP = 128
NODES_HERE = 512
KEYS = 7168
SCALE = 1.0 / math.sqrt(HEAD_DIM)
BF = jnp.bfloat16
F32 = jnp.float32
NT = (((1,), (1,)), ((), ()))


def vm(limit_mib=32):
    return pltpu.CompilerParams(vmem_limit_bytes=limit_mib * 1024 * 1024)


def cost(flops, nbytes):
    return pl.CostEstimate(flops=int(flops), bytes_accessed=int(nbytes), transcendentals=0)


def whole():
    return pl.BlockSpec(memory_space=pltpu.VMEM)


def smem():
    return pl.BlockSpec(memory_space=pltpu.SMEM)


def sds(shape, dtype=BF):
    return jax.ShapeDtypeStruct(shape, dtype)


def swap(x):
    return lax.ppermute(x, "head", [(i, i ^ 1) for i in range(16)])


def shift_z(x, k):
    return lax.ppermute(x, "head", [(i, ((i // 2 + k) % 8) * 2 + i % 2) for i in range(16)])


def outward_pairs():
    return [(2 * z + c, 2 * ((z + (1 if c else -1)) % 8) + c) for z in range(8) for c in range(2)]


def outward(x):
    return lax.ppermute(x, "head", outward_pairs())


def inward(x):
    return lax.ppermute(x, "head", [(t, s) for s, t in outward_pairs()])


def crossed(x):
    pairs = [(2 * z, 2 * ((z - 1) % 8) + 1) for z in range(8)]
    return lax.ppermute(x, "head", pairs + [(t, s) for s, t in pairs])


def up_band(x):
    return lax.ppermute(x, "band", [(i, i + 1) for i in range(15)])


def down_band(x):
    return lax.ppermute(x, "band", [(i + 1, i) for i in range(15)])


def gather_group(x):
    behind = shift_z(x, 2)
    ahead = shift_z(x, -2)
    far = shift_z(x, 4)
    return [x, ahead, far, behind]


def scatter_group(parts):
    return [parts[0], shift_z(parts[1], 2), shift_z(parts[2], 4), shift_z(parts[3], -2)]


def four_shards(x):
    third = outward(x)
    return [x, swap(x), third, swap(third)]


def exchange(pieces):
    return [pieces[0], swap(pieces[1]), inward(pieces[2]), crossed(pieces[3])]


def give_back(pieces):
    return [pieces[0], swap(pieces[1]), outward(pieces[2]), crossed(pieces[3])]


def normed_rows(values, gain):
    mean = jnp.mean(values, axis=-1, keepdims=True)
    centred = values - mean
    variance = jnp.mean(centred * centred, axis=-1, keepdims=True)
    return (centred * lax.rsqrt(variance + 1e-05) * gain).astype(BF)


def grid_kv_body(x_ref, gain_ref, w_ref, w_both):
    @pl.when(pl.program_id(0) == 0)
    def _():
        w_both[:, :HEAD_DIM] = w_ref[0]
        w_both[:, HEAD_DIM:] = w_ref[1]

    normed = normed_rows(x_ref[...].astype(F32), gain_ref[0:1, :])
    return jnp.dot(normed, w_both[...], preferred_element_type=F32).astype(BF)


def grid_kv_edges_kernel(x_ref, gain_ref, w_ref, low_ref, high_ref, w_both):
    out = grid_kv_body(x_ref, gain_ref, w_ref, w_both)
    half = EDGE // KV_BLOCK

    @pl.when(pl.program_id(0) < half)
    def _():
        low_ref[...] = out

    @pl.when(pl.program_id(0) >= half)
    def _():
        high_ref[...] = out


def grid_kv_middle_kernel(x_ref, gain_ref, w_ref, out_ref, w_both):
    out_ref[...] = grid_kv_body(x_ref, gain_ref, w_ref, w_both)


def grid_kv_edges(grid_latent, gains, w):
    d = grid_latent.shape[1]
    half = EDGE // KV_BLOCK
    skip = grid_latent.shape[0] // KV_BLOCK - 2 * half
    return pl.pallas_call(
        grid_kv_edges_kernel,
        grid=(2 * half,),
        in_specs=[
            pl.BlockSpec((KV_BLOCK, d), lambda i: (jnp.where(i < half, i, i + skip), 0)),
            pl.BlockSpec(gains.shape, lambda i: (0, 0)),
            pl.BlockSpec(w.shape, lambda i: (0, 0, 0)),
        ],
        out_specs=[
            pl.BlockSpec((KV_BLOCK, 128), lambda i: (jnp.minimum(i, half - 1), 0)),
            pl.BlockSpec((KV_BLOCK, 128), lambda i: (jnp.maximum(i - half, 0), 0)),
        ],
        out_shape=[sds((EDGE, 128)), sds((EDGE, 128))],
        scratch_shapes=[pltpu.VMEM((d, 128), BF)],
        compiler_params=vm(),
        cost_estimate=cost(2 * 3072 * d * 128, 3072 * d * 2),
        name="grid_kv_edges",
    )(grid_latent, gains, w)


def grid_kv_middle(grid_latent, gains, w):
    d = grid_latent.shape[1]
    half = EDGE // KV_BLOCK
    rows = grid_latent.shape[0] - 2 * EDGE
    return pl.pallas_call(
        grid_kv_middle_kernel,
        grid=(rows // KV_BLOCK,),
        in_specs=[
            pl.BlockSpec((KV_BLOCK, d), lambda i: (i + half, 0)),
            pl.BlockSpec(gains.shape, lambda i: (0, 0)),
            pl.BlockSpec(w.shape, lambda i: (0, 0, 0)),
        ],
        out_specs=pl.BlockSpec((KV_BLOCK, 128), lambda i: (i, 0)),
        out_shape=sds((rows, 128)),
        scratch_shapes=[pltpu.VMEM((d, 128), BF)],
        compiler_params=vm(),
        cost_estimate=cost(2 * 1024 * d * 128, 1024 * d * 2),
        name="grid_kv_middle",
    )(grid_latent, gains, w)


COUNT_STEP = 64
TILES = KEYS // 128


def edge_count_kernel(high_ref, low_ref, out_ref):
    row_high = lax.broadcasted_iota(jnp.int32, (TILES * 8, 256), 0)
    row_low = lax.broadcasted_iota(jnp.int32, (128, 256), 0)

    def counts(group):
        left = jnp.where(row_high == high_ref[pl.ds(group, 1), :], 1.0, 0.0).astype(BF)
        right = jnp.where(row_low == low_ref[pl.ds(group, 1), :], 1.0, 0.0).astype(BF)
        return lax.dot_general(left, right, NT, preferred_element_type=F32)

    def pair(i, carry):
        first = counts(2 * i)
        second = counts(2 * i + 1)
        rows = pl.ds(pl.multiple_of(i * 16, 16), 16)
        for t in range(TILES):
            both = jnp.concatenate([first[t * 8 : t * 8 + 8], second[t * 8 : t * 8 + 8]], axis=0)
            out_ref[rows, t * 128 : (t + 1) * 128] = both.astype(BF)
        return carry

    lax.fori_loop(0, COUNT_STEP // 16, pair, 0)


def edge_counts(high_key, low_key):
    return pl.pallas_call(
        edge_count_kernel,
        grid=(NODES_HERE // COUNT_STEP,),
        in_specs=[
            pl.BlockSpec((COUNT_STEP // 8, 256), lambda i: (i, 0)),
            pl.BlockSpec((COUNT_STEP // 8, 256), lambda i: (i, 0)),
        ],
        out_specs=pl.BlockSpec((COUNT_STEP, KEYS), lambda i: (i, 0)),
        out_shape=sds((NODES_HERE, KEYS)),
        compiler_params=vm(),
        cost_estimate=cost(4e9, 10e6),
        name="edge_counts",
    )(high_key, low_key)


def node_query_kernel(b0, b1, b2, b3, gain_ref, w0, w1, w2, w3, q0, q1, q2, q3):
    rows = jnp.concatenate([b0[...], b1[...], b2[...], b3[...]], axis=0).astype(F32)
    normed = normed_rows(rows, gain_ref[1:2, :])
    for w, q in ((w0, q0), (w1, q1), (w2, q2), (w3, q3)):
        q[...] = lax.dot_general(normed, w[HEAD_DIM:, :], NT, preferred_element_type=F32).astype(BF)


def node_queries(blocks, gains, enc_shards):
    return pl.pallas_call(
        node_query_kernel,
        in_specs=[whole()] * 9,
        out_specs=[whole()] * 4,
        out_shape=[sds((GROUP, HEAD_DIM))] * 4,
        compiler_params=vm(),
        cost_estimate=cost(7e7, 1e6),
        name="node_queries",
    )(*blocks, gains, *enc_shards)


T_STEP = 128
CHUNK = 512


def edge_attention_kernel(
    blk_ref, q0, q1, q2, q3, kv0, kv1, kv2, kv3, kv4, count_ref, order_ref,
    o0, o1, o2, o3, q_all, scores, heads, pick,
):
    step = pl.program_id(0)

    @pl.when(step == 0)
    def _():
        for g, q in enumerate((q0, q1, q2, q3)):
            for k in range(4):
                start = pl.multiple_of(blk_ref[g * 4 + k] * BLOCK, BLOCK)
                q_all[pl.ds(start, BLOCK), :] = q[k * BLOCK : (k + 1) * BLOCK, :]

    q = q_all[pl.ds(pl.multiple_of(step * T_STEP, T_STEP), T_STEP), :]
    chunks = []
    for kv in (kv0, kv1, kv2, kv3, kv4):
        for start in range(0, kv.shape[0], CHUNK):
            chunks.append((kv, start))
    top = None
    for i, (kv, start) in enumerate(chunks):
        keys = kv[start : start + CHUNK, :][:, :HEAD_DIM]
        s = lax.dot_general(q, keys, NT, preferred_element_type=F32) * SCALE
        cols = slice(i * CHUNK, (i + 1) * CHUNK)
        s = jnp.where(count_ref[:, cols].astype(F32) > 0.0, s, -jnp.inf)
        scores[:, cols] = s
        part = jnp.maximum(
            jnp.maximum(s[:, 0:128], s[:, 128:256]), jnp.maximum(s[:, 256:384], s[:, 384:512])
        )
        top = part if top is None else jnp.maximum(top, part)
    top = jnp.max(top, axis=-1, keepdims=True)
    total = jnp.zeros((T_STEP, 128), F32)
    out = jnp.zeros((T_STEP, 128), F32)
    for i, (kv, start) in enumerate(chunks):
        cols = slice(i * CHUNK, (i + 1) * CHUNK)
        e = jnp.exp(scores[:, cols] - top) * count_ref[:, cols].astype(F32)
        total += (e[:, 0:128] + e[:, 128:256]) + (e[:, 256:384] + e[:, 384:512])
        out += jnp.dot(e.astype(BF), kv[start : start + CHUNK, :], preferred_element_type=F32)
    total = jnp.sum(total, axis=-1, keepdims=True)
    rows = pl.ds(pl.multiple_of(step * T_STEP, T_STEP), T_STEP)
    heads[rows, :] = (out / total).astype(BF)

    @pl.when(step == pl.num_programs(0) - 1)
    def _():
        node = lax.broadcasted_iota(jnp.int32, (BLOCK, NODES_HERE), 1)
        for g, o in enumerate((o0, o1, o2, o3)):
            for k in range(4):
                start = pl.multiple_of(blk_ref[g * 4 + k] * BLOCK, BLOCK)
                wanted = order_ref[pl.ds(start, BLOCK), :]
                pick[k * BLOCK : (k + 1) * BLOCK, :] = jnp.where(node == wanted, 1.0, 0.0).astype(BF)
            taken = jnp.dot(pick[...], heads[...], preferred_element_type=F32)
            o[...] = taken[:, HEAD_DIM:].astype(BF)


def edge_attention(blk, queries, kv_parts, counts, order_col):
    def full(x):
        return pl.BlockSpec(x.shape, lambda i: (0,) * x.ndim)

    return pl.pallas_call(
        edge_attention_kernel,
        grid=(NODES_HERE // T_STEP,),
        in_specs=[smem()]
        + [full(q) for q in queries]
        + [full(kv) for kv in kv_parts]
        + [pl.BlockSpec((T_STEP, KEYS), lambda i: (i, 0)), full(order_col)],
        out_specs=[pl.BlockSpec((GROUP, HEAD_DIM), lambda i: (0, 0))] * 4,
        out_shape=[sds((GROUP, HEAD_DIM))] * 4,
        scratch_shapes=[
            pltpu.VMEM((NODES_HERE, HEAD_DIM), BF),
            pltpu.VMEM((T_STEP, KEYS), F32),
            pltpu.VMEM((NODES_HERE, 128), BF),
            pltpu.VMEM((GROUP, NODES_HERE), BF),
        ],
        compiler_params=vm(40),
        cost_estimate=cost(2e9, 12e6),
        name="edge_attention",
    )(blk, *queries, *kv_parts, counts, order_col)


def head_sum_kernel(h0, h1, h2, h3, w0, w1, w2, w3, p0, p1, p2, p3):
    heads = jnp.concatenate([h0[...], h1[...], h2[...], h3[...]], axis=1)
    rows = jnp.concatenate([w0[...], w1[...], w2[...], w3[...]], axis=0)
    total = jnp.dot(heads, rows, preferred_element_type=F32).astype(BF)
    for k, p in enumerate((p0, p1, p2, p3)):
        p[...] = total[k * BLOCK : (k + 1) * BLOCK]


def head_sum(heads, shards, row_block):
    d = shards[0].shape[1]
    full = pl.BlockSpec((GROUP, HEAD_DIM), lambda i: (0, 0))
    return pl.pallas_call(
        head_sum_kernel,
        grid=(1,),
        in_specs=[full] * 4 + [pl.BlockSpec((HEAD_DIM, d), lambda i: (row_block, 0))] * 4,
        out_specs=[pl.BlockSpec((BLOCK, d), lambda i: (0, 0))] * 4,
        out_shape=[sds((BLOCK, d))] * 4,
        compiler_params=vm(),
        cost_estimate=cost(7e7, 1e6),
        name="head_sum",
    )(*heads, *shards)


def close_sum_kernel(gain_row, r_ref, p0, p1, p2, p3, gain_ref, stream_ref, normed_ref):
    total = (p0[...].astype(F32) + p1[...].astype(F32)) + (p2[...].astype(F32) + p3[...].astype(F32))
    stream = (r_ref[...].astype(F32) + total).astype(BF)
    stream_ref[...] = stream
    normed_ref[...] = normed_rows(stream.astype(F32), gain_ref[gain_row : gain_row + 1, :])


def close_sum(residual, parts, gains, gain_row):
    shape = residual.shape
    return pl.pallas_call(
        functools.partial(close_sum_kernel, gain_row),
        in_specs=[whole()] * 6,
        out_specs=[whole()] * 2,
        out_shape=[sds(shape), sds(shape)],
        compiler_params=vm(),
        cost_estimate=cost(1e6, 4e5),
        name="close_sum",
    )(residual, *parts, gains)


def final_sum_kernel(r_ref, p0, p1, p2, p3, stream_ref):
    total = (p0[...].astype(F32) + p1[...].astype(F32)) + (p2[...].astype(F32) + p3[...].astype(F32))
    stream_ref[...] = (r_ref[...].astype(F32) + total).astype(BF)


def final_sum(residual, parts):
    return pl.pallas_call(
        final_sum_kernel,
        in_specs=[whole()] * 5,
        out_specs=whole(),
        out_shape=sds(residual.shape),
        compiler_params=vm(),
        cost_estimate=cost(1e6, 4e5),
        name="final_sum",
    )(residual, *parts)


def qkv_kernel(b0, b1, b2, b3, *refs):
    rows = jnp.concatenate([b0[...], b1[...], b2[...], b3[...]], axis=0)
    for i in range(4):
        out = refs[8 + i]
        out[:, :128] = jnp.dot(rows, refs[2 * i][...], preferred_element_type=F32).astype(BF)
        out[:, 128:] = jnp.dot(rows, refs[2 * i + 1][...], preferred_element_type=F32).astype(BF)


def qkv(blocks, shards, layer):
    d = blocks[0].shape[1]
    weight_specs = []
    weights = []
    for shard in shards:
        weight_specs.append(pl.BlockSpec((d, 128), lambda i: (0, 4 + 2 * layer)))
        weight_specs.append(pl.BlockSpec((d, 128), lambda i: (0, 5)))
        weights += [shard, shard]
    return pl.pallas_call(
        qkv_kernel,
        grid=(1,),
        in_specs=[pl.BlockSpec((BLOCK, d), lambda i: (0, 0))] * 4 + weight_specs,
        out_specs=[pl.BlockSpec((GROUP, 256), lambda i: (0, 0))] * 4,
        out_shape=[sds((GROUP, 256))] * 4,
        compiler_params=vm(),
        cost_estimate=cost(3e8, 2.5e6),
        name="qkv",
    )(*blocks, *weights)


def window_kernel(layer, flag_ref, a0, a1, a2, a3, kv_ref, low_ref, high_ref, pos_col, pos_row, o0, o1, o2, o3):
    kv = kv_ref[...]
    low = low_ref[...]
    high = high_ref[...]
    has_low = flag_ref[0] > 0
    has_high = flag_ref[1] > 0
    col = pos_row[...]
    first = HEAD_DIM * layer
    for g, (a, o) in enumerate(((a0, o0), (a1, o1), (a2, o2), (a3, o3))):
        q = a[:, 128:][:, first : first + HEAD_DIM]
        row = pos_col[g * GROUP : (g + 1) * GROUP, :]
        s_own = lax.dot_general(q, kv[:, :HEAD_DIM], NT, preferred_element_type=F32) * SCALE
        s_low = lax.dot_general(q, low[:, :HEAD_DIM], NT, preferred_element_type=F32) * SCALE
        s_high = lax.dot_general(q, high[:, :HEAD_DIM], NT, preferred_element_type=F32) * SCALE
        after = col >= row
        in_low = jnp.logical_and(after, has_low)
        in_high = jnp.logical_and(jnp.logical_not(after), has_high)
        s_far = jnp.where(in_low, s_low, jnp.where(in_high, s_high, -jnp.inf))
        top = jnp.maximum(
            jnp.max(s_own, axis=-1, keepdims=True), jnp.max(s_far, axis=-1, keepdims=True)
        )
        e_own = jnp.exp(s_own - top)
        e_far = jnp.exp(s_far - top)
        total = jnp.sum(e_own + e_far, axis=-1, keepdims=True)
        e_low = jnp.where(in_low, e_far, 0.0).astype(BF)
        e_high = jnp.where(in_high, e_far, 0.0).astype(BF)
        out = jnp.dot(e_own.astype(BF), kv, preferred_element_type=F32)
        out += jnp.dot(e_low, low, preferred_element_type=F32)
        out += jnp.dot(e_high, high, preferred_element_type=F32)
        o[...] = (out / total)[:, HEAD_DIM:].astype(BF)


def window_attention(layer, flags, pieces, kv, low, high, pos_col, pos_row):
    return pl.pallas_call(
        functools.partial(window_kernel, layer),
        in_specs=[smem()] + [whole()] * 9,
        out_specs=[whole()] * 4,
        out_shape=[sds((GROUP, HEAD_DIM))] * 4,
        compiler_params=vm(),
        cost_estimate=cost(4e8, 1e6),
        name="window_attention",
    )(flags, *pieces, kv, low, high, pos_col, pos_row)


def feed_forward_kernel(b0, b1, b2, b3, *refs):
    rows = jnp.concatenate([b0[...], b1[...], b2[...], b3[...]], axis=0)
    total = None
    for i in range(4):
        up = jnp.dot(rows, refs[i][...], preferred_element_type=F32)
        hidden = jax.nn.gelu(up).astype(BF)
        part = jnp.dot(hidden, refs[4 + i][...], preferred_element_type=F32)
        total = part if total is None else total + part
    total = total.astype(BF)
    for k in range(4):
        refs[8 + k][...] = total[k * BLOCK : (k + 1) * BLOCK]


def feed_forward(blocks, up_shards, down_shards, layer):
    d = blocks[0].shape[1]
    hidden = 256
    return pl.pallas_call(
        feed_forward_kernel,
        grid=(1,),
        in_specs=[pl.BlockSpec((BLOCK, d), lambda i: (0, 0))] * 4
        + [pl.BlockSpec((d, hidden), lambda i: (0, layer))] * 4
        + [pl.BlockSpec((hidden, d), lambda i: (layer, 0))] * 4,
        out_specs=[pl.BlockSpec((BLOCK, d), lambda i: (0, 0))] * 4,
        out_shape=[sds((BLOCK, d))] * 4,
        compiler_params=vm(),
        cost_estimate=cost(5e8, 5e6),
        name="feed_forward",
    )(*blocks, *up_shards, *down_shards)


def shards(
    grid_latent,
    node_latent,
    src_index,
    in_degree,
    node_order,
    norm_gains,
    enc_wq,
    enc_wkv,
    enc_wo,
    proc_wqkv,
    proc_wo,
    w_up,
    w_down,
):
    d = grid_latent.shape[1]
    grid_count = grid_latent.shape[0]
    band = lax.axis_index("band")
    head = lax.axis_index("head")
    bands = lax.axis_size("band")
    z, core = head // 2, head % 2

    node_all = lax.all_gather(node_latent, "head", axis=0, tiled=True)
    node_blocks = gather_group(node_latent)
    enc_pack = jnp.concatenate([enc_wo, enc_wq.T], axis=0)
    enc_shards = four_shards(enc_pack)

    side = 2 * core - 1
    z_of = jnp.stack([z, z, z + side, z + side])
    core_of = jnp.stack([core, 1 - core, core, 1 - core])
    steps = 2 * jnp.arange(4, dtype=jnp.int32)
    blk = (2 * ((z_of[:, None] + steps[None, :] + 8) % 8) + core_of[:, None]).astype(jnp.int32)
    blk = blk.reshape(16)
    pos = (blk[:, None] * BLOCK + jnp.arange(BLOCK, dtype=jnp.int32)[None, :]).reshape(NODES_HERE)
    order_local = node_order - band * NODES_HERE
    flags = jnp.stack([band > 0, band < bands - 1]).astype(jnp.int32)

    edge_low, edge_high = grid_kv_edges(grid_latent, norm_gains, enc_wkv)
    from_low = up_band(edge_high)
    from_high = down_band(edge_low)
    middle = grid_kv_middle(grid_latent, norm_gains, enc_wkv)

    local = src_index - (band * grid_count - EDGE)
    slot = lax.broadcasted_iota(jnp.int32, src_index.shape, 1)
    node_in_8 = lax.broadcasted_iota(jnp.int32, src_index.shape, 0) % 8
    high_key = jnp.where(slot < in_degree[:, None], (local // 128) * 8 + node_in_8, -1)
    high_key = high_key.reshape(NODES_HERE // 8, 8 * K_MAX)
    low_key = (local % 128).reshape(NODES_HERE // 8, 8 * K_MAX)
    counts = edge_counts(high_key, low_key)

    queries = exchange(node_queries(node_blocks, norm_gains, enc_shards))

    kv_cols = [proc_wqkv[layer, i] for layer in range(LAYERS) for i in (1, 2)]
    q_cols = [proc_wqkv[layer, 0] for layer in range(LAYERS)]
    wide = jnp.concatenate([w_up[0], w_up[1], *kv_cols[:2], *q_cols, *kv_cols[2:]], axis=1)
    tall = jnp.concatenate([w_down.reshape(-1, d), proc_wo.reshape(-1, d)], axis=0)
    tall, wide, _ = lax.optimization_barrier((tall, wide, node_blocks[2]))
    tall_shards = four_shards(tall)
    wide_shards = four_shards(wide)

    own_order = lax.dynamic_slice_in_dim(order_local, head * BLOCK, BLOCK, 0)
    residual = node_all.at[own_order].get(mode="promise_in_bounds")

    kv_parts = [from_low, edge_low, middle, edge_high, from_high]
    enc_heads = edge_attention(blk, queries, kv_parts, counts, order_local[:, None])
    parts = scatter_group(head_sum(give_back(enc_heads), enc_shards, 0))
    stream, normed = close_sum(residual, parts, norm_gains, 2)

    wo_first = w_down.shape[0] * w_down.shape[1] // HEAD_DIM
    pos_col, pos_row = pos[:, None], pos[None, :]
    for layer in range(LAYERS):
        pieces = exchange(qkv(gather_group(normed), wide_shards, layer))
        kv = jnp.concatenate([piece[:, :128] for piece in pieces], axis=0)
        low = up_band(kv)
        high = down_band(kv)
        win_heads = window_attention(layer, flags, pieces, kv, low, high, pos_col, pos_row)
        parts = scatter_group(head_sum(give_back(win_heads), tall_shards, wo_first + layer))
        stream, normed = close_sum(stream, parts, norm_gains, 3 + 2 * layer)
        parts = scatter_group(feed_forward(gather_group(normed), wide_shards, tall_shards, layer))
        if layer + 1 < LAYERS:
            stream, normed = close_sum(stream, parts, norm_gains, 4 + 2 * layer)
        else:
            stream = final_sum(stream, parts)
    return stream


def solution(mesh):
    in_specs = (
        P("band", None),
        P(("band", "head"), None),
        P("band", None),
        P("band"),
        P("band"),
        P(),
        P(None, "head"),
        P(None, None, "head"),
        P("head", None),
        P(None, None, None, "head"),
        P(None, "head", None),
        P(None, None, "head"),
        P(None, "head", None),
    )
    out_specs = P(("band", "head"), None)
    return jax.shard_map(shards, mesh=mesh, in_specs=in_specs, out_specs=out_specs, check_vma=False)
```

```python
import functools
import math

import jax
import jax.numpy as jnp
from jax import lax
from jax.experimental import pallas as pl
from jax.experimental.pallas import tpu as pltpu
from jax.sharding import PartitionSpec as P

HEAD_DIM = 64
K_MAX = 32
HALF_WIN = 512
LAYERS = 2
EDGE = 1536
KV_BLOCK = 512
BLOCK = 32
GROUP = 128
NODES_HERE = 512
KEYS = 7168
SCALE = 1.0 / math.sqrt(HEAD_DIM)
BF = jnp.bfloat16
F32 = jnp.float32
NT = (((1,), (1,)), ((), ()))


def vm(limit_mib=32):
    return pltpu.CompilerParams(vmem_limit_bytes=limit_mib * 1024 * 1024)


def cost(flops, nbytes):
    return pl.CostEstimate(flops=int(flops), bytes_accessed=int(nbytes), transcendentals=0)


def whole():
    return pl.BlockSpec(memory_space=pltpu.VMEM)


def smem():
    return pl.BlockSpec(memory_space=pltpu.SMEM)


def sds(shape, dtype=BF):
    return jax.ShapeDtypeStruct(shape, dtype)


def swap(x):
    return lax.ppermute(x, "head", [(i, i ^ 1) for i in range(16)])


def shift_z(x, k):
    return lax.ppermute(x, "head", [(i, ((i // 2 + k) % 8) * 2 + i % 2) for i in range(16)])


def outward_pairs():
    return [(2 * z + c, 2 * ((z + (1 if c else -1)) % 8) + c) for z in range(8) for c in range(2)]


def outward(x):
    return lax.ppermute(x, "head", outward_pairs())


def inward(x):
    return lax.ppermute(x, "head", [(t, s) for s, t in outward_pairs()])


def crossed(x):
    pairs = [(2 * z, 2 * ((z - 1) % 8) + 1) for z in range(8)]
    return lax.ppermute(x, "head", pairs + [(t, s) for s, t in pairs])


def up_band(x):
    return lax.ppermute(x, "band", [(i, i + 1) for i in range(15)])


def down_band(x):
    return lax.ppermute(x, "band", [(i + 1, i) for i in range(15)])


def gather_group(x):
    behind = shift_z(x, 2)
    ahead = shift_z(x, -2)
    far = shift_z(x, 4)
    return [x, ahead, far, behind]


def scatter_group(parts):
    return [parts[0], shift_z(parts[1], 2), shift_z(parts[2], 4), shift_z(parts[3], -2)]


def four_shards(x):
    third = outward(x)
    return [x, swap(x), third, swap(third)]


def exchange(pieces):
    return [pieces[0], swap(pieces[1]), inward(pieces[2]), crossed(pieces[3])]


def give_back(pieces):
    return [pieces[0], swap(pieces[1]), outward(pieces[2]), crossed(pieces[3])]


def normed_rows(values, gain):
    mean = jnp.mean(values, axis=-1, keepdims=True)
    centred = values - mean
    variance = jnp.mean(centred * centred, axis=-1, keepdims=True)
    return (centred * lax.rsqrt(variance + 1e-05) * gain).astype(BF)


def grid_kv_body(x_ref, gain_ref, w_ref):
    weight = w_ref[...].reshape(2 * HEAD_DIM, x_ref.shape[1])
    outs = []
    for start in range(0, KV_BLOCK, 128):
        normed = normed_rows(x_ref[start : start + 128, :].astype(F32), gain_ref[0:1, :])
        outs.append(lax.dot_general(normed, weight, NT, preferred_element_type=F32).astype(BF))
    return jnp.concatenate(outs, axis=0)


def grid_kv_edges_kernel(x_ref, gain_ref, w_ref, low_ref, high_ref):
    out = grid_kv_body(x_ref, gain_ref, w_ref)
    half = EDGE // KV_BLOCK

    @pl.when(pl.program_id(0) < half)
    def _():
        low_ref[...] = out

    @pl.when(pl.program_id(0) >= half)
    def _():
        high_ref[...] = out


def grid_kv_middle_kernel(x_ref, gain_ref, w_ref, out_ref):
    out_ref[...] = grid_kv_body(x_ref, gain_ref, w_ref)


def grid_kv_edges(grid_latent, gains, w):
    d = grid_latent.shape[1]
    half = EDGE // KV_BLOCK
    skip = grid_latent.shape[0] // KV_BLOCK - 2 * half
    return pl.pallas_call(
        grid_kv_edges_kernel,
        grid=(2 * half,),
        in_specs=[
            pl.BlockSpec((KV_BLOCK, d), lambda i: (jnp.where(i < half, i, i + skip), 0)),
            pl.BlockSpec(gains.shape, lambda i: (0, 0)),
            pl.BlockSpec(w.shape, lambda i: (0, 0, 0)),
        ],
        out_specs=[
            pl.BlockSpec((KV_BLOCK, 128), lambda i: (jnp.minimum(i, half - 1), 0)),
            pl.BlockSpec((KV_BLOCK, 128), lambda i: (jnp.maximum(i - half, 0), 0)),
        ],
        out_shape=[sds((EDGE, 128)), sds((EDGE, 128))],
        compiler_params=vm(56),
        cost_estimate=cost(2 * 3072 * d * 128, 3072 * d * 2),
        name="grid_kv_edges",
    )(grid_latent, gains, w)


def grid_kv_middle(grid_latent, gains, w):
    d = grid_latent.shape[1]
    half = EDGE // KV_BLOCK
    rows = grid_latent.shape[0] - 2 * EDGE
    return pl.pallas_call(
        grid_kv_middle_kernel,
        grid=(rows // KV_BLOCK,),
        in_specs=[
            pl.BlockSpec((KV_BLOCK, d), lambda i: (i + half, 0)),
            pl.BlockSpec(gains.shape, lambda i: (0, 0)),
            pl.BlockSpec(w.shape, lambda i: (0, 0, 0)),
        ],
        out_specs=pl.BlockSpec((KV_BLOCK, 128), lambda i: (i, 0)),
        out_shape=sds((rows, 128)),
        compiler_params=vm(56),
        cost_estimate=cost(2 * 1024 * d * 128, 1024 * d * 2),
        name="grid_kv_middle",
    )(grid_latent, gains, w)


COUNT_STEP = 64
TILES = KEYS // 128


def edge_count_kernel(place_ref, src_ref, degree_ref, out_ref, by_node, high_key, low_key):
    step = pl.program_id(0)

    @pl.when(step == 0)
    def _():
        shape = src_ref.shape
        local = src_ref[...] - (place_ref[0] * place_ref[2] - EDGE)
        used = lax.broadcasted_iota(jnp.int32, shape, 0) < degree_ref[...]
        by_node[...] = jnp.transpose(jnp.where(used, local, -1))
        for t in range(8):
            local_rows = by_node[pl.ds(t, NODES_HERE // 8, stride=8), :]
            cols = slice(t * K_MAX, (t + 1) * K_MAX)
            high_key[:, cols] = jnp.where(local_rows < 0, -1, (local_rows >> 7) * 8 + t)
            low_key[:, cols] = local_rows & 127

    row_high = lax.broadcasted_iota(jnp.int32, (TILES * 8, 256), 0)
    row_low = lax.broadcasted_iota(jnp.int32, (128, 256), 0)

    def counts(group):
        left = jnp.where(row_high == high_key[pl.ds(group, 1), :], 1.0, 0.0).astype(BF)
        right = jnp.where(row_low == low_key[pl.ds(group, 1), :], 1.0, 0.0).astype(BF)
        return lax.dot_general(left, right, NT, preferred_element_type=F32)

    def pair(i, carry):
        group = step * (COUNT_STEP // 8) + 2 * i
        first = counts(group)
        second = counts(group + 1)
        rows = pl.ds(pl.multiple_of(i * 16, 16), 16)
        for t in range(TILES):
            both = jnp.concatenate([first[t * 8 : t * 8 + 8], second[t * 8 : t * 8 + 8]], axis=0)
            out_ref[rows, t * 128 : (t + 1) * 128] = both.astype(BF)
        return carry

    lax.fori_loop(0, COUNT_STEP // 16, pair, 0)


def edge_counts(place, sources, degrees):
    return pl.pallas_call(
        edge_count_kernel,
        grid=(NODES_HERE // COUNT_STEP,),
        in_specs=[
            smem(),
            pl.BlockSpec(sources.shape, lambda i: (0, 0)),
            pl.BlockSpec(degrees.shape, lambda i: (0, 0)),
        ],
        out_specs=pl.BlockSpec((COUNT_STEP, KEYS), lambda i: (i, 0)),
        out_shape=sds((NODES_HERE, KEYS)),
        scratch_shapes=[
            pltpu.VMEM((NODES_HERE, K_MAX), jnp.int32),
            pltpu.VMEM((NODES_HERE // 8, 8 * K_MAX), jnp.int32),
            pltpu.VMEM((NODES_HERE // 8, 8 * K_MAX), jnp.int32),
        ],
        compiler_params=vm(),
        cost_estimate=cost(4e9, 10e6),
        name="edge_counts",
    )(place, sources, degrees)


def block_places(head):
    z, core = head // 2, head % 2
    side = 2 * core - 1
    places = []
    for g in range(4):
        from_z = z if g < 2 else z + side
        from_core = core if g % 2 == 0 else 1 - core
        places += [2 * ((from_z + 2 * k + 8) % 8) + from_core for k in range(4)]
    return places


def row_positions(places):
    lane = lax.broadcasted_iota(jnp.int32, (1, NODES_HERE), 1)
    pos = jnp.zeros((1, NODES_HERE), jnp.int32)
    for i, place in enumerate(places):
        pos = jnp.where(lane // BLOCK == i, place * BLOCK + lane % BLOCK, pos)
    return pos


def node_query_kernel(place_ref, r0, r1, r2, r3, gain_ref, w_ref, order_ref, q_ref, mine_ref, order_col, rows):
    head = place_ref[1]
    places = block_places(head)
    for g, r in enumerate((r0, r1, r2, r3)):
        rows[g * GROUP : (g + 1) * GROUP, :] = r[...]
        normed = normed_rows(r[...].astype(F32), gain_ref[1:2, :])
        q = lax.dot_general(normed, w_ref[...], NT, preferred_element_type=F32).astype(BF)
        for k in range(4):
            start = pl.multiple_of(places[g * 4 + k] * BLOCK, BLOCK)
            q_ref[pl.ds(start, BLOCK), :] = q[k * BLOCK : (k + 1) * BLOCK, :]
    local = order_ref[...] - place_ref[0] * NODES_HERE
    order_col[...] = jnp.transpose(jnp.broadcast_to(local, (8, NODES_HERE)))
    wanted = order_col[pl.ds(pl.multiple_of(head * BLOCK, BLOCK), BLOCK), 0:1]
    pick = jnp.where(row_positions(places) == wanted, 1.0, 0.0).astype(BF)
    mine_ref[...] = jnp.dot(pick, rows[...], preferred_element_type=F32).astype(BF)


def node_queries(place, pieces, gains, wq_t, order):
    d = wq_t.shape[1]
    return pl.pallas_call(
        node_query_kernel,
        in_specs=[smem()] + [whole()] * 7,
        out_specs=[whole()] * 2,
        out_shape=[sds((NODES_HERE, HEAD_DIM)), sds((BLOCK, d))],
        scratch_shapes=[pltpu.VMEM((NODES_HERE, 8), jnp.int32), pltpu.VMEM((NODES_HERE, d), BF)],
        compiler_params=vm(),
        cost_estimate=cost(1e8, 2e6),
        name="node_queries",
    )(place, *pieces, gains, wq_t, order)


T_STEP = 128
CHUNK = 512


def edge_attention_kernel(
    place_ref, q_all, kv0, kv1, kv2, kv3, kv4, count_ref, order_ref,
    o0, o1, o2, o3, scores, heads, pick, order_col,
):
    step = pl.program_id(0)
    q = q_all[pl.ds(pl.multiple_of(step * T_STEP, T_STEP), T_STEP), :]
    chunks = []
    for kv in (kv0, kv1, kv2, kv3, kv4):
        for start in range(0, kv.shape[0], CHUNK):
            chunks.append((kv, start))
    top = None
    for i, (kv, start) in enumerate(chunks):
        keys = kv[start : start + CHUNK, :][:, :HEAD_DIM]
        s = lax.dot_general(q, keys, NT, preferred_element_type=F32) * SCALE
        cols = slice(i * CHUNK, (i + 1) * CHUNK)
        s = jnp.where(count_ref[:, cols].astype(F32) > 0.0, s, -jnp.inf)
        scores[:, cols] = s
        part = jnp.maximum(
            jnp.maximum(s[:, 0:128], s[:, 128:256]), jnp.maximum(s[:, 256:384], s[:, 384:512])
        )
        top = part if top is None else jnp.maximum(top, part)
    top = jnp.max(top, axis=-1, keepdims=True)
    total = jnp.zeros((T_STEP, 128), F32)
    out = jnp.zeros((T_STEP, 128), F32)
    for i, (kv, start) in enumerate(chunks):
        cols = slice(i * CHUNK, (i + 1) * CHUNK)
        e = jnp.exp(scores[:, cols] - top) * count_ref[:, cols].astype(F32)
        total += (e[:, 0:128] + e[:, 128:256]) + (e[:, 256:384] + e[:, 384:512])
        out += jnp.dot(e.astype(BF), kv[start : start + CHUNK, :], preferred_element_type=F32)
    total = jnp.sum(total, axis=-1, keepdims=True)
    rows = pl.ds(pl.multiple_of(step * T_STEP, T_STEP), T_STEP)
    heads[rows, :] = (out / total).astype(BF)

    @pl.when(step == pl.num_programs(0) - 1)
    def _():
        local = order_ref[...] - place_ref[0] * NODES_HERE
        order_col[...] = jnp.transpose(jnp.broadcast_to(local, (8, NODES_HERE)))
        places = block_places(place_ref[1])
        node = lax.broadcasted_iota(jnp.int32, (BLOCK, NODES_HERE), 1)
        for g, o in enumerate((o0, o1, o2, o3)):
            for k in range(4):
                start = pl.multiple_of(places[g * 4 + k] * BLOCK, BLOCK)
                wanted = order_col[pl.ds(start, BLOCK), 0:1]
                pick[k * BLOCK : (k + 1) * BLOCK, :] = jnp.where(node == wanted, 1.0, 0.0).astype(BF)
            taken = jnp.dot(pick[...], heads[...], preferred_element_type=F32)
            o[...] = taken[:, HEAD_DIM:].astype(BF)


def edge_attention(place, queries, kv_parts, counts, order):
    def full(x):
        return pl.BlockSpec(x.shape, lambda i: (0,) * x.ndim)

    return pl.pallas_call(
        edge_attention_kernel,
        grid=(NODES_HERE // T_STEP,),
        in_specs=[smem(), full(queries)]
        + [full(kv) for kv in kv_parts]
        + [pl.BlockSpec((T_STEP, KEYS), lambda i: (i, 0)), full(order)],
        out_specs=[pl.BlockSpec((GROUP, HEAD_DIM), lambda i: (0, 0))] * 4,
        out_shape=[sds((GROUP, HEAD_DIM))] * 4,
        scratch_shapes=[
            pltpu.VMEM((T_STEP, KEYS), F32),
            pltpu.VMEM((NODES_HERE, 128), BF),
            pltpu.VMEM((GROUP, NODES_HERE), BF),
            pltpu.VMEM((NODES_HERE, 8), jnp.int32),
        ],
        compiler_params=vm(40),
        cost_estimate=cost(2e9, 12e6),
        name="edge_attention",
    )(place, queries, *kv_parts, counts, order)


def head_sum_kernel(h0, h1, h2, h3, w0, w1, w2, w3, p0, p1, p2, p3):
    heads = jnp.concatenate([h0[...], h1[...], h2[...], h3[...]], axis=1)
    rows = jnp.concatenate([w0[...], w1[...], w2[...], w3[...]], axis=0)
    total = jnp.dot(heads, rows, preferred_element_type=F32).astype(BF)
    for k, p in enumerate((p0, p1, p2, p3)):
        p[...] = total[k * BLOCK : (k + 1) * BLOCK]


def head_sum(heads, shards, row_block):
    d = shards[0].shape[1]
    full = pl.BlockSpec((GROUP, HEAD_DIM), lambda i: (0, 0))
    return pl.pallas_call(
        head_sum_kernel,
        grid=(1,),
        in_specs=[full] * 4 + [pl.BlockSpec((HEAD_DIM, d), lambda i: (row_block, 0))] * 4,
        out_specs=[pl.BlockSpec((BLOCK, d), lambda i: (0, 0))] * 4,
        out_shape=[sds((BLOCK, d))] * 4,
        compiler_params=vm(),
        cost_estimate=cost(7e7, 1e6),
        name="head_sum",
    )(*heads, *shards)


def close_sum_kernel(gain_row, r_ref, p0, p1, p2, p3, gain_ref, stream_ref, normed_ref):
    total = (p0[...].astype(F32) + p1[...].astype(F32)) + (p2[...].astype(F32) + p3[...].astype(F32))
    stream = (r_ref[...].astype(F32) + total).astype(BF)
    stream_ref[...] = stream
    normed_ref[...] = normed_rows(stream.astype(F32), gain_ref[gain_row : gain_row + 1, :])


def close_sum(residual, parts, gains, gain_row):
    shape = residual.shape
    return pl.pallas_call(
        functools.partial(close_sum_kernel, gain_row),
        in_specs=[whole()] * 6,
        out_specs=[whole()] * 2,
        out_shape=[sds(shape), sds(shape)],
        compiler_params=vm(),
        cost_estimate=cost(1e6, 4e5),
        name="close_sum",
    )(residual, *parts, gains)


def final_sum_kernel(r_ref, p0, p1, p2, p3, stream_ref):
    total = (p0[...].astype(F32) + p1[...].astype(F32)) + (p2[...].astype(F32) + p3[...].astype(F32))
    stream_ref[...] = (r_ref[...].astype(F32) + total).astype(BF)


def final_sum(residual, parts):
    return pl.pallas_call(
        final_sum_kernel,
        in_specs=[whole()] * 5,
        out_specs=whole(),
        out_shape=sds(residual.shape),
        compiler_params=vm(),
        cost_estimate=cost(1e6, 4e5),
        name="final_sum",
    )(residual, *parts)


def qkv_kernel(b0, b1, b2, b3, w0, w1, w2, w3, p0, p1, p2, p3):
    rows = jnp.concatenate([b0[...], b1[...], b2[...], b3[...]], axis=0)
    for w, out in ((w0, p0), (w1, p1), (w2, p2), (w3, p3)):
        all_cols = lax.dot_general(rows, w[...], NT, preferred_element_type=F32).astype(BF)
        out[:, :128] = all_cols[:, HEAD_DIM:]
        out[:, 128:] = all_cols[:, :HEAD_DIM]


def qkv(blocks, shards, layer):
    d = blocks[0].shape[1]
    return pl.pallas_call(
        qkv_kernel,
        grid=(1,),
        in_specs=[pl.BlockSpec((BLOCK, d), lambda i: (0, 0))] * 4
        + [pl.BlockSpec((3 * HEAD_DIM, d), lambda i: (layer, 0))] * 4,
        out_specs=[pl.BlockSpec((GROUP, 3 * HEAD_DIM), lambda i: (0, 0))] * 4,
        out_shape=[sds((GROUP, 3 * HEAD_DIM))] * 4,
        compiler_params=vm(),
        cost_estimate=cost(3e8, 2.5e6),
        name="qkv",
    )(*blocks, *shards)


def window_kernel(place_ref, a0, a1, a2, a3, kv_ref, low_ref, high_ref, o0, o1, o2, o3):
    kv = kv_ref[...]
    low = low_ref[...]
    high = high_ref[...]
    has_low = place_ref[0] > 0
    has_high = place_ref[0] < place_ref[3] - 1
    places = block_places(place_ref[1])
    col = row_positions(places)
    line = lax.broadcasted_iota(jnp.int32, (GROUP, 1), 0)
    for g, (a, o) in enumerate(((a0, o0), (a1, o1), (a2, o2), (a3, o3))):
        q = a[:, 128:]
        row = jnp.zeros((GROUP, 1), jnp.int32)
        for k in range(4):
            row = jnp.where(line // BLOCK == k, places[g * 4 + k] * BLOCK + line % BLOCK, row)
        s_own = lax.dot_general(q, kv[:, :HEAD_DIM], NT, preferred_element_type=F32) * SCALE
        s_low = lax.dot_general(q, low[:, :HEAD_DIM], NT, preferred_element_type=F32) * SCALE
        s_high = lax.dot_general(q, high[:, :HEAD_DIM], NT, preferred_element_type=F32) * SCALE
        after = col >= row
        in_low = jnp.logical_and(after, has_low)
        in_high = jnp.logical_and(jnp.logical_not(after), has_high)
        s_far = jnp.where(in_low, s_low, jnp.where(in_high, s_high, -jnp.inf))
        top = jnp.maximum(
            jnp.max(s_own, axis=-1, keepdims=True), jnp.max(s_far, axis=-1, keepdims=True)
        )
        e_own = jnp.exp(s_own - top)
        e_far = jnp.exp(s_far - top)
        total = jnp.sum(e_own + e_far, axis=-1, keepdims=True)
        e_low = jnp.where(in_low, e_far, 0.0).astype(BF)
        e_high = jnp.where(in_high, e_far, 0.0).astype(BF)
        out = jnp.dot(e_own.astype(BF), kv, preferred_element_type=F32)
        out += jnp.dot(e_low, low, preferred_element_type=F32)
        out += jnp.dot(e_high, high, preferred_element_type=F32)
        o[...] = (out / total)[:, HEAD_DIM:].astype(BF)


def window_attention(place, pieces, kv, low, high):
    return pl.pallas_call(
        window_kernel,
        in_specs=[smem()] + [whole()] * 7,
        out_specs=[whole()] * 4,
        out_shape=[sds((GROUP, HEAD_DIM))] * 4,
        compiler_params=vm(),
        cost_estimate=cost(4e8, 1e6),
        name="window_attention",
    )(place, *pieces, kv, low, high)


def feed_forward_kernel(b0, b1, b2, b3, *refs):
    rows = jnp.concatenate([b0[...], b1[...], b2[...], b3[...]], axis=0)
    total = None
    for i in range(4):
        up = jnp.dot(rows, refs[i][0], preferred_element_type=F32)
        hidden = jax.nn.gelu(up).astype(BF)
        part = jnp.dot(hidden, refs[4 + i][0], preferred_element_type=F32)
        total = part if total is None else total + part
    total = total.astype(BF)
    for k in range(4):
        refs[8 + k][...] = total[k * BLOCK : (k + 1) * BLOCK]


def feed_forward(blocks, up_shards, down_shards, layer):
    d = blocks[0].shape[1]
    hidden = up_shards[0].shape[2]
    return pl.pallas_call(
        feed_forward_kernel,
        grid=(1,),
        in_specs=[pl.BlockSpec((BLOCK, d), lambda i: (0, 0))] * 4
        + [pl.BlockSpec((1, d, hidden), lambda i: (layer, 0, 0))] * 4
        + [pl.BlockSpec((1, hidden, d), lambda i: (layer, 0, 0))] * 4,
        out_specs=[pl.BlockSpec((BLOCK, d), lambda i: (0, 0))] * 4,
        out_shape=[sds((BLOCK, d))] * 4,
        compiler_params=vm(),
        cost_estimate=cost(5e8, 5e6),
        name="feed_forward",
    )(*blocks, *up_shards, *down_shards)


def shards(
    grid_latent,
    node_latent,
    src_index,
    in_degree,
    node_order,
    norm_gains,
    enc_wq,
    enc_wkv,
    enc_wo,
    proc_wqkv,
    proc_wo,
    w_up,
    w_down,
):
    d = grid_latent.shape[1]
    band = lax.axis_index("band")
    head = lax.axis_index("head")
    place = jnp.stack([band, head, grid_latent.shape[0], lax.axis_size("band")]).astype(jnp.int32)
    order = node_order[None, :]

    wkv_t = jnp.swapaxes(enc_wkv, 1, 2)
    edge_low, edge_high = grid_kv_edges(grid_latent, norm_gains, wkv_t)
    from_low = up_band(edge_high)
    from_high = down_band(edge_low)
    node_blocks = gather_group(node_latent)
    sources, grid_latent, _ = lax.optimization_barrier((src_index.T, grid_latent, edge_low))
    middle = grid_kv_middle(grid_latent, norm_gains, wkv_t)
    counts = edge_counts(place, sources, in_degree[None, :])
    node_blocks, counts, middle, from_low, from_high = lax.optimization_barrier(
        (node_blocks, counts, middle, from_low, from_high)
    )
    node_group = jnp.concatenate(node_blocks, axis=0)
    node_pieces = exchange([node_group] * 4)
    queries, residual = node_queries(place, node_pieces, norm_gains, enc_wq.T, order)

    qkv_t = jnp.swapaxes(proc_wqkv, 2, 3).reshape(-1, d)
    tall = jnp.concatenate([qkv_t, proc_wo.reshape(-1, d), enc_wo], axis=0)
    tall, w_up, w_down, _ = lax.optimization_barrier((tall, w_up, w_down, queries))
    tall_shards = four_shards(tall)
    down_shards = four_shards(w_down)
    up_shards = four_shards(w_up)

    kv_parts = [from_low, edge_low, middle, edge_high, from_high]
    enc_heads = edge_attention(place, queries, kv_parts, counts, order)
    wo_first = qkv_t.shape[0] // HEAD_DIM
    parts = scatter_group(head_sum(give_back(enc_heads), tall_shards, wo_first + LAYERS))
    stream, normed = close_sum(residual, parts, norm_gains, 2)

    for layer in range(LAYERS):
        pieces = exchange(qkv(gather_group(normed), tall_shards, layer))
        kv = jnp.concatenate([piece[:, :128] for piece in pieces], axis=0)
        low = up_band(kv)
        high = down_band(kv)
        win_heads = window_attention(place, pieces, kv, low, high)
        parts = scatter_group(head_sum(give_back(win_heads), tall_shards, wo_first + layer))
        stream, normed = close_sum(stream, parts, norm_gains, 3 + 2 * layer)
        parts = scatter_group(feed_forward(gather_group(normed), up_shards, down_shards, layer))
        if layer + 1 < LAYERS:
            stream, normed = close_sum(stream, parts, norm_gains, 4 + 2 * layer)
        else:
            stream = final_sum(stream, parts)
    return stream


def solution(mesh):
    in_specs = (
        P("band", None),
        P(("band", "head"), None),
        P("band", None),
        P("band"),
        P("band"),
        P(),
        P(None, "head"),
        P(None, None, "head"),
        P("head", None),
        P(None, None, None, "head"),
        P(None, "head", None),
        P(None, None, "head"),
        P(None, "head", None),
    )
    out_specs = P(("band", "head"), None)
    return jax.shard_map(shards, mesh=mesh, in_specs=in_specs, out_specs=out_specs, check_vma=False)
```

```python
import functools
import math

import jax
import jax.numpy as jnp
from jax import lax
from jax.experimental import pallas as pl
from jax.experimental.pallas import tpu as pltpu
from jax.sharding import PartitionSpec as P

HEAD_DIM = 64
K_MAX = 32
HALF_WIN = 512
LAYERS = 2
EDGE = 1536
KV_BLOCK = 512
BLOCK = 32
GROUP = 128
NODES_HERE = 512
KEYS = 7168
SCALE = 1.0 / math.sqrt(HEAD_DIM)
BF = jnp.bfloat16
F32 = jnp.float32
NT = (((1,), (1,)), ((), ()))


def vm(limit_mib=20):
    return pltpu.CompilerParams(vmem_limit_bytes=limit_mib * 1024 * 1024)


def cost(flops, nbytes):
    return pl.CostEstimate(flops=int(flops), bytes_accessed=int(nbytes), transcendentals=0)


def whole():
    return pl.BlockSpec(memory_space=pltpu.VMEM)


def smem():
    return pl.BlockSpec(memory_space=pltpu.SMEM)


def sds(shape, dtype=BF):
    return jax.ShapeDtypeStruct(shape, dtype)


def swap(x):
    return lax.ppermute(x, "head", [(i, i ^ 1) for i in range(16)])


def shift_z(x, k):
    return lax.ppermute(x, "head", [(i, ((i // 2 + k) % 8) * 2 + i % 2) for i in range(16)])


def outward_pairs():
    return [(2 * z + c, 2 * ((z + (1 if c else -1)) % 8) + c) for z in range(8) for c in range(2)]


def outward(x):
    return lax.ppermute(x, "head", outward_pairs())


def inward(x):
    return lax.ppermute(x, "head", [(t, s) for s, t in outward_pairs()])


def crossed(x):
    pairs = [(2 * z, 2 * ((z - 1) % 8) + 1) for z in range(8)]
    return lax.ppermute(x, "head", pairs + [(t, s) for s, t in pairs])


def up_band(x):
    return lax.ppermute(x, "band", [(i, i + 1) for i in range(15)])


def down_band(x):
    return lax.ppermute(x, "band", [(i + 1, i) for i in range(15)])


def gather_group(x):
    behind = shift_z(x, 2)
    ahead = shift_z(x, -2)
    far = shift_z(x, 4)
    return [x, ahead, far, behind]


def scatter_group(parts):
    return [parts[0], shift_z(parts[1], 2), shift_z(parts[2], 4), shift_z(parts[3], -2)]


def four_shards(x):
    third = outward(x)
    return [x, swap(x), third, swap(third)]


def exchange(pieces):
    return [pieces[0], swap(pieces[1]), inward(pieces[2]), crossed(pieces[3])]


def give_back(pieces):
    return [pieces[0], swap(pieces[1]), outward(pieces[2]), crossed(pieces[3])]


def stack_kernel(b0, b1, b2, b3, out_ref):
    rows, cols = b0.shape[0], out_ref.shape[1]
    for k, b in enumerate((b0, b1, b2, b3)):
        out_ref[k * rows : (k + 1) * rows, :] = b[:, :cols]


def stack(blocks, cols):
    rows = blocks[0].shape[0]
    return pl.pallas_call(
        stack_kernel,
        in_specs=[whole()] * 4,
        out_specs=whole(),
        out_shape=sds((4 * rows, cols)),
        compiler_params=vm(),
        cost_estimate=cost(1e5, 4 * rows * cols * 4),
        name="stack",
    )(*blocks)


def normed_rows(values, gain):
    mean = jnp.mean(values, axis=-1, keepdims=True)
    centred = values - mean
    variance = jnp.mean(centred * centred, axis=-1, keepdims=True)
    return (centred * lax.rsqrt(variance + 1e-05) * gain).astype(BF)


def grid_kv_body(x_refs, gain_ref, w_ref, w_both):
    @pl.when(pl.program_id(0) == 0)
    def _():
        for i in range(2):
            turned = jnp.transpose(w_ref[i].astype(F32)).astype(BF)
            w_both[:, i * HEAD_DIM : (i + 1) * HEAD_DIM] = turned

    outs = []
    for x_ref in x_refs:
        normed = normed_rows(x_ref[...].astype(F32), gain_ref[0:1, :])
        outs.append(jnp.dot(normed, w_both[...], preferred_element_type=F32).astype(BF))
    return jnp.concatenate(outs, axis=0)


def grid_kv_edges_kernel(x0, x1, x2, x3, gain_ref, w_ref, low_ref, high_ref, w_both):
    out = grid_kv_body((x0, x1, x2, x3), gain_ref, w_ref, w_both)
    half = EDGE // KV_BLOCK

    @pl.when(pl.program_id(0) < half)
    def _():
        low_ref[...] = out

    @pl.when(pl.program_id(0) >= half)
    def _():
        high_ref[...] = out


def grid_kv_middle_kernel(x0, x1, x2, x3, gain_ref, w_ref, out_ref, w_both):
    out_ref[...] = grid_kv_body((x0, x1, x2, x3), gain_ref, w_ref, w_both)


def grid_kv_edges(grid_latent, gains, w):
    d = grid_latent.shape[1]
    half = EDGE // KV_BLOCK
    skip = grid_latent.shape[0] // KV_BLOCK - 2 * half
    return pl.pallas_call(
        grid_kv_edges_kernel,
        grid=(2 * half,),
        in_specs=[
            pl.BlockSpec((KV_BLOCK // 4, d), lambda i, k=k: (4 * jnp.where(i < half, i, i + skip) + k, 0))
            for k in range(4)
        ]
        + [
            pl.BlockSpec(gains.shape, lambda i: (0, 0)),
            pl.BlockSpec(w.shape, lambda i: (0, 0, 0)),
        ],
        out_specs=[
            pl.BlockSpec((KV_BLOCK, 128), lambda i: (jnp.minimum(i, half - 1), 0)),
            pl.BlockSpec((KV_BLOCK, 128), lambda i: (jnp.maximum(i - half, 0), 0)),
        ],
        out_shape=[sds((EDGE, 128)), sds((EDGE, 128))],
        scratch_shapes=[pltpu.VMEM((d, 128), BF)],
        compiler_params=vm(56),
        cost_estimate=cost(2 * 3072 * d * 128, 3072 * d * 2),
        name="grid_kv_edges",
    )(*[grid_latent] * 4, gains, w)


def grid_kv_middle(grid_latent, gains, w):
    d = grid_latent.shape[1]
    half = EDGE // KV_BLOCK
    rows = grid_latent.shape[0] - 2 * EDGE
    return pl.pallas_call(
        grid_kv_middle_kernel,
        grid=(rows // KV_BLOCK,),
        in_specs=[
            pl.BlockSpec((KV_BLOCK // 4, d), lambda i, k=k: (4 * (i + half) + k, 0)) for k in range(4)
        ]
        + [
            pl.BlockSpec(gains.shape, lambda i: (0, 0)),
            pl.BlockSpec(w.shape, lambda i: (0, 0, 0)),
        ],
        out_specs=pl.BlockSpec((KV_BLOCK, 128), lambda i: (i, 0)),
        out_shape=sds((rows, 128)),
        scratch_shapes=[pltpu.VMEM((d, 128), BF)],
        compiler_params=vm(56),
        cost_estimate=cost(2 * 1024 * d * 128, 1024 * d * 2),
        name="grid_kv_middle",
    )(*[grid_latent] * 4, gains, w)


COUNT_STEP = 64
TILES = KEYS // 128


def edge_count_kernel(place_ref, src_ref, degree_ref, out_ref, by_node, high_key, low_key):
    step = pl.program_id(0)

    @pl.when(step == 0)
    def _():
        shape = src_ref.shape
        local = src_ref[...] - (place_ref[0] * place_ref[2] - EDGE)
        used = lax.broadcasted_iota(jnp.int32, shape, 0) < degree_ref[...]
        by_node[...] = jnp.transpose(jnp.where(used, local, -1))
        for t in range(8):
            local_rows = by_node[pl.ds(t, NODES_HERE // 8, stride=8), :]
            cols = slice(t * K_MAX, (t + 1) * K_MAX)
            high_key[:, cols] = jnp.where(local_rows < 0, -1, (local_rows >> 7) * 8 + t)
            low_key[:, cols] = local_rows & 127

    row_high = lax.broadcasted_iota(jnp.int32, (TILES * 8, 256), 0)
    row_low = lax.broadcasted_iota(jnp.int32, (128, 256), 0)

    def counts(group):
        left = jnp.where(row_high == high_key[pl.ds(group, 1), :], 1.0, 0.0).astype(BF)
        right = jnp.where(row_low == low_key[pl.ds(group, 1), :], 1.0, 0.0).astype(BF)
        return lax.dot_general(left, right, NT, preferred_element_type=F32)

    def pair(i, carry):
        group = step * (COUNT_STEP // 8) + 2 * i
        first = counts(group)
        second = counts(group + 1)
        rows = pl.ds(pl.multiple_of(i * 16, 16), 16)
        for t in range(TILES):
            both = jnp.concatenate([first[t * 8 : t * 8 + 8], second[t * 8 : t * 8 + 8]], axis=0)
            out_ref[rows, t * 128 : (t + 1) * 128] = both.astype(BF)
        return carry

    lax.fori_loop(0, COUNT_STEP // 16, pair, 0)


def edge_counts(place, sources, degrees):
    return pl.pallas_call(
        edge_count_kernel,
        grid=(NODES_HERE // COUNT_STEP,),
        in_specs=[
            smem(),
            pl.BlockSpec(sources.shape, lambda i: (0, 0)),
            pl.BlockSpec(degrees.shape, lambda i: (0, 0)),
        ],
        out_specs=pl.BlockSpec((COUNT_STEP, KEYS), lambda i: (i, 0)),
        out_shape=sds((NODES_HERE, KEYS)),
        scratch_shapes=[
            pltpu.VMEM((NODES_HERE, K_MAX), jnp.int32),
            pltpu.VMEM((NODES_HERE // 8, 8 * K_MAX), jnp.int32),
            pltpu.VMEM((NODES_HERE // 8, 8 * K_MAX), jnp.int32),
        ],
        compiler_params=vm(56),
        cost_estimate=cost(4e9, 10e6),
        name="edge_counts",
    )(place, sources, degrees)


def block_places(head):
    z, core = head // 2, head % 2
    side = 2 * core - 1
    places = []
    for g in range(4):
        from_z = z if g < 2 else z + side
        from_core = core if g % 2 == 0 else 1 - core
        places += [2 * ((from_z + 2 * k + 8) % 8) + from_core for k in range(4)]
    return places


def row_positions(places):
    lane = lax.broadcasted_iota(jnp.int32, (1, NODES_HERE), 1)
    pos = jnp.zeros((1, NODES_HERE), jnp.int32)
    for i, place in enumerate(places):
        pos = jnp.where(lane // BLOCK == i, place * BLOCK + lane % BLOCK, pos)
    return pos


def node_query_kernel(place_ref, r0, r1, r2, r3, gain_ref, w_ref, order_ref, q_ref, mine_ref, order_col, rows):
    head = place_ref[1]
    places = block_places(head)
    for g, r in enumerate((r0, r1, r2, r3)):
        rows[g * GROUP : (g + 1) * GROUP, :] = r[...]
        normed = normed_rows(r[...].astype(F32), gain_ref[1:2, :])
        q = lax.dot_general(normed, w_ref[...], NT, preferred_element_type=F32).astype(BF)
        for k in range(4):
            start = pl.multiple_of(places[g * 4 + k] * BLOCK, BLOCK)
            q_ref[pl.ds(start, BLOCK), :] = q[k * BLOCK : (k + 1) * BLOCK, :]
    local = order_ref[...] - place_ref[0] * NODES_HERE
    order_col[...] = jnp.transpose(jnp.broadcast_to(local, (8, NODES_HERE)))
    wanted = order_col[pl.ds(pl.multiple_of(head * BLOCK, BLOCK), BLOCK), 0:1]
    pick = jnp.where(row_positions(places) == wanted, 1.0, 0.0).astype(BF)
    mine_ref[...] = jnp.dot(pick, rows[...], preferred_element_type=F32).astype(BF)


def node_queries(place, pieces, gains, wq_t, order):
    d = wq_t.shape[1]
    return pl.pallas_call(
        node_query_kernel,
        in_specs=[smem()] + [whole()] * 7,
        out_specs=[whole()] * 2,
        out_shape=[sds((NODES_HERE, HEAD_DIM)), sds((BLOCK, d))],
        scratch_shapes=[pltpu.VMEM((NODES_HERE, 8), jnp.int32), pltpu.VMEM((NODES_HERE, d), BF)],
        compiler_params=vm(),
        cost_estimate=cost(1e8, 2e6),
        name="node_queries",
    )(place, *pieces, gains, wq_t, order)


T_STEP = 128
CHUNK = 512


def edge_attention_kernel(
    place_ref, q_all, kv0, kv1, kv2, kv3, kv4, count_ref, order_ref,
    o0, o1, o2, o3, scores, heads, pick, order_col,
):
    step = pl.program_id(0)
    q = q_all[pl.ds(pl.multiple_of(step * T_STEP, T_STEP), T_STEP), :]
    chunks = []
    for kv in (kv0, kv1, kv2, kv3, kv4):
        for start in range(0, kv.shape[0], CHUNK):
            chunks.append((kv, start))
    top = None
    for i, (kv, start) in enumerate(chunks):
        keys = kv[start : start + CHUNK, :][:, :HEAD_DIM]
        s = lax.dot_general(q, keys, NT, preferred_element_type=F32) * SCALE
        cols = slice(i * CHUNK, (i + 1) * CHUNK)
        s = jnp.where(count_ref[:, cols].astype(F32) > 0.0, s, -jnp.inf)
        scores[:, cols] = s
        part = jnp.maximum(
            jnp.maximum(s[:, 0:128], s[:, 128:256]), jnp.maximum(s[:, 256:384], s[:, 384:512])
        )
        top = part if top is None else jnp.maximum(top, part)
    top = jnp.max(top, axis=-1, keepdims=True)
    total = jnp.zeros((T_STEP, 128), F32)
    out = jnp.zeros((T_STEP, 128), F32)
    for i, (kv, start) in enumerate(chunks):
        cols = slice(i * CHUNK, (i + 1) * CHUNK)
        e = jnp.exp(scores[:, cols] - top) * count_ref[:, cols].astype(F32)
        total += (e[:, 0:128] + e[:, 128:256]) + (e[:, 256:384] + e[:, 384:512])
        out += jnp.dot(e.astype(BF), kv[start : start + CHUNK, :], preferred_element_type=F32)
    total = jnp.sum(total, axis=-1, keepdims=True)
    rows = pl.ds(pl.multiple_of(step * T_STEP, T_STEP), T_STEP)
    heads[rows, :] = (out / total).astype(BF)

    @pl.when(step == pl.num_programs(0) - 1)
    def _():
        local = order_ref[...] - place_ref[0] * NODES_HERE
        order_col[...] = jnp.transpose(jnp.broadcast_to(local, (8, NODES_HERE)))
        places = block_places(place_ref[1])
        node = lax.broadcasted_iota(jnp.int32, (BLOCK, NODES_HERE), 1)
        for g, o in enumerate((o0, o1, o2, o3)):
            for k in range(4):
                start = pl.multiple_of(places[g * 4 + k] * BLOCK, BLOCK)
                wanted = order_col[pl.ds(start, BLOCK), 0:1]
                pick[k * BLOCK : (k + 1) * BLOCK, :] = jnp.where(node == wanted, 1.0, 0.0).astype(BF)
            taken = jnp.dot(pick[...], heads[...], preferred_element_type=F32)
            o[...] = taken[:, HEAD_DIM:].astype(BF)


def edge_attention(place, queries, kv_parts, counts, order):
    def full(x):
        return pl.BlockSpec(x.shape, lambda i: (0,) * x.ndim)

    return pl.pallas_call(
        edge_attention_kernel,
        grid=(NODES_HERE // T_STEP,),
        in_specs=[smem(), full(queries)]
        + [full(kv) for kv in kv_parts]
        + [pl.BlockSpec((T_STEP, KEYS), lambda i: (i, 0)), full(order)],
        out_specs=[pl.BlockSpec((GROUP, HEAD_DIM), lambda i: (0, 0))] * 4,
        out_shape=[sds((GROUP, HEAD_DIM))] * 4,
        scratch_shapes=[
            pltpu.VMEM((T_STEP, KEYS), F32),
            pltpu.VMEM((NODES_HERE, 128), BF),
            pltpu.VMEM((GROUP, NODES_HERE), BF),
            pltpu.VMEM((NODES_HERE, 8), jnp.int32),
        ],
        compiler_params=vm(56),
        cost_estimate=cost(2e9, 12e6),
        name="edge_attention",
    )(place, queries, *kv_parts, counts, order)


def head_sum_kernel(h0, h1, h2, h3, w0, w1, w2, w3, p0, p1, p2, p3):
    heads = jnp.concatenate([h0[...], h1[...], h2[...], h3[...]], axis=1)
    rows = jnp.concatenate([w0[...], w1[...], w2[...], w3[...]], axis=0)
    total = jnp.dot(heads, rows, preferred_element_type=F32).astype(BF)
    for k, p in enumerate((p0, p1, p2, p3)):
        p[...] = total[k * BLOCK : (k + 1) * BLOCK]


def head_sum(heads, shards, row_block):
    d = shards[0].shape[1]
    full = pl.BlockSpec((GROUP, HEAD_DIM), lambda i: (0, 0))
    return pl.pallas_call(
        head_sum_kernel,
        grid=(1,),
        in_specs=[full] * 4 + [pl.BlockSpec((HEAD_DIM, d), lambda i: (row_block, 0))] * 4,
        out_specs=[pl.BlockSpec((BLOCK, d), lambda i: (0, 0))] * 4,
        out_shape=[sds((BLOCK, d))] * 4,
        compiler_params=vm(),
        cost_estimate=cost(7e7, 1e6),
        name="head_sum",
    )(*heads, *shards)


def close_sum_kernel(gain_row, r_ref, p0, p1, p2, p3, gain_ref, stream_ref, normed_ref):
    total = (p0[...].astype(F32) + p1[...].astype(F32)) + (p2[...].astype(F32) + p3[...].astype(F32))
    stream = (r_ref[...].astype(F32) + total).astype(BF)
    stream_ref[...] = stream
    normed_ref[...] = normed_rows(stream.astype(F32), gain_ref[gain_row : gain_row + 1, :])


def close_sum(residual, parts, gains, gain_row):
    shape = residual.shape
    return pl.pallas_call(
        functools.partial(close_sum_kernel, gain_row),
        in_specs=[whole()] * 6,
        out_specs=[whole()] * 2,
        out_shape=[sds(shape), sds(shape)],
        compiler_params=vm(),
        cost_estimate=cost(1e6, 4e5),
        name="close_sum",
    )(residual, *parts, gains)


def final_sum_kernel(r_ref, p0, p1, stream_ref):
    total = p0[...].astype(F32) + p1[...].astype(F32)
    stream_ref[...] = (r_ref[...].astype(F32) + total).astype(BF)


def final_sum(residual, parts):
    return pl.pallas_call(
        final_sum_kernel,
        in_specs=[whole()] * 3,
        out_specs=whole(),
        out_shape=sds(residual.shape),
        compiler_params=vm(),
        cost_estimate=cost(1e6, 4e5),
        name="final_sum",
    )(residual, *parts)


def qkv_kernel(b0, b1, b2, b3, w0, w1, w2, w3, p0, p1, p2, p3):
    rows = jnp.concatenate([b0[...], b1[...], b2[...], b3[...]], axis=0)
    for w, out in ((w0, p0), (w1, p1), (w2, p2), (w3, p3)):
        all_cols = lax.dot_general(rows, w[...], NT, preferred_element_type=F32).astype(BF)
        out[:, :128] = all_cols[:, HEAD_DIM:]
        out[:, 128:] = all_cols[:, :HEAD_DIM]


def qkv(blocks, shards, layer):
    d = blocks[0].shape[1]
    return pl.pallas_call(
        qkv_kernel,
        grid=(1,),
        in_specs=[pl.BlockSpec((BLOCK, d), lambda i: (0, 0))] * 4
        + [pl.BlockSpec((3 * HEAD_DIM, d), lambda i: (layer, 0))] * 4,
        out_specs=[pl.BlockSpec((GROUP, 3 * HEAD_DIM), lambda i: (0, 0))] * 4,
        out_shape=[sds((GROUP, 3 * HEAD_DIM))] * 4,
        compiler_params=vm(),
        cost_estimate=cost(3e8, 2.5e6),
        name="qkv",
    )(*blocks, *shards)


def window_kernel(place_ref, a0, a1, a2, a3, kv_ref, low_ref, high_ref, o0, o1, o2, o3):
    kv = kv_ref[...]
    low = low_ref[...]
    high = high_ref[...]
    has_low = place_ref[0] > 0
    has_high = place_ref[0] < place_ref[3] - 1
    places = block_places(place_ref[1])
    col = row_positions(places)
    line = lax.broadcasted_iota(jnp.int32, (GROUP, 1), 0)
    for g, (a, o) in enumerate(((a0, o0), (a1, o1), (a2, o2), (a3, o3))):
        q = a[:, 128:]
        row = jnp.zeros((GROUP, 1), jnp.int32)
        for k in range(4):
            row = jnp.where(line // BLOCK == k, places[g * 4 + k] * BLOCK + line % BLOCK, row)
        s_own = lax.dot_general(q, kv[:, :HEAD_DIM], NT, preferred_element_type=F32) * SCALE
        s_low = lax.dot_general(q, low[:, :HEAD_DIM], NT, preferred_element_type=F32) * SCALE
        s_high = lax.dot_general(q, high[:, :HEAD_DIM], NT, preferred_element_type=F32) * SCALE
        after = col >= row
        in_low = jnp.logical_and(after, has_low)
        in_high = jnp.logical_and(jnp.logical_not(after), has_high)
        s_far = jnp.where(in_low, s_low, jnp.where(in_high, s_high, -jnp.inf))
        top = jnp.maximum(
            jnp.max(s_own, axis=-1, keepdims=True), jnp.max(s_far, axis=-1, keepdims=True)
        )
        e_own = jnp.exp(s_own - top)
        e_far = jnp.exp(s_far - top)
        total = jnp.sum(e_own + e_far, axis=-1, keepdims=True)
        e_low = jnp.where(in_low, e_far, 0.0).astype(BF)
        e_high = jnp.where(in_high, e_far, 0.0).astype(BF)
        out = jnp.dot(e_own.astype(BF), kv, preferred_element_type=F32)
        out += jnp.dot(e_low, low, preferred_element_type=F32)
        out += jnp.dot(e_high, high, preferred_element_type=F32)
        o[...] = (out / total)[:, HEAD_DIM:].astype(BF)


def window_attention(place, pieces, kv, low, high):
    return pl.pallas_call(
        window_kernel,
        in_specs=[smem()] + [whole()] * 7,
        out_specs=[whole()] * 4,
        out_shape=[sds((GROUP, HEAD_DIM))] * 4,
        compiler_params=vm(),
        cost_estimate=cost(4e8, 1e6),
        name="window_attention",
    )(place, *pieces, kv, low, high)


def pack_kernel(up_ref, down_ref, out_ref):
    rows = down_ref.shape[1]
    for q in range(4):
        out_ref[:rows, q * rows : (q + 1) * rows] = up_ref[0, q * rows : (q + 1) * rows, :]
    out_ref[rows:, :] = down_ref[0]


def pack(w_up, w_down, layer):
    d, hidden = w_up.shape[1:]
    return pl.pallas_call(
        pack_kernel,
        grid=(1,),
        in_specs=[
            pl.BlockSpec((1, d, hidden), lambda i: (layer, 0, 0)),
            pl.BlockSpec((1, hidden, d), lambda i: (layer, 0, 0)),
        ],
        out_specs=pl.BlockSpec((2 * hidden, d), lambda i: (0, 0)),
        out_shape=sds((2 * hidden, d)),
        compiler_params=vm(),
        cost_estimate=cost(1e5, 2e6),
        name="pack",
    )(w_up, w_down)


def feed_forward_kernel(b0, b1, b2, b3, w0, w1, w2, w3, p0, p1, p2, p3):
    rows = jnp.concatenate([b0[...], b1[...], b2[...], b3[...]], axis=0)
    total = None
    for w in (w0, w1, w2, w3):
        hidden = w.shape[0] // 2
        up = None
        for q in range(4):
            cols = slice(q * hidden, (q + 1) * hidden)
            part = jnp.dot(rows[:, cols], w[:hidden, cols], preferred_element_type=F32)
            up = part if up is None else up + part
        part = jnp.dot(jax.nn.gelu(up).astype(BF), w[hidden:, :], preferred_element_type=F32)
        total = part if total is None else total + part
    total = total.astype(BF)
    for k, p in enumerate((p0, p1, p2, p3)):
        p[...] = total[k * BLOCK : (k + 1) * BLOCK]


def feed_forward(blocks, shards):
    d = blocks[0].shape[1]
    return pl.pallas_call(
        feed_forward_kernel,
        in_specs=[whole()] * 8,
        out_specs=[whole()] * 4,
        out_shape=[sds((BLOCK, d))] * 4,
        compiler_params=vm(),
        cost_estimate=cost(5e8, 5e6),
        name="feed_forward",
    )(*blocks, *shards)


def pair_feed_forward_kernel(mine_ref, other_ref, w0, w1, w2, w3, own_ref, send_ref, total):
    step = pl.program_id(0)
    w = jnp.concatenate([w0[:, 0], w1[:, 0], w2[:, 0], w3[:, 0]], axis=0)
    hidden = w.shape[0] * 16
    rows = jnp.concatenate([mine_ref[...], other_ref[...]], axis=0)
    up = None
    for q in range(4):
        cols = slice(q * 256, (q + 1) * 256)
        weight = w[:, :16, cols].reshape(256, hidden)
        part = jnp.dot(rows[:, cols], weight, preferred_element_type=F32)
        up = part if up is None else up + part
    weight = w[:, 16:, :].reshape(hidden, rows.shape[1])
    part = jnp.dot(jax.nn.gelu(up).astype(BF), weight, preferred_element_type=F32)

    @pl.when(step == 0)
    def _():
        total[...] = part

    @pl.when(step > 0)
    def _():
        total[...] += part

    @pl.when(step == pl.num_programs(0) - 1)
    def _():
        own_ref[...] = total[:BLOCK, :].astype(BF)
        send_ref[...] = total[BLOCK:, :].astype(BF)


def pair_feed_forward(mine, other, weights):
    d = mine.shape[1]
    bands, shards_here = weights.shape[:2]
    full = pl.BlockSpec((BLOCK, d), lambda i: (0, 0))
    return pl.pallas_call(
        pair_feed_forward_kernel,
        grid=(shards_here,),
        in_specs=[full, full]
        + [pl.BlockSpec((bands // 4, 1, 32, d), lambda i, k=k: (k, i, 0, 0)) for k in range(4)],
        out_specs=[full, full],
        out_shape=[sds((BLOCK, d))] * 2,
        scratch_shapes=[pltpu.VMEM((2 * BLOCK, d), F32)],
        compiler_params=vm(50),
        cost_estimate=cost(5e8, 9e6),
        name="pair_feed_forward",
    )(mine, other, *[weights] * 4)


def sixteenth_kernel(place_ref, up_ref, down_ref, out_ref):
    for q in range(4):
        out_ref[:16, q * 256 : (q + 1) * 256] = up_ref[0, q, 0]
    out_ref[16:, :] = down_ref[0]


def sixteenth(place, w_up, w_down, layer):
    d, hidden = w_up.shape[1:]
    grid_spec = pltpu.PrefetchScalarGridSpec(
        num_scalar_prefetch=1,
        grid=(1,),
        in_specs=[
            pl.BlockSpec((1, 4, 1, 16, hidden), lambda i, place: (layer, 0, place[0], 0, 0)),
            pl.BlockSpec((1, 16, d), lambda i, place: (layer, place[0], 0)),
        ],
        out_specs=pl.BlockSpec((32, d), lambda i, place: (0, 0)),
    )
    return pl.pallas_call(
        sixteenth_kernel,
        grid_spec=grid_spec,
        out_shape=sds((32, d)),
        compiler_params=vm(),
        cost_estimate=cost(1e5, 2e5),
        name="sixteenth",
    )(place, w_up.reshape(-1, 4, 16, 16, hidden), w_down)


def both_cores_weights(over_head, core):
    d = over_head.shape[2]
    half = lax.dynamic_index_in_dim(over_head.reshape(8, 2, 32, d), core, 1, keepdims=False)
    return lax.all_gather(half, "band")


def shards(
    grid_latent,
    node_latent,
    src_index,
    in_degree,
    node_order,
    norm_gains,
    enc_wq,
    enc_wkv,
    enc_wo,
    proc_wqkv,
    proc_wo,
    w_up,
    w_down,
):
    d = grid_latent.shape[1]
    band = lax.axis_index("band")
    head = lax.axis_index("head")
    place = jnp.stack([band, head, grid_latent.shape[0], lax.axis_size("band")]).astype(jnp.int32)
    order = node_order[None, :]

    barrier = lax.optimization_barrier
    late_weights = lax.all_gather(sixteenth(place, w_up, w_down, 1), "head")

    node_blocks = gather_group(node_latent)
    wkv_t = jnp.swapaxes(enc_wkv, 1, 2)
    edge_low, edge_high = grid_kv_edges(grid_latent, norm_gains, wkv_t)
    node_blocks, edge_low, edge_high = barrier((node_blocks, edge_low, edge_high))
    node_group = stack(node_blocks, d)
    node_pieces = exchange([node_group] * 4)
    from_low = up_band(edge_high)
    from_high = down_band(edge_low)

    qkv_t = jnp.swapaxes(proc_wqkv, 2, 3).reshape(-1, d)
    tall = jnp.concatenate([qkv_t, proc_wo.reshape(-1, d), enc_wo], axis=0)
    sources, grid_latent, tall, _ = barrier((src_index.T, grid_latent, tall, node_group))
    first = pack(w_up, w_down, 0)
    tall_third = outward(tall)
    tall_other = swap(tall)
    middle = grid_kv_middle(grid_latent, norm_gains, wkv_t)
    counts = edge_counts(place, sources, in_degree[None, :])
    node_pieces, counts, middle, from_low, from_high, tall_third, tall_other = barrier(
        (node_pieces, counts, middle, from_low, from_high, tall_third, tall_other)
    )
    queries, residual = node_queries(place, node_pieces, norm_gains, enc_wq.T, order)

    first, tall_third, queries = barrier((first, tall_third, queries))
    tall_fourth = swap(tall_third)
    first_third, first_other = outward(first), swap(first)
    kv_parts = [from_low, edge_low, middle, edge_high, from_high]
    enc_heads = edge_attention(place, queries, kv_parts, counts, order)
    enc_heads, first_third, first_other, tall_fourth = barrier(
        (enc_heads, first_third, first_other, tall_fourth)
    )
    first_fourth = swap(first_third)
    tall_shards = [tall, tall_other, tall_third, tall_fourth]
    wo_first = qkv_t.shape[0] // HEAD_DIM
    sums = head_sum(give_back(enc_heads), tall_shards, wo_first + LAYERS)
    sums, first_fourth = barrier((sums, first_fourth))
    first_shards = [first, first_other, first_third, first_fourth]
    stream, normed = close_sum(residual, scatter_group(sums), norm_gains, 2)

    for layer in range(LAYERS):
        pieces = exchange(qkv(gather_group(normed), tall_shards, layer))
        kv = stack(pieces, 2 * HEAD_DIM)
        low = up_band(kv)
        high = down_band(kv)
        if layer == 0:
            low, high, late_weights = barrier((low, high, late_weights))
            late_weights = both_cores_weights(late_weights, head % 2)
        win_heads = window_attention(place, pieces, kv, low, high)
        parts = scatter_group(head_sum(give_back(win_heads), tall_shards, wo_first + layer))
        stream, normed = close_sum(stream, parts, norm_gains, 3 + 2 * layer)
        if layer == 0:
            parts = scatter_group(feed_forward(gather_group(normed), first_shards))
            stream, normed = close_sum(stream, parts, norm_gains, 4 + 2 * layer)
        else:
            own, other = pair_feed_forward(normed, swap(normed), late_weights)
            stream = final_sum(stream, [own, swap(other)])
    return stream


def solution(mesh):
    in_specs = (
        P("band", None),
        P(("band", "head"), None),
        P("band", None),
        P("band"),
        P("band"),
        P(),
        P(None, "head"),
        P(None, None, "head"),
        P("head", None),
        P(None, None, None, "head"),
        P(None, "head", None),
        P(None, None, "head"),
        P(None, "head", None),
    )
    out_specs = P(("band", "head"), None)
    return jax.shard_map(shards, mesh=mesh, in_specs=in_specs, out_specs=out_specs, check_vma=False)
```

```python
import functools
import math

import jax
import jax.numpy as jnp
from jax import lax
from jax.experimental import pallas as pl
from jax.experimental.pallas import tpu as pltpu
from jax.sharding import PartitionSpec as P

HEAD_DIM = 64
K_MAX = 32
HALF_WIN = 512
LAYERS = 2
EDGE = 1536
KV_BLOCK = 512
BLOCK = 32
GROUP = 128
NODES_HERE = 512
KEYS = 7168
SCALE = 1.0 / math.sqrt(HEAD_DIM)
BF = jnp.bfloat16
F32 = jnp.float32
NT = (((1,), (1,)), ((), ()))


def vm(limit_mib=20):
    return pltpu.CompilerParams(vmem_limit_bytes=limit_mib * 1024 * 1024)


def cost(flops, nbytes):
    return pl.CostEstimate(flops=int(flops), bytes_accessed=int(nbytes), transcendentals=0)


def whole():
    return pl.BlockSpec(memory_space=pltpu.VMEM)


def hbm():
    return pl.BlockSpec(memory_space=pltpu.HBM)


def smem():
    return pl.BlockSpec(memory_space=pltpu.SMEM)


def sds(shape, dtype=BF):
    return jax.ShapeDtypeStruct(shape, dtype)


def swap(x):
    return lax.ppermute(x, "head", [(i, i ^ 1) for i in range(16)])


def shift_z(x, k):
    steps = (k, -k)
    return lax.ppermute(x, "head", [(i, ((i // 2 + steps[i % 2]) % 8) * 2 + i % 2) for i in range(16)])


def outward_pairs():
    return [(2 * z + c, 2 * ((z + (1 if c else -1)) % 8) + c) for z in range(8) for c in range(2)]


def outward(x):
    return lax.ppermute(x, "head", outward_pairs())


def inward(x):
    return lax.ppermute(x, "head", [(t, s) for s, t in outward_pairs()])


def crossed(x):
    pairs = [(2 * z, 2 * ((z - 1) % 8) + 1) for z in range(8)]
    return lax.ppermute(x, "head", pairs + [(t, s) for s, t in pairs])


def up_band(x):
    return lax.ppermute(x, "band", [(i, i + 1) for i in range(15)])


def down_band(x):
    return lax.ppermute(x, "band", [(i + 1, i) for i in range(15)])


def gather_group(x):
    behind = shift_z(x, 2)
    ahead = shift_z(x, -2)
    far = shift_z(x, 4)
    return [x, ahead, far, behind]


def scatter_group(parts):
    return [parts[0], shift_z(parts[1], 2), shift_z(parts[2], 4), shift_z(parts[3], -2)]


def four_shards(x):
    third = outward(x)
    return [x, swap(x), third, swap(third)]


def exchange(pieces):
    return [pieces[0], swap(pieces[1]), inward(pieces[2]), crossed(pieces[3])]


def give_back(pieces):
    return [pieces[0], swap(pieces[1]), outward(pieces[2]), crossed(pieces[3])]


def stack_kernel(b0, b1, b2, b3, out_ref):
    rows, cols = b0.shape[0], out_ref.shape[1]
    for k, b in enumerate((b0, b1, b2, b3)):
        out_ref[k * rows : (k + 1) * rows, :] = b[:, :cols]


def stack(blocks, cols):
    rows = blocks[0].shape[0]
    return pl.pallas_call(
        stack_kernel,
        in_specs=[whole()] * 4,
        out_specs=whole(),
        out_shape=sds((4 * rows, cols)),
        compiler_params=vm(),
        cost_estimate=cost(1e5, 4 * rows * cols * 4),
        name="stack",
    )(*blocks)


def normed_rows(values, gain):
    mean = jnp.mean(values, axis=-1, keepdims=True)
    centred = values - mean
    variance = jnp.mean(centred * centred, axis=-1, keepdims=True)
    return (centred * lax.rsqrt(variance + 1e-05) * gain).astype(BF)


def grid_kv_kernel(starts, first, x_ref, *refs):
    if first:
        gain_ref, w_ref, *refs = refs
    else:
        w_both, *refs = refs
    outs, refs = refs[: len(starts)], refs[len(starts) :]
    if first:
        w_both, *refs = refs
    rows, sems = refs
    blocks = outs[0].shape[0] // KV_BLOCK
    copies = [
        pltpu.make_async_copy(
            x_ref.at[pl.ds(start + i * KV_BLOCK, KV_BLOCK)],
            rows.at[part * blocks + i],
            sems.at[part * blocks + i],
        )
        for part, start in enumerate(starts)
        for i in range(blocks)
    ]
    for copy in copies:
        copy.start()
    if first:
        for i in range(2):
            turned = jnp.transpose(w_ref[i].astype(F32) * gain_ref[0:1, :]).astype(BF)
            w_both[:, i * HEAD_DIM : (i + 1) * HEAD_DIM] = turned
    for part, out in enumerate(outs):
        for i in range(blocks):
            copies[part * blocks + i].wait()

            x = rows[part * blocks + i].astype(F32)
            x = x - jnp.mean(x, axis=-1, keepdims=True)
            variance = jnp.mean(x * x, axis=-1, keepdims=True)
            kv = jnp.dot(x.astype(BF), w_both[...], preferred_element_type=F32)
            kv = kv * lax.rsqrt(variance + 1e-05)
            out[i * KV_BLOCK : (i + 1) * KV_BLOCK, :] = kv.astype(BF)


def grid_kv(grid_latent, starts, count, gains=None, w=None, w_both=None):
    d = grid_latent.shape[1]
    blocks = len(starts) * count // KV_BLOCK
    first = w_both is None
    weight_shape = sds((d, 128))
    out_shape = [sds((count, 128))] * len(starts) + ([weight_shape] if first else [])
    return pl.pallas_call(
        functools.partial(grid_kv_kernel, starts, first),
        in_specs=[hbm()] + [whole()] * (2 if first else 1),
        out_specs=[whole()] * len(out_shape),
        out_shape=out_shape,
        scratch_shapes=[
            pltpu.VMEM((blocks, KV_BLOCK, d), BF),
            pltpu.SemaphoreType.DMA((blocks,)),
        ],
        compiler_params=vm(56),
        cost_estimate=cost(2 * blocks * KV_BLOCK * d * 128, blocks * KV_BLOCK * d * 2),
        name="grid_kv",
    )(grid_latent, *((gains, w) if first else (w_both,)))


COUNT_STEP = 64
TILES = KEYS // 128


def edge_count_kernel(place_ref, src_ref, degree_ref, out_ref, by_node, high_key, low_key):
    step = pl.program_id(0)

    @pl.when(step == 0)
    def _():
        shape = src_ref.shape
        local = src_ref[...] - (place_ref[0] * place_ref[2] - EDGE)
        used = lax.broadcasted_iota(jnp.int32, shape, 0) < degree_ref[...]
        by_node[...] = jnp.transpose(jnp.where(used, local, -1))
        for t in range(8):
            local_rows = by_node[pl.ds(t, NODES_HERE // 8, stride=8), :]
            cols = slice(t * K_MAX, (t + 1) * K_MAX)
            high_key[:, cols] = jnp.where(local_rows < 0, -1, (local_rows >> 7) * 8 + t)
            low_key[:, cols] = local_rows & 127

    row_high = lax.broadcasted_iota(jnp.int32, (TILES * 8, 256), 0)
    row_low = lax.broadcasted_iota(jnp.int32, (128, 256), 0)

    def counts(group):
        left = jnp.where(row_high == high_key[pl.ds(group, 1), :], 1.0, 0.0).astype(BF)
        right = jnp.where(row_low == low_key[pl.ds(group, 1), :], 1.0, 0.0).astype(BF)
        return lax.dot_general(left, right, NT, preferred_element_type=F32)

    def pair(i, carry):
        group = step * (COUNT_STEP // 8) + 2 * i
        first = counts(group)
        second = counts(group + 1)
        rows = pl.ds(pl.multiple_of(i * 16, 16), 16)
        for t in range(TILES):
            both = jnp.concatenate([first[t * 8 : t * 8 + 8], second[t * 8 : t * 8 + 8]], axis=0)
            out_ref[rows, t * 128 : (t + 1) * 128] = both.astype(BF)
        return carry

    lax.fori_loop(0, COUNT_STEP // 16, pair, 0)


def edge_counts(place, sources, degrees):
    return pl.pallas_call(
        edge_count_kernel,
        grid=(NODES_HERE // COUNT_STEP,),
        in_specs=[
            smem(),
            pl.BlockSpec(sources.shape, lambda i: (0, 0)),
            pl.BlockSpec(degrees.shape, lambda i: (0, 0)),
        ],
        out_specs=pl.BlockSpec((COUNT_STEP, KEYS), lambda i: (i, 0)),
        out_shape=sds((NODES_HERE, KEYS)),
        scratch_shapes=[
            pltpu.VMEM((NODES_HERE, K_MAX), jnp.int32),
            pltpu.VMEM((NODES_HERE // 8, 8 * K_MAX), jnp.int32),
            pltpu.VMEM((NODES_HERE // 8, 8 * K_MAX), jnp.int32),
        ],
        compiler_params=vm(),
        cost_estimate=cost(4e9, 10e6),
        name="edge_counts",
    )(place, sources, degrees)


def block_places(head):
    z, core = head // 2, head % 2
    side = 2 * core - 1
    places = []
    for g in range(4):
        from_z = z if g < 2 else z + side
        from_core = core if g % 2 == 0 else 1 - core
        step = 2 - 4 * from_core
        places += [2 * ((from_z + step * k + 16) & 7) + from_core for k in range(4)]
    return places


def row_positions(places):
    lane = lax.broadcasted_iota(jnp.int32, (1, NODES_HERE), 1)
    pos = jnp.zeros((1, NODES_HERE), jnp.int32)
    for i, place in enumerate(places):
        pos = jnp.where(lane // BLOCK == i, place * BLOCK + lane % BLOCK, pos)
    return pos


def node_query_kernel(place_ref, r0, r1, r2, r3, gain_ref, w_ref, order_ref, q_ref, mine_ref, order_col, rows):
    head = place_ref[1]
    places = block_places(head)
    for g, r in enumerate((r0, r1, r2, r3)):
        rows[g * GROUP : (g + 1) * GROUP, :] = r[...]
        normed = normed_rows(r[...].astype(F32), gain_ref[1:2, :])
        q = lax.dot_general(normed, w_ref[...], NT, preferred_element_type=F32).astype(BF)
        for k in range(4):
            start = pl.multiple_of(places[g * 4 + k] * BLOCK, BLOCK)
            q_ref[pl.ds(start, BLOCK), :] = q[k * BLOCK : (k + 1) * BLOCK, :]
    local = order_ref[...] - place_ref[0] * NODES_HERE
    order_col[...] = jnp.transpose(jnp.broadcast_to(local, (8, NODES_HERE)))
    wanted = order_col[pl.ds(pl.multiple_of(head * BLOCK, BLOCK), BLOCK), 0:1]
    pick = jnp.where(row_positions(places) == wanted, 1.0, 0.0).astype(BF)
    mine_ref[...] = jnp.dot(pick, rows[...], preferred_element_type=F32).astype(BF)


def node_queries(place, pieces, gains, wq_t, order):
    d = wq_t.shape[1]
    return pl.pallas_call(
        node_query_kernel,
        in_specs=[smem()] + [whole()] * 7,
        out_specs=[whole()] * 2,
        out_shape=[sds((NODES_HERE, HEAD_DIM)), sds((BLOCK, d))],
        scratch_shapes=[pltpu.VMEM((NODES_HERE, 8), jnp.int32), pltpu.VMEM((NODES_HERE, d), BF)],
        compiler_params=vm(),
        cost_estimate=cost(1e8, 2e6),
        name="node_queries",
    )(place, *pieces, gains, wq_t, order)


T_STEP = 128
CHUNK = 512


def edge_attention_kernel(
    place_ref, q_all, kv0, kv1, kv2, kv3, kv4, count_ref, order_ref,
    o0, o1, o2, o3, scores, heads, pick, order_col,
):
    step = pl.program_id(0)
    q = q_all[pl.ds(pl.multiple_of(step * T_STEP, T_STEP), T_STEP), :]
    chunks = []
    for kv in (kv0, kv1, kv2, kv3, kv4):
        for start in range(0, kv.shape[0], CHUNK):
            chunks.append((kv, start))
    top = None
    for i, (kv, start) in enumerate(chunks):
        keys = kv[start : start + CHUNK, :][:, :HEAD_DIM]
        s = lax.dot_general(q, keys, NT, preferred_element_type=F32) * SCALE
        cols = slice(i * CHUNK, (i + 1) * CHUNK)
        s = jnp.where(count_ref[:, cols].astype(F32) > 0.0, s, -jnp.inf)
        scores[:, cols] = s
        part = jnp.maximum(
            jnp.maximum(s[:, 0:128], s[:, 128:256]), jnp.maximum(s[:, 256:384], s[:, 384:512])
        )
        top = part if top is None else jnp.maximum(top, part)
    top = jnp.max(top, axis=-1, keepdims=True)
    total = jnp.zeros((T_STEP, 128), F32)
    out = jnp.zeros((T_STEP, 128), F32)
    for i, (kv, start) in enumerate(chunks):
        cols = slice(i * CHUNK, (i + 1) * CHUNK)
        e = jnp.exp(scores[:, cols] - top) * count_ref[:, cols].astype(F32)
        total += (e[:, 0:128] + e[:, 128:256]) + (e[:, 256:384] + e[:, 384:512])
        out += jnp.dot(e.astype(BF), kv[start : start + CHUNK, :], preferred_element_type=F32)
    total = jnp.sum(total, axis=-1, keepdims=True)
    rows = pl.ds(pl.multiple_of(step * T_STEP, T_STEP), T_STEP)
    heads[rows, :] = (out / total).astype(BF)

    @pl.when(step == pl.num_programs(0) - 1)
    def _():
        local = order_ref[...] - place_ref[0] * NODES_HERE
        order_col[...] = jnp.transpose(jnp.broadcast_to(local, (8, NODES_HERE)))
        places = block_places(place_ref[1])
        node = lax.broadcasted_iota(jnp.int32, (BLOCK, NODES_HERE), 1)
        for g, o in enumerate((o0, o1, o2, o3)):
            for k in range(4):
                start = pl.multiple_of(places[g * 4 + k] * BLOCK, BLOCK)
                wanted = order_col[pl.ds(start, BLOCK), 0:1]
                pick[k * BLOCK : (k + 1) * BLOCK, :] = jnp.where(node == wanted, 1.0, 0.0).astype(BF)
            taken = jnp.dot(pick[...], heads[...], preferred_element_type=F32)
            o[...] = taken[:, HEAD_DIM:].astype(BF)


def edge_attention(place, queries, kv_parts, counts, order):
    def full(x):
        return pl.BlockSpec(x.shape, lambda i: (0,) * x.ndim)

    return pl.pallas_call(
        edge_attention_kernel,
        grid=(NODES_HERE // T_STEP,),
        in_specs=[smem(), full(queries)]
        + [full(kv) for kv in kv_parts]
        + [pl.BlockSpec((T_STEP, KEYS), lambda i: (i, 0)), full(order)],
        out_specs=[pl.BlockSpec((GROUP, HEAD_DIM), lambda i: (0, 0))] * 4,
        out_shape=[sds((GROUP, HEAD_DIM))] * 4,
        scratch_shapes=[
            pltpu.VMEM((T_STEP, KEYS), F32),
            pltpu.VMEM((NODES_HERE, 128), BF),
            pltpu.VMEM((GROUP, NODES_HERE), BF),
            pltpu.VMEM((NODES_HERE, 8), jnp.int32),
        ],
        compiler_params=vm(40),
        cost_estimate=cost(2e9, 12e6),
        name="edge_attention",
    )(place, queries, *kv_parts, counts, order)


def head_sum_kernel(h0, h1, h2, h3, w0, w1, w2, w3, p0, p1, p2, p3):
    heads = jnp.concatenate([h0[...], h1[...], h2[...], h3[...]], axis=1)
    rows = jnp.concatenate([w0[...], w1[...], w2[...], w3[...]], axis=0)
    total = jnp.dot(heads, rows, preferred_element_type=F32).astype(BF)
    for k, p in enumerate((p0, p1, p2, p3)):
        p[...] = total[k * BLOCK : (k + 1) * BLOCK]


def head_sum(heads, shards, row_block):
    d = shards[0].shape[1]
    full = pl.BlockSpec((GROUP, HEAD_DIM), lambda i: (0, 0))
    return pl.pallas_call(
        head_sum_kernel,
        grid=(1,),
        in_specs=[full] * 4 + [pl.BlockSpec((HEAD_DIM, d), lambda i: (row_block, 0))] * 4,
        out_specs=[pl.BlockSpec((BLOCK, d), lambda i: (0, 0))] * 4,
        out_shape=[sds((BLOCK, d))] * 4,
        compiler_params=vm(),
        cost_estimate=cost(7e7, 1e6),
        name="head_sum",
    )(*heads, *shards)


def close_sum_kernel(gain_row, r_ref, p0, p1, p2, p3, gain_ref, stream_ref, normed_ref):
    total = (p0[...].astype(F32) + p1[...].astype(F32)) + (p2[...].astype(F32) + p3[...].astype(F32))
    stream = (r_ref[...].astype(F32) + total).astype(BF)
    stream_ref[...] = stream
    normed_ref[...] = normed_rows(stream.astype(F32), gain_ref[gain_row : gain_row + 1, :])


def close_sum(residual, parts, gains, gain_row):
    shape = residual.shape
    return pl.pallas_call(
        functools.partial(close_sum_kernel, gain_row),
        in_specs=[whole()] * 6,
        out_specs=[whole()] * 2,
        out_shape=[sds(shape), sds(shape)],
        compiler_params=vm(),
        cost_estimate=cost(1e6, 4e5),
        name="close_sum",
    )(residual, *parts, gains)


def final_sum_kernel(r_ref, p0, p1, stream_ref):
    total = p0[...].astype(F32) + p1[...].astype(F32)
    stream_ref[...] = (r_ref[...].astype(F32) + total).astype(BF)


def final_sum(residual, parts):
    return pl.pallas_call(
        final_sum_kernel,
        in_specs=[whole()] * 3,
        out_specs=whole(),
        out_shape=sds(residual.shape),
        compiler_params=vm(),
        cost_estimate=cost(1e6, 4e5),
        name="final_sum",
    )(residual, *parts)


def qkv_kernel(b0, b1, b2, b3, w0, w1, w2, w3, p0, p1, p2, p3):
    rows = jnp.concatenate([b0[...], b1[...], b2[...], b3[...]], axis=0)
    for w, out in ((w0, p0), (w1, p1), (w2, p2), (w3, p3)):
        all_cols = lax.dot_general(rows, w[...], NT, preferred_element_type=F32).astype(BF)
        out[:, :128] = all_cols[:, HEAD_DIM:]
        out[:, 128:] = all_cols[:, :HEAD_DIM]


def qkv(blocks, shards, layer):
    d = blocks[0].shape[1]
    return pl.pallas_call(
        qkv_kernel,
        grid=(1,),
        in_specs=[pl.BlockSpec((BLOCK, d), lambda i: (0, 0))] * 4
        + [pl.BlockSpec((3 * HEAD_DIM, d), lambda i: (layer, 0))] * 4,
        out_specs=[pl.BlockSpec((GROUP, 3 * HEAD_DIM), lambda i: (0, 0))] * 4,
        out_shape=[sds((GROUP, 3 * HEAD_DIM))] * 4,
        compiler_params=vm(),
        cost_estimate=cost(3e8, 2.5e6),
        name="qkv",
    )(*blocks, *shards)


def window_kernel(place_ref, a0, a1, a2, a3, kv_ref, low_ref, high_ref, out_ref):
    kv = kv_ref[...]
    low = low_ref[...]
    high = high_ref[...]
    has_low = place_ref[0] > 0
    has_high = place_ref[0] < place_ref[3] - 1
    places = block_places(place_ref[1])
    col = row_positions(places)
    line = lax.broadcasted_iota(jnp.int32, (GROUP, 1), 0)
    for g, a in enumerate((a0, a1, a2, a3)):
        q = a[:, 128:]
        row = jnp.zeros((GROUP, 1), jnp.int32)
        for k in range(4):
            row = jnp.where(line // BLOCK == k, places[g * 4 + k] * BLOCK + line % BLOCK, row)
        s_own = lax.dot_general(q, kv[:, :HEAD_DIM], NT, preferred_element_type=F32) * SCALE
        s_low = lax.dot_general(q, low[:, :HEAD_DIM], NT, preferred_element_type=F32) * SCALE
        s_high = lax.dot_general(q, high[:, :HEAD_DIM], NT, preferred_element_type=F32) * SCALE
        after = col >= row
        in_low = jnp.logical_and(after, has_low)
        in_high = jnp.logical_and(jnp.logical_not(after), has_high)
        s_far = jnp.where(in_low, s_low, jnp.where(in_high, s_high, -jnp.inf))
        top = jnp.maximum(
            jnp.max(s_own, axis=-1, keepdims=True), jnp.max(s_far, axis=-1, keepdims=True)
        )
        e_own = jnp.exp(s_own - top)
        e_far = jnp.exp(s_far - top)
        total = jnp.sum(e_own + e_far, axis=-1, keepdims=True)
        e_low = jnp.where(in_low, e_far, 0.0).astype(BF)
        e_high = jnp.where(in_high, e_far, 0.0).astype(BF)
        out = jnp.dot(e_own.astype(BF), kv, preferred_element_type=F32)
        out += jnp.dot(e_low, low, preferred_element_type=F32)
        out += jnp.dot(e_high, high, preferred_element_type=F32)
        heads = (out / total)[:, HEAD_DIM:].astype(BF)
        for k in range(4):
            out_ref[places[g * 4 + k]] = heads[k * BLOCK : (k + 1) * BLOCK]


def window_attention(place, pieces, kv, low, high):
    return pl.pallas_call(
        window_kernel,
        in_specs=[smem()] + [whole()] * 7,
        out_specs=whole(),
        out_shape=sds((NODES_HERE // BLOCK, BLOCK, HEAD_DIM)),
        compiler_params=vm(),
        cost_estimate=cost(4e8, 1e6),
        name="window_attention",
    )(place, *pieces, kv, low, high)


def heads_to_stream_kernel(layer, gain_row, heads_ref, wo_ref, r_ref, gain_ref, stream_ref, normed_ref, held, sems):
    count = heads_ref.shape[0]
    step = count // 4
    copies = [
        pltpu.make_async_copy(
            wo_ref.at[q * step : (q + 1) * step, layer], held.at[q * step : (q + 1) * step], sems.at[q]
        )
        for q in range(4)
    ]
    for copy in copies:
        copy.start()
    total = r_ref[...].astype(F32)
    for q, copy in enumerate(copies):
        heads = jnp.concatenate([heads_ref[h] for h in range(q * step, (q + 1) * step)], axis=1)
        copy.wait()
        weight = held[q * step : (q + 1) * step].reshape(step * HEAD_DIM, r_ref.shape[1])
        total += jnp.dot(heads, weight, preferred_element_type=F32)
    stream = total.astype(BF)
    stream_ref[...] = stream
    normed_ref[...] = normed_rows(stream.astype(F32), gain_ref[gain_row : gain_row + 1, :])


def heads_to_stream(heads, wo_all, layer, residual, gains, gain_row):
    count, _, rows, d = wo_all.shape
    return pl.pallas_call(
        functools.partial(heads_to_stream_kernel, layer, gain_row),
        in_specs=[whole(), hbm(), whole(), whole()],
        out_specs=[whole()] * 2,
        out_shape=[sds(residual.shape)] * 2,
        scratch_shapes=[pltpu.VMEM((count, rows, d), BF), pltpu.SemaphoreType.DMA((4,))],
        compiler_params=vm(),
        cost_estimate=cost(7e7, 2.5e6),
        name="heads_to_stream",
    )(heads, wo_all, residual, gains)


def pack_kernel(layer, up_ref, down_ref, out_ref, sems):
    rows = down_ref.shape[1]
    copies = [
        pltpu.make_async_copy(
            up_ref.at[layer, q * rows : (q + 1) * rows],
            out_ref.at[:rows, q * rows : (q + 1) * rows],
            sems.at[q],
        )
        for q in range(4)
    ]
    copies.append(pltpu.make_async_copy(down_ref.at[layer], out_ref.at[rows:, :], sems.at[4]))
    for copy in copies:
        copy.start()
    for copy in copies:
        copy.wait()


def pack(w_up, w_down, layer):
    d, hidden = w_up.shape[1:]
    return pl.pallas_call(
        functools.partial(pack_kernel, layer),
        in_specs=[hbm(), hbm()],
        out_specs=whole(),
        out_shape=sds((2 * hidden, d)),
        scratch_shapes=[pltpu.SemaphoreType.DMA((5,))],
        compiler_params=vm(63),
        cost_estimate=cost(1e5, 2e6),
        name="pack",
    )(w_up, w_down)


def feed_forward_kernel(b0, b1, b2, b3, w0, w1, w2, w3, p0, p1, p2, p3):
    rows = jnp.concatenate([b0[...], b1[...], b2[...], b3[...]], axis=0)
    total = None
    for w in (w0, w1, w2, w3):
        hidden = w.shape[0] // 2
        up = None
        for q in range(4):
            cols = slice(q * hidden, (q + 1) * hidden)
            part = jnp.dot(rows[:, cols], w[:hidden, cols], preferred_element_type=F32)
            up = part if up is None else up + part
        part = jnp.dot(jax.nn.gelu(up).astype(BF), w[hidden:, :], preferred_element_type=F32)
        total = part if total is None else total + part
    total = total.astype(BF)
    for k, p in enumerate((p0, p1, p2, p3)):
        p[...] = total[k * BLOCK : (k + 1) * BLOCK]


def feed_forward(blocks, shards):
    d = blocks[0].shape[1]
    return pl.pallas_call(
        feed_forward_kernel,
        in_specs=[whole()] * 8,
        out_specs=[whole()] * 4,
        out_shape=[sds((BLOCK, d))] * 4,
        compiler_params=vm(),
        cost_estimate=cost(5e8, 5e6),
        name="feed_forward",
    )(*blocks, *shards)


def pair_feed_forward_kernel(mine_ref, other_ref, w_ref, own_ref, send_ref, total, held, sems):
    count = held.shape[0]
    hidden = held.shape[1] * 16

    def copy(i):
        return pltpu.make_async_copy(w_ref.at[:, i], held.at[i], sems.at[i])

    for i in range(count):
        copy(i).start()
    rows = jnp.concatenate([mine_ref[...], other_ref[...]], axis=0)
    total[...] = jnp.zeros_like(total)

    def shard(i, carry):
        copy(i).wait()
        up = None
        for q in range(4):
            cols = slice(q * 256, (q + 1) * 256)
            weight = held[i, :, :16, cols].reshape(256, hidden)
            part = jnp.dot(rows[:, cols], weight, preferred_element_type=F32)
            up = part if up is None else up + part
        weight = held[i, :, 16:, :].reshape(hidden, rows.shape[1])
        total[...] += jnp.dot(jax.nn.gelu(up).astype(BF), weight, preferred_element_type=F32)
        return carry

    lax.fori_loop(0, count, shard, 0)
    own_ref[...] = total[:BLOCK, :].astype(BF)
    send_ref[...] = total[BLOCK:, :].astype(BF)


def pair_feed_forward(mine, other, weights):
    d = mine.shape[1]
    bands, count = weights.shape[:2]
    return pl.pallas_call(
        pair_feed_forward_kernel,
        in_specs=[whole(), whole(), hbm()],
        out_specs=[whole()] * 2,
        out_shape=[sds((BLOCK, d))] * 2,
        scratch_shapes=[
            pltpu.VMEM((2 * BLOCK, d), F32),
            pltpu.VMEM((count, bands, 32, d), BF),
            pltpu.SemaphoreType.DMA((count,)),
        ],
        compiler_params=vm(50),
        cost_estimate=cost(5e8, 9e6),
        name="pair_feed_forward",
    )(mine, other, weights)


def sixteenth_kernel(layer, place_ref, up_ref, down_ref, out_ref, sems):
    band = place_ref[0]
    copies = [
        pltpu.make_async_copy(
            up_ref.at[layer, q, band], out_ref.at[:16, q * 256 : (q + 1) * 256], sems.at[q]
        )
        for q in range(4)
    ]
    rows = pl.ds(pl.multiple_of(band * 16, 16), 16)
    copies.append(pltpu.make_async_copy(down_ref.at[layer, rows], out_ref.at[16:, :], sems.at[4]))
    for copy in copies:
        copy.start()
    for copy in copies:
        copy.wait()


def sixteenth(place, w_up, w_down, layer):
    d, hidden = w_up.shape[1:]
    return pl.pallas_call(
        functools.partial(sixteenth_kernel, layer),
        in_specs=[smem(), hbm(), hbm()],
        out_specs=whole(),
        out_shape=sds((32, d)),
        scratch_shapes=[pltpu.SemaphoreType.DMA((5,))],
        compiler_params=vm(63),
        cost_estimate=cost(1e5, 2e5),
        name="sixteenth",
    )(place, w_up.reshape(-1, 4, 16, 16, hidden), w_down)


def one_parity_kernel(place_ref, all_ref, out_ref, sems):
    core = place_ref[1] % 2
    copies = [
        pltpu.make_async_copy(all_ref.at[2 * i + core], out_ref.at[i], sems.at[i])
        for i in range(out_ref.shape[0])
    ]
    for copy in copies:
        copy.start()
    for copy in copies:
        copy.wait()


def one_parity(place, over_head):
    count, rows, d = over_head.shape
    return pl.pallas_call(
        one_parity_kernel,
        in_specs=[smem(), pl.BlockSpec(memory_space=pl.ANY)],
        out_specs=pl.BlockSpec(memory_space=pl.ANY),
        out_shape=sds((count // 2, rows, d)),
        scratch_shapes=[pltpu.SemaphoreType.DMA((count // 2,))],
        compiler_params=vm(),
        cost_estimate=cost(1e5, count * rows * d * 2),
        name="one_parity",
    )(place, over_head)


def shards(
    grid_latent,
    node_latent,
    src_index,
    in_degree,
    node_order,
    norm_gains,
    enc_wq,
    enc_wkv,
    enc_wo,
    proc_wqkv,
    proc_wo,
    w_up,
    w_down,
):
    d = grid_latent.shape[1]
    band = lax.axis_index("band")
    head = lax.axis_index("head")
    place = jnp.stack([band, head, grid_latent.shape[0], lax.axis_size("band")]).astype(jnp.int32)
    order = node_order[None, :]

    barrier = lax.optimization_barrier
    wo_all = lax.all_gather(proc_wo, "head")
    qkv_t = jnp.swapaxes(proc_wqkv, 2, 3).reshape(-1, d)
    tall = jnp.concatenate([qkv_t, enc_wo], axis=0)

    node_blocks = gather_group(node_latent)
    wkv_t = jnp.swapaxes(enc_wkv, 1, 2)
    grid_rows = grid_latent.shape[0]
    edge_low, edge_high, w_both = grid_kv(
        grid_latent, (0, grid_rows - EDGE), EDGE, gains=norm_gains, w=wkv_t
    )
    node_blocks, edge_low, edge_high = barrier((node_blocks, edge_low, edge_high))
    node_group = stack(node_blocks, d)
    node_pieces = exchange([node_group] * 4)
    from_low = up_band(edge_high)
    from_high = down_band(edge_low)

    w_up, w_down, grid_latent, _ = barrier((w_up, w_down, grid_latent, node_group))
    first = pack(w_up, w_down, 0)
    late_part = sixteenth(place, w_up, w_down, 1)
    middle = grid_kv(grid_latent, (EDGE,), grid_rows - 2 * EDGE, w_both=w_both)[0]
    sources, middle, first, late_part = barrier((src_index.T, middle, first, late_part))
    counts = edge_counts(place, sources, in_degree[None, :])
    node_pieces, counts, from_low, from_high, tall = barrier((node_pieces, counts, from_low, from_high, tall))

    tall_third, tall_other = outward(tall), swap(tall)
    queries, residual = node_queries(place, node_pieces, norm_gains, enc_wq.T, order)
    kv_parts = [from_low, edge_low, middle, edge_high, from_high]
    enc_heads = edge_attention(place, queries, kv_parts, counts, order)
    enc_heads, tall_third, tall_other, late_part, wo_all = barrier(
        (enc_heads, tall_third, tall_other, late_part, wo_all)
    )
    late_weights = lax.all_gather(late_part, "head")
    tall_shards = [tall, tall_other, tall_third, swap(tall_third)]
    sums = head_sum(give_back(enc_heads), tall_shards, qkv_t.shape[0] // HEAD_DIM)
    stream, normed = close_sum(residual, scatter_group(sums), norm_gains, 2)

    for layer in range(LAYERS):
        pieces = exchange(qkv(gather_group(normed), tall_shards, layer))
        kv = stack(pieces, 2 * HEAD_DIM)
        low = up_band(kv)
        high = down_band(kv)
        if layer == 0:
            first, _ = barrier((first, kv))
            first_third, first_other = outward(first), swap(first)
            low, high, late_weights, first_third, first_other = barrier(
                (low, high, late_weights, first_third, first_other)
            )
            late_weights = lax.all_gather(one_parity(place, late_weights), "band")
        win_heads = window_attention(place, pieces, kv, low, high)
        if layer == 0:
            first_shards = [first, first_other, first_third, swap(first_third)]
        win_heads = lax.all_to_all(win_heads, "head", 0, 0)
        stream, normed = heads_to_stream(win_heads, wo_all, layer, stream, norm_gains, 3 + 2 * layer)
        if layer == 0:
            parts = scatter_group(feed_forward(gather_group(normed), first_shards))
            stream, normed = close_sum(stream, parts, norm_gains, 4 + 2 * layer)
        else:
            own, other = pair_feed_forward(normed, swap(normed), late_weights)
            stream = final_sum(stream, [own, swap(other)])
    return stream


def solution(mesh):
    in_specs = (
        P("band", None),
        P(("band", "head"), None),
        P("band", None),
        P("band"),
        P("band"),
        P(),
        P(None, "head"),
        P(None, None, "head"),
        P("head", None),
        P(None, None, None, "head"),
        P(None, "head", None),
        P(None, None, "head"),
        P(None, "head", None),
    )
    out_specs = P(("band", "head"), None)
    return jax.shard_map(shards, mesh=mesh, in_specs=in_specs, out_specs=out_specs, check_vma=False)
```

```python
import functools
import math

import jax
import jax.numpy as jnp
from jax import lax
from jax.experimental import pallas as pl
from jax.experimental.pallas import tpu as pltpu
from jax.sharding import PartitionSpec as P

HEAD_DIM = 64
K_MAX = 32
HALF_WIN = 512
LAYERS = 2
EDGE = 1536
KV_BLOCK = 512
BLOCK = 32
GROUP = 128
NODES_HERE = 512
KEYS = 7168
SCALE = 1.0 / math.sqrt(HEAD_DIM)
BF = jnp.bfloat16
F32 = jnp.float32
NT = (((1,), (1,)), ((), ()))


def vm(limit_mib=20):
    return pltpu.CompilerParams(vmem_limit_bytes=limit_mib * 1024 * 1024)


def cost(flops, nbytes):
    return pl.CostEstimate(flops=int(flops), bytes_accessed=int(nbytes), transcendentals=0)


def whole():
    return pl.BlockSpec(memory_space=pltpu.VMEM)


def hbm():
    return pl.BlockSpec(memory_space=pltpu.HBM)


def smem():
    return pl.BlockSpec(memory_space=pltpu.SMEM)


def sds(shape, dtype=BF):
    return jax.ShapeDtypeStruct(shape, dtype)


def swap(x):
    return lax.ppermute(x, "head", [(i, i ^ 1) for i in range(16)])


def shift_z(x, k):
    steps = (k, -k)
    return lax.ppermute(x, "head", [(i, ((i // 2 + steps[i % 2]) % 8) * 2 + i % 2) for i in range(16)])


def outward_pairs():
    return [(2 * z + c, 2 * ((z + (1 if c else -1)) % 8) + c) for z in range(8) for c in range(2)]


def outward(x):
    return lax.ppermute(x, "head", outward_pairs())


def inward(x):
    return lax.ppermute(x, "head", [(t, s) for s, t in outward_pairs()])


def crossed(x):
    pairs = [(2 * z, 2 * ((z - 1) % 8) + 1) for z in range(8)]
    return lax.ppermute(x, "head", pairs + [(t, s) for s, t in pairs])


def up_band(x):
    return lax.ppermute(x, "band", [(i, i + 1) for i in range(15)])


def down_band(x):
    return lax.ppermute(x, "band", [(i + 1, i) for i in range(15)])


def gather_group(x):
    behind = shift_z(x, 2)
    ahead = shift_z(x, -2)
    far = shift_z(x, 4)
    return [x, ahead, far, behind]


def scatter_group(parts):
    return [parts[0], shift_z(parts[1], 2), shift_z(parts[2], 4), shift_z(parts[3], -2)]


def four_shards(x):
    third = outward(x)
    return [x, swap(x), third, swap(third)]


def exchange(pieces):
    return [pieces[0], swap(pieces[1]), inward(pieces[2]), crossed(pieces[3])]


def give_back(pieces):
    return [pieces[0], swap(pieces[1]), outward(pieces[2]), crossed(pieces[3])]


def stack_kernel(b0, b1, b2, b3, out_ref):
    rows, cols = b0.shape[0], out_ref.shape[1]
    for k, b in enumerate((b0, b1, b2, b3)):
        out_ref[k * rows : (k + 1) * rows, :] = b[:, :cols]


def stack(blocks, cols):
    rows = blocks[0].shape[0]
    return pl.pallas_call(
        stack_kernel,
        in_specs=[whole()] * 4,
        out_specs=whole(),
        out_shape=sds((4 * rows, cols)),
        compiler_params=vm(),
        cost_estimate=cost(1e5, 4 * rows * cols * 4),
        name="stack",
    )(*blocks)


def normed_rows(values, gain):
    mean = jnp.mean(values, axis=-1, keepdims=True)
    centred = values - mean
    variance = jnp.mean(centred * centred, axis=-1, keepdims=True)
    return (centred * lax.rsqrt(variance + 1e-05) * gain).astype(BF)


def grid_kv_kernel(starts, first, x_ref, *refs):
    if first:
        gain_ref, w_ref, *refs = refs
    else:
        w_both, *refs = refs
    outs, refs = refs[: len(starts)], refs[len(starts) :]
    if first:
        w_both, *refs = refs
    rows, sems = refs
    blocks = outs[0].shape[0] // KV_BLOCK
    copies = [
        pltpu.make_async_copy(
            x_ref.at[pl.ds(start + i * KV_BLOCK, KV_BLOCK)],
            rows.at[part * blocks + i],
            sems.at[part * blocks + i],
        )
        for part, start in enumerate(starts)
        for i in range(blocks)
    ]
    for copy in copies:
        copy.start()
    if first:
        for i in range(2):
            turned = jnp.transpose(w_ref[i].astype(F32) * gain_ref[0:1, :]).astype(BF)
            w_both[:, i * HEAD_DIM : (i + 1) * HEAD_DIM] = turned
    for part, out in enumerate(outs):
        for i in range(blocks):
            copies[part * blocks + i].wait()

            x = rows[part * blocks + i].astype(F32)
            x = x - jnp.mean(x, axis=-1, keepdims=True)
            variance = jnp.mean(x * x, axis=-1, keepdims=True)
            scale = lax.rsqrt(variance + 1e-05)
            x = x.astype(BF)
            for line in range(0, KV_BLOCK, 128):
                kv = jnp.dot(x[line : line + 128], w_both[...], preferred_element_type=F32)
                at = i * KV_BLOCK + line
                out[at : at + 128, :] = (kv * scale[line : line + 128]).astype(BF)


def grid_kv(grid_latent, starts, count, gains=None, w=None, w_both=None):
    d = grid_latent.shape[1]
    blocks = len(starts) * count // KV_BLOCK
    first = w_both is None
    weight_shape = sds((d, 128))
    out_shape = [sds((count, 128))] * len(starts) + ([weight_shape] if first else [])
    return pl.pallas_call(
        functools.partial(grid_kv_kernel, starts, first),
        in_specs=[hbm()] + [whole()] * (2 if first else 1),
        out_specs=[whole()] * len(out_shape),
        out_shape=out_shape,
        scratch_shapes=[
            pltpu.VMEM((blocks, KV_BLOCK, d), BF),
            pltpu.SemaphoreType.DMA((blocks,)),
        ],
        compiler_params=vm(56),
        cost_estimate=cost(2 * blocks * KV_BLOCK * d * 128, blocks * KV_BLOCK * d * 2),
        name="grid_kv",
    )(grid_latent, *((gains, w) if first else (w_both,)))


COUNT_STEP = 64
TILES = KEYS // 128


def edge_count_kernel(place_ref, src_ref, degree_ref, out_ref, by_node, high_key, low_key):
    step = pl.program_id(0)

    @pl.when(step == 0)
    def _():
        shape = src_ref.shape
        local = src_ref[...] - (place_ref[0] * place_ref[2] - EDGE)
        used = lax.broadcasted_iota(jnp.int32, shape, 0) < degree_ref[...]
        by_node[...] = jnp.transpose(jnp.where(used, local, -1))
        for t in range(8):
            local_rows = by_node[pl.ds(t, NODES_HERE // 8, stride=8), :]
            cols = slice(t * K_MAX, (t + 1) * K_MAX)
            high_key[:, cols] = jnp.where(local_rows < 0, -1, (local_rows >> 7) * 8 + t)
            low_key[:, cols] = local_rows & 127

    row_high = lax.broadcasted_iota(jnp.int32, (TILES * 8, 256), 0)
    row_low = lax.broadcasted_iota(jnp.int32, (128, 256), 0)

    def counts(group):
        left = jnp.where(row_high == high_key[pl.ds(group, 1), :], 1.0, 0.0).astype(BF)
        right = jnp.where(row_low == low_key[pl.ds(group, 1), :], 1.0, 0.0).astype(BF)
        return lax.dot_general(left, right, NT, preferred_element_type=F32)

    def pair(i, carry):
        group = step * (COUNT_STEP // 8) + 2 * i
        first = counts(group)
        second = counts(group + 1)
        rows = pl.ds(pl.multiple_of(i * 16, 16), 16)
        for t in range(TILES):
            both = jnp.concatenate([first[t * 8 : t * 8 + 8], second[t * 8 : t * 8 + 8]], axis=0)
            out_ref[rows, t * 128 : (t + 1) * 128] = both.astype(BF)
        return carry

    lax.fori_loop(0, COUNT_STEP // 16, pair, 0, unroll=COUNT_STEP // 16)


def edge_counts(place, sources, degrees):
    return pl.pallas_call(
        edge_count_kernel,
        grid=(NODES_HERE // COUNT_STEP,),
        in_specs=[
            smem(),
            pl.BlockSpec(sources.shape, lambda i: (0, 0)),
            pl.BlockSpec(degrees.shape, lambda i: (0, 0)),
        ],
        out_specs=pl.BlockSpec((COUNT_STEP, KEYS), lambda i: (i, 0)),
        out_shape=sds((NODES_HERE, KEYS)),
        scratch_shapes=[
            pltpu.VMEM((NODES_HERE, K_MAX), jnp.int32),
            pltpu.VMEM((NODES_HERE // 8, 8 * K_MAX), jnp.int32),
            pltpu.VMEM((NODES_HERE // 8, 8 * K_MAX), jnp.int32),
        ],
        compiler_params=vm(),
        cost_estimate=cost(4e9, 10e6),
        name="edge_counts",
    )(place, sources, degrees)


def block_places(head):
    z, core = head // 2, head % 2
    side = 2 * core - 1
    places = []
    for g in range(4):
        from_z = z if g < 2 else z + side
        from_core = core if g % 2 == 0 else 1 - core
        step = 2 - 4 * from_core
        places += [2 * ((from_z + step * k + 16) & 7) + from_core for k in range(4)]
    return places


def row_positions(places):
    lane = lax.broadcasted_iota(jnp.int32, (1, NODES_HERE), 1)
    pos = jnp.zeros((1, NODES_HERE), jnp.int32)
    for i, place in enumerate(places):
        pos = jnp.where(lane // BLOCK == i, place * BLOCK + lane % BLOCK, pos)
    return pos


def node_query_kernel(place_ref, r0, r1, r2, r3, gain_ref, w_ref, order_ref, q_ref, mine_ref, order_col, rows):
    head = place_ref[1]
    places = block_places(head)
    for g, r in enumerate((r0, r1, r2, r3)):
        rows[g * GROUP : (g + 1) * GROUP, :] = r[...]
        normed = normed_rows(r[...].astype(F32), gain_ref[1:2, :])
        q = lax.dot_general(normed, w_ref[...], NT, preferred_element_type=F32).astype(BF)
        for k in range(4):
            start = pl.multiple_of(places[g * 4 + k] * BLOCK, BLOCK)
            q_ref[pl.ds(start, BLOCK), :] = q[k * BLOCK : (k + 1) * BLOCK, :]
    local = order_ref[...] - place_ref[0] * NODES_HERE
    order_col[...] = jnp.transpose(jnp.broadcast_to(local, (8, NODES_HERE)))
    wanted = order_col[pl.ds(pl.multiple_of(head * BLOCK, BLOCK), BLOCK), 0:1]
    pick = jnp.where(row_positions(places) == wanted, 1.0, 0.0).astype(BF)
    mine_ref[...] = jnp.dot(pick, rows[...], preferred_element_type=F32).astype(BF)


def node_queries(place, pieces, gains, wq_t, order):
    d = wq_t.shape[1]
    return pl.pallas_call(
        node_query_kernel,
        in_specs=[smem()] + [whole()] * 7,
        out_specs=[whole()] * 2,
        out_shape=[sds((NODES_HERE, HEAD_DIM)), sds((BLOCK, d))],
        scratch_shapes=[pltpu.VMEM((NODES_HERE, 8), jnp.int32), pltpu.VMEM((NODES_HERE, d), BF)],
        compiler_params=vm(),
        cost_estimate=cost(1e8, 2e6),
        name="node_queries",
    )(place, *pieces, gains, wq_t, order)


T_STEP = 128
CHUNK = 512


def edge_attention_kernel(
    place_ref, q_all, kv0, kv1, kv2, kv3, kv4, count_ref, order_ref,
    o0, o1, o2, o3, scores, heads, pick, order_col,
):
    step = pl.program_id(0)
    q = q_all[pl.ds(pl.multiple_of(step * T_STEP, T_STEP), T_STEP), :]
    chunks = []
    for kv in (kv0, kv1, kv2, kv3, kv4):
        for start in range(0, kv.shape[0], CHUNK):
            chunks.append((kv, start))
    top = None
    for i, (kv, start) in enumerate(chunks):
        keys = kv[start : start + CHUNK, :][:, :HEAD_DIM]
        s = lax.dot_general(q, keys, NT, preferred_element_type=F32) * SCALE
        cols = slice(i * CHUNK, (i + 1) * CHUNK)
        s = jnp.where(count_ref[:, cols].astype(F32) > 0.0, s, -jnp.inf)
        scores[:, cols] = s
        part = jnp.maximum(
            jnp.maximum(s[:, 0:128], s[:, 128:256]), jnp.maximum(s[:, 256:384], s[:, 384:512])
        )
        top = part if top is None else jnp.maximum(top, part)
    top = jnp.max(top, axis=-1, keepdims=True)
    total = jnp.zeros((T_STEP, 128), F32)
    out = jnp.zeros((T_STEP, 128), F32)
    for i, (kv, start) in enumerate(chunks):
        cols = slice(i * CHUNK, (i + 1) * CHUNK)
        e = jnp.exp(scores[:, cols] - top) * count_ref[:, cols].astype(F32)
        total += (e[:, 0:128] + e[:, 128:256]) + (e[:, 256:384] + e[:, 384:512])
        out += jnp.dot(e.astype(BF), kv[start : start + CHUNK, :], preferred_element_type=F32)
    total = jnp.sum(total, axis=-1, keepdims=True)
    rows = pl.ds(pl.multiple_of(step * T_STEP, T_STEP), T_STEP)
    heads[rows, :] = (out / total).astype(BF)

    @pl.when(step == pl.num_programs(0) - 1)
    def _():
        local = order_ref[...] - place_ref[0] * NODES_HERE
        order_col[...] = jnp.transpose(jnp.broadcast_to(local, (8, NODES_HERE)))
        places = block_places(place_ref[1])
        node = lax.broadcasted_iota(jnp.int32, (BLOCK, NODES_HERE), 1)
        for g, o in enumerate((o0, o1, o2, o3)):
            for k in range(4):
                start = pl.multiple_of(places[g * 4 + k] * BLOCK, BLOCK)
                wanted = order_col[pl.ds(start, BLOCK), 0:1]
                pick[k * BLOCK : (k + 1) * BLOCK, :] = jnp.where(node == wanted, 1.0, 0.0).astype(BF)
            taken = jnp.dot(pick[...], heads[...], preferred_element_type=F32)
            o[...] = taken[:, HEAD_DIM:].astype(BF)


def edge_attention(place, queries, kv_parts, counts, order):
    def full(x):
        return pl.BlockSpec(x.shape, lambda i: (0,) * x.ndim)

    return pl.pallas_call(
        edge_attention_kernel,
        grid=(NODES_HERE // T_STEP,),
        in_specs=[smem(), full(queries)]
        + [full(kv) for kv in kv_parts]
        + [pl.BlockSpec((T_STEP, KEYS), lambda i: (i, 0)), full(order)],
        out_specs=[pl.BlockSpec((GROUP, HEAD_DIM), lambda i: (0, 0))] * 4,
        out_shape=[sds((GROUP, HEAD_DIM))] * 4,
        scratch_shapes=[
            pltpu.VMEM((T_STEP, KEYS), F32),
            pltpu.VMEM((NODES_HERE, 128), BF),
            pltpu.VMEM((GROUP, NODES_HERE), BF),
            pltpu.VMEM((NODES_HERE, 8), jnp.int32),
        ],
        compiler_params=vm(40),
        cost_estimate=cost(2e9, 12e6),
        name="edge_attention",
    )(place, queries, *kv_parts, counts, order)


def head_sum_kernel(h0, h1, h2, h3, w0, w1, w2, w3, p0, p1, p2, p3):
    heads = jnp.concatenate([h0[...], h1[...], h2[...], h3[...]], axis=1)
    rows = jnp.concatenate([w0[...], w1[...], w2[...], w3[...]], axis=0)
    total = jnp.dot(heads, rows, preferred_element_type=F32).astype(BF)
    for k, p in enumerate((p0, p1, p2, p3)):
        p[...] = total[k * BLOCK : (k + 1) * BLOCK]


def head_sum(heads, shards, row_block):
    d = shards[0].shape[1]
    full = pl.BlockSpec((GROUP, HEAD_DIM), lambda i: (0, 0))
    return pl.pallas_call(
        head_sum_kernel,
        grid=(1,),
        in_specs=[full] * 4 + [pl.BlockSpec((HEAD_DIM, d), lambda i: (row_block, 0))] * 4,
        out_specs=[pl.BlockSpec((BLOCK, d), lambda i: (0, 0))] * 4,
        out_shape=[sds((BLOCK, d))] * 4,
        compiler_params=vm(),
        cost_estimate=cost(7e7, 1e6),
        name="head_sum",
    )(*heads, *shards)


def close_sum_kernel(gain_row, r_ref, p0, p1, p2, p3, gain_ref, stream_ref, normed_ref):
    total = (p0[...].astype(F32) + p1[...].astype(F32)) + (p2[...].astype(F32) + p3[...].astype(F32))
    stream = (r_ref[...].astype(F32) + total).astype(BF)
    stream_ref[...] = stream
    normed_ref[...] = normed_rows(stream.astype(F32), gain_ref[gain_row : gain_row + 1, :])


def close_sum(residual, parts, gains, gain_row):
    shape = residual.shape
    return pl.pallas_call(
        functools.partial(close_sum_kernel, gain_row),
        in_specs=[whole()] * 6,
        out_specs=[whole()] * 2,
        out_shape=[sds(shape), sds(shape)],
        compiler_params=vm(),
        cost_estimate=cost(1e6, 4e5),
        name="close_sum",
    )(residual, *parts, gains)


def final_sum_kernel(r_ref, p0, p1, stream_ref):
    total = p0[...].astype(F32) + p1[...].astype(F32)
    stream_ref[...] = (r_ref[...].astype(F32) + total).astype(BF)


def final_sum(residual, parts):
    return pl.pallas_call(
        final_sum_kernel,
        in_specs=[whole()] * 3,
        out_specs=whole(),
        out_shape=sds(residual.shape),
        compiler_params=vm(),
        cost_estimate=cost(1e6, 4e5),
        name="final_sum",
    )(residual, *parts)


def qkv_kernel(b0, b1, b2, b3, w0, w1, w2, w3, p0, p1, p2, p3):
    rows = jnp.concatenate([b0[...], b1[...], b2[...], b3[...]], axis=0)
    for w, out in ((w0, p0), (w1, p1), (w2, p2), (w3, p3)):
        all_cols = lax.dot_general(rows, w[...], NT, preferred_element_type=F32).astype(BF)
        out[:, :128] = all_cols[:, HEAD_DIM:]
        out[:, 128:] = all_cols[:, :HEAD_DIM]


def qkv(blocks, shards, layer):
    d = blocks[0].shape[1]
    return pl.pallas_call(
        qkv_kernel,
        grid=(1,),
        in_specs=[pl.BlockSpec((BLOCK, d), lambda i: (0, 0))] * 4
        + [pl.BlockSpec((3 * HEAD_DIM, d), lambda i: (layer, 0))] * 4,
        out_specs=[pl.BlockSpec((GROUP, 3 * HEAD_DIM), lambda i: (0, 0))] * 4,
        out_shape=[sds((GROUP, 3 * HEAD_DIM))] * 4,
        compiler_params=vm(),
        cost_estimate=cost(3e8, 2.5e6),
        name="qkv",
    )(*blocks, *shards)


def window_kernel(place_ref, a0, a1, a2, a3, kv_ref, low_ref, high_ref, out_ref):
    kv = kv_ref[...]
    low = low_ref[...]
    high = high_ref[...]
    has_low = place_ref[0] > 0
    has_high = place_ref[0] < place_ref[3] - 1
    places = block_places(place_ref[1])
    col = row_positions(places)
    line = lax.broadcasted_iota(jnp.int32, (GROUP, 1), 0)
    for g, a in enumerate((a0, a1, a2, a3)):
        q = a[:, 128:]
        row = jnp.zeros((GROUP, 1), jnp.int32)
        for k in range(4):
            row = jnp.where(line // BLOCK == k, places[g * 4 + k] * BLOCK + line % BLOCK, row)
        s_own = lax.dot_general(q, kv[:, :HEAD_DIM], NT, preferred_element_type=F32) * SCALE
        s_low = lax.dot_general(q, low[:, :HEAD_DIM], NT, preferred_element_type=F32) * SCALE
        s_high = lax.dot_general(q, high[:, :HEAD_DIM], NT, preferred_element_type=F32) * SCALE
        after = col >= row
        in_low = jnp.logical_and(after, has_low)
        in_high = jnp.logical_and(jnp.logical_not(after), has_high)
        s_far = jnp.where(in_low, s_low, jnp.where(in_high, s_high, -jnp.inf))
        top = jnp.maximum(
            jnp.max(s_own, axis=-1, keepdims=True), jnp.max(s_far, axis=-1, keepdims=True)
        )
        e_own = jnp.exp(s_own - top)
        e_far = jnp.exp(s_far - top)
        total = jnp.sum(e_own + e_far, axis=-1, keepdims=True)
        e_low = jnp.where(in_low, e_far, 0.0).astype(BF)
        e_high = jnp.where(in_high, e_far, 0.0).astype(BF)
        out = jnp.dot(e_own.astype(BF), kv, preferred_element_type=F32)
        out += jnp.dot(e_low, low, preferred_element_type=F32)
        out += jnp.dot(e_high, high, preferred_element_type=F32)
        heads = (out / total)[:, HEAD_DIM:].astype(BF)
        for k in range(4):
            out_ref[places[g * 4 + k]] = heads[k * BLOCK : (k + 1) * BLOCK]


def window_attention(place, pieces, kv, low, high):
    return pl.pallas_call(
        window_kernel,
        in_specs=[smem()] + [whole()] * 7,
        out_specs=whole(),
        out_shape=sds((NODES_HERE // BLOCK, BLOCK, HEAD_DIM)),
        compiler_params=vm(),
        cost_estimate=cost(4e8, 1e6),
        name="window_attention",
    )(place, *pieces, kv, low, high)


def one_layer_kernel(w_ref, out_ref):
    out_ref[...] = w_ref[:, 0].reshape(out_ref.shape)


def one_layer(wo_all, layer):
    count, _, rows, d = wo_all.shape
    return pl.pallas_call(
        one_layer_kernel,
        grid=(4,),
        in_specs=[pl.BlockSpec((count // 4, 1, rows, d), lambda i: (i, layer, 0, 0))],
        out_specs=pl.BlockSpec((count // 4 * rows, d), lambda i: (i, 0)),
        out_shape=sds((count * rows, d)),
        compiler_params=vm(),
        cost_estimate=cost(1e5, 2 * count * rows * d * 2),
        name="one_layer",
    )(wo_all)


def heads_to_stream_kernel(gain_row, heads_ref, wo_ref, r_ref, gain_ref, stream_ref, normed_ref):
    count = heads_ref.shape[0]
    heads = jnp.concatenate([heads_ref[h] for h in range(count)], axis=1)
    total = jnp.dot(heads, wo_ref[...], preferred_element_type=F32)
    stream = (r_ref[...].astype(F32) + total).astype(BF)
    stream_ref[...] = stream
    normed_ref[...] = normed_rows(stream.astype(F32), gain_ref[gain_row : gain_row + 1, :])


def heads_to_stream(heads, wo, residual, gains, gain_row):
    return pl.pallas_call(
        functools.partial(heads_to_stream_kernel, gain_row),
        in_specs=[whole()] * 4,
        out_specs=[whole()] * 2,
        out_shape=[sds(residual.shape)] * 2,
        compiler_params=vm(),
        cost_estimate=cost(7e7, 2.5e6),
        name="heads_to_stream",
    )(heads, wo, residual, gains)


def pack_kernel(layer, up_ref, down_ref, out_ref, sems):
    rows = down_ref.shape[1]
    copies = [
        pltpu.make_async_copy(
            up_ref.at[layer, q * rows : (q + 1) * rows],
            out_ref.at[:rows, q * rows : (q + 1) * rows],
            sems.at[q],
        )
        for q in range(4)
    ]
    copies.append(pltpu.make_async_copy(down_ref.at[layer], out_ref.at[rows:, :], sems.at[4]))
    for copy in copies:
        copy.start()
    for copy in copies:
        copy.wait()


def pack(w_up, w_down, layer):
    d, hidden = w_up.shape[1:]
    return pl.pallas_call(
        functools.partial(pack_kernel, layer),
        in_specs=[hbm(), hbm()],
        out_specs=whole(),
        out_shape=sds((2 * hidden, d)),
        scratch_shapes=[pltpu.SemaphoreType.DMA((5,))],
        compiler_params=vm(),
        cost_estimate=cost(1e5, 2e6),
        name="pack",
    )(w_up, w_down)


def feed_forward_kernel(b0, b1, b2, b3, w0, w1, w2, w3, p0, p1, p2, p3):
    rows = jnp.concatenate([b0[...], b1[...], b2[...], b3[...]], axis=0)
    total = None
    for w in (w0, w1, w2, w3):
        hidden = w.shape[0] // 2
        up = None
        for q in range(4):
            cols = slice(q * hidden, (q + 1) * hidden)
            part = jnp.dot(rows[:, cols], w[:hidden, cols], preferred_element_type=F32)
            up = part if up is None else up + part
        part = jnp.dot(jax.nn.gelu(up).astype(BF), w[hidden:, :], preferred_element_type=F32)
        total = part if total is None else total + part
    total = total.astype(BF)
    for k, p in enumerate((p0, p1, p2, p3)):
        p[...] = total[k * BLOCK : (k + 1) * BLOCK]


def feed_forward(blocks, shards):
    d = blocks[0].shape[1]
    return pl.pallas_call(
        feed_forward_kernel,
        in_specs=[whole()] * 8,
        out_specs=[whole()] * 4,
        out_shape=[sds((BLOCK, d))] * 4,
        compiler_params=vm(),
        cost_estimate=cost(5e8, 5e6),
        name="feed_forward",
    )(*blocks, *shards)


def pair_feed_forward_kernel(mine_ref, other_ref, w_ref, own_ref, send_ref, total, held, sems):
    count = held.shape[0]
    hidden = held.shape[1] * 16

    def copy(i):
        return pltpu.make_async_copy(w_ref.at[:, i], held.at[i], sems.at[i])

    for i in range(count):
        copy(i).start()
    rows = jnp.concatenate([mine_ref[...], other_ref[...]], axis=0)
    total[...] = jnp.zeros_like(total)

    def shard(i, carry):
        copy(i).wait()
        up = None
        for q in range(4):
            cols = slice(q * 256, (q + 1) * 256)
            weight = held[i, :, :16, cols].reshape(256, hidden)
            part = jnp.dot(rows[:, cols], weight, preferred_element_type=F32)
            up = part if up is None else up + part
        weight = held[i, :, 16:, :].reshape(hidden, rows.shape[1])
        total[...] += jnp.dot(jax.nn.gelu(up).astype(BF), weight, preferred_element_type=F32)
        return carry

    lax.fori_loop(0, count, shard, 0)
    own_ref[...] = total[:BLOCK, :].astype(BF)
    send_ref[...] = total[BLOCK:, :].astype(BF)


def pair_feed_forward(mine, other, weights):
    d = mine.shape[1]
    bands, count = weights.shape[:2]
    return pl.pallas_call(
        pair_feed_forward_kernel,
        in_specs=[whole(), whole(), hbm()],
        out_specs=[whole()] * 2,
        out_shape=[sds((BLOCK, d))] * 2,
        scratch_shapes=[
            pltpu.VMEM((2 * BLOCK, d), F32),
            pltpu.VMEM((count, bands, 32, d), BF),
            pltpu.SemaphoreType.DMA((count,)),
        ],
        compiler_params=vm(50),
        cost_estimate=cost(5e8, 9e6),
        name="pair_feed_forward",
    )(mine, other, weights)


def sixteenth_kernel(layer, place_ref, up_ref, down_ref, out_ref, sems):
    band = place_ref[0]
    copies = [
        pltpu.make_async_copy(
            up_ref.at[layer, q, band], out_ref.at[:16, q * 256 : (q + 1) * 256], sems.at[q]
        )
        for q in range(4)
    ]
    rows = pl.ds(pl.multiple_of(band * 16, 16), 16)
    copies.append(pltpu.make_async_copy(down_ref.at[layer, rows], out_ref.at[16:, :], sems.at[4]))
    for copy in copies:
        copy.start()
    for copy in copies:
        copy.wait()


def sixteenth(place, w_up, w_down, layer):
    d, hidden = w_up.shape[1:]
    return pl.pallas_call(
        functools.partial(sixteenth_kernel, layer),
        in_specs=[smem(), hbm(), hbm()],
        out_specs=whole(),
        out_shape=sds((32, d)),
        scratch_shapes=[pltpu.SemaphoreType.DMA((5,))],
        compiler_params=vm(63),
        cost_estimate=cost(1e5, 2e5),
        name="sixteenth",
    )(place, w_up.reshape(-1, 4, 16, 16, hidden), w_down)


def one_parity_kernel(place_ref, all_ref, out_ref, sems):
    core = place_ref[1] % 2
    copies = [
        pltpu.make_async_copy(all_ref.at[2 * i + core], out_ref.at[i], sems.at[i])
        for i in range(out_ref.shape[0])
    ]
    for copy in copies:
        copy.start()
    for copy in copies:
        copy.wait()


def one_parity(place, over_head):
    count, rows, d = over_head.shape
    return pl.pallas_call(
        one_parity_kernel,
        in_specs=[smem(), pl.BlockSpec(memory_space=pl.ANY)],
        out_specs=pl.BlockSpec(memory_space=pl.ANY),
        out_shape=sds((count // 2, rows, d)),
        scratch_shapes=[pltpu.SemaphoreType.DMA((count // 2,))],
        compiler_params=vm(),
        cost_estimate=cost(1e5, count * rows * d * 2),
        name="one_parity",
    )(place, over_head)


def shards(
    grid_latent,
    node_latent,
    src_index,
    in_degree,
    node_order,
    norm_gains,
    enc_wq,
    enc_wkv,
    enc_wo,
    proc_wqkv,
    proc_wo,
    w_up,
    w_down,
):
    d = grid_latent.shape[1]
    band = lax.axis_index("band")
    head = lax.axis_index("head")
    place = jnp.stack([band, head, grid_latent.shape[0], lax.axis_size("band")]).astype(jnp.int32)
    order = node_order[None, :]

    barrier = lax.optimization_barrier
    wo_all = lax.all_gather(proc_wo, "head")
    qkv_t = jnp.swapaxes(proc_wqkv, 2, 3).reshape(-1, d)
    tall = jnp.concatenate([qkv_t, enc_wo], axis=0)

    node_blocks = gather_group(node_latent)
    wkv_t = jnp.swapaxes(enc_wkv, 1, 2)
    grid_rows = grid_latent.shape[0]
    edge_low, edge_high, w_both = grid_kv(
        grid_latent, (0, grid_rows - EDGE), EDGE, gains=norm_gains, w=wkv_t
    )
    node_blocks, edge_low, edge_high = barrier((node_blocks, edge_low, edge_high))
    node_group = stack(node_blocks, d)
    node_pieces = exchange([node_group] * 4)
    from_low = up_band(edge_high)
    from_high = down_band(edge_low)

    w_up, w_down, grid_latent, _ = barrier((w_up, w_down, grid_latent, node_group))
    late_part = sixteenth(place, w_up, w_down, 1)
    middle = grid_kv(grid_latent, (EDGE,), grid_rows - 2 * EDGE, w_both=w_both)[0]
    sources, middle, late_part = barrier((src_index.T, middle, late_part))
    counts = edge_counts(place, sources, in_degree[None, :])
    node_pieces, counts, from_low, from_high, tall = barrier((node_pieces, counts, from_low, from_high, tall))

    tall_third, tall_other = outward(tall), swap(tall)
    queries, residual = node_queries(place, node_pieces, norm_gains, enc_wq.T, order)
    kv_parts = [from_low, edge_low, middle, edge_high, from_high]
    enc_heads = edge_attention(place, queries, kv_parts, counts, order)
    enc_heads, tall_third, tall_other, late_part, wo_all = barrier(
        (enc_heads, tall_third, tall_other, late_part, wo_all)
    )
    late_weights = lax.all_gather(late_part, "head")
    tall_shards = [tall, tall_other, tall_third, swap(tall_third)]
    sums = head_sum(give_back(enc_heads), tall_shards, qkv_t.shape[0] // HEAD_DIM)
    stream, normed = close_sum(residual, scatter_group(sums), norm_gains, 2)

    for layer in range(LAYERS):
        blocks = gather_group(normed)
        if layer == 0:
            w_up, w_down, _ = barrier((w_up, w_down, normed))
            blocks, first = barrier((blocks, pack(w_up, w_down, 0)))
        pieces = exchange(qkv(blocks, tall_shards, layer))
        kv = stack(pieces, 2 * HEAD_DIM)
        low = up_band(kv)
        high = down_band(kv)
        wo_all, _ = barrier((wo_all, kv))
        wo = one_layer(wo_all, layer)
        low, high, wo = barrier((low, high, wo))
        if layer == 0:
            first, late_weights, _ = barrier((first, late_weights, kv))
            first_third, first_other = outward(first), swap(first)
            late_weights = one_parity(place, late_weights)
            low, high, late_weights, first_third, first_other = barrier(
                (low, high, late_weights, first_third, first_other)
            )
            late_weights = lax.all_gather(late_weights, "band")
        win_heads = window_attention(place, pieces, kv, low, high)
        if layer == 0:
            first_shards = [first, first_other, first_third, swap(first_third)]
        win_heads = lax.all_to_all(win_heads, "head", 0, 0)
        stream, normed = heads_to_stream(win_heads, wo, stream, norm_gains, 3 + 2 * layer)
        if layer == 0:
            parts = scatter_group(feed_forward(gather_group(normed), first_shards))
            stream, normed = close_sum(stream, parts, norm_gains, 4 + 2 * layer)
        else:
            own, other = pair_feed_forward(normed, swap(normed), late_weights)
            stream = final_sum(stream, [own, swap(other)])
    return stream


def solution(mesh):
    in_specs = (
        P("band", None),
        P(("band", "head"), None),
        P("band", None),
        P("band"),
        P("band"),
        P(),
        P(None, "head"),
        P(None, None, "head"),
        P("head", None),
        P(None, None, None, "head"),
        P(None, "head", None),
        P(None, None, "head"),
        P(None, "head", None),
    )
    out_specs = P(("band", "head"), None)
    return jax.shard_map(shards, mesh=mesh, in_specs=in_specs, out_specs=out_specs, check_vma=False)
```

```python
import functools
import math

import jax
import jax.numpy as jnp
from jax import lax
from jax.experimental import pallas as pl
from jax.experimental.pallas import tpu as pltpu
from jax.sharding import PartitionSpec as P

HEAD_DIM = 64
K_MAX = 32
HALF_WIN = 512
LAYERS = 2
EDGE = 1536
KV_BLOCK = 512
BLOCK = 32
GROUP = 128
NODES_HERE = 512
KEYS = 7168
SCALE = 1.0 / math.sqrt(HEAD_DIM)
BF = jnp.bfloat16
F32 = jnp.float32
NT = (((1,), (1,)), ((), ()))


def vm(limit_mib=20):
    return pltpu.CompilerParams(vmem_limit_bytes=limit_mib * 1024 * 1024)


def cost(flops, nbytes):
    return pl.CostEstimate(flops=int(flops), bytes_accessed=int(nbytes), transcendentals=0)


def whole():
    return pl.BlockSpec(memory_space=pltpu.VMEM)


def hbm():
    return pl.BlockSpec(memory_space=pltpu.HBM)


def smem():
    return pl.BlockSpec(memory_space=pltpu.SMEM)


def sds(shape, dtype=BF):
    return jax.ShapeDtypeStruct(shape, dtype)


def swap(x):
    return lax.ppermute(x, "head", [(i, i ^ 1) for i in range(16)])


def shift_z(x, k):
    steps = (k, -k)
    return lax.ppermute(x, "head", [(i, ((i // 2 + steps[i % 2]) % 8) * 2 + i % 2) for i in range(16)])


def outward_pairs():
    return [(2 * z + c, 2 * ((z + (1 if c else -1)) % 8) + c) for z in range(8) for c in range(2)]


def outward(x):
    return lax.ppermute(x, "head", outward_pairs())


def inward(x):
    return lax.ppermute(x, "head", [(t, s) for s, t in outward_pairs()])


def crossed(x):
    pairs = [(2 * z, 2 * ((z - 1) % 8) + 1) for z in range(8)]
    return lax.ppermute(x, "head", pairs + [(t, s) for s, t in pairs])


def up_band(x):
    return lax.ppermute(x, "band", [(i, i + 1) for i in range(15)])


def down_band(x):
    return lax.ppermute(x, "band", [(i + 1, i) for i in range(15)])


def gather_group(x):
    behind = shift_z(x, 2)
    ahead = shift_z(x, -2)
    far = shift_z(x, 4)
    return [x, ahead, far, behind]


def scatter_group(parts):
    return [parts[0], shift_z(parts[1], 2), shift_z(parts[2], 4), shift_z(parts[3], -2)]


def four_shards(x):
    third = outward(x)
    return [x, swap(x), third, swap(third)]


def exchange(pieces):
    return [pieces[0], swap(pieces[1]), inward(pieces[2]), crossed(pieces[3])]


def give_back(pieces):
    return [pieces[0], swap(pieces[1]), outward(pieces[2]), crossed(pieces[3])]


def stack_kernel(b0, b1, b2, b3, out_ref):
    rows, cols = b0.shape[0], out_ref.shape[1]
    for k, b in enumerate((b0, b1, b2, b3)):
        out_ref[k * rows : (k + 1) * rows, :] = b[:, :cols]


def stack(blocks, cols):
    rows = blocks[0].shape[0]
    return pl.pallas_call(
        stack_kernel,
        in_specs=[whole()] * 4,
        out_specs=whole(),
        out_shape=sds((4 * rows, cols)),
        compiler_params=vm(),
        cost_estimate=cost(1e5, 4 * rows * cols * 4),
        name="stack",
    )(*blocks)


def normed_rows(values, gain):
    mean = jnp.mean(values, axis=-1, keepdims=True)
    centred = values - mean
    variance = jnp.mean(centred * centred, axis=-1, keepdims=True)
    return (centred * lax.rsqrt(variance + 1e-05) * gain).astype(BF)


def grid_kv_kernel(starts, first, x_ref, *refs):
    if first:
        gain_ref, w_ref, *refs = refs
    else:
        w_both, *refs = refs
    outs, refs = refs[: len(starts)], refs[len(starts) :]
    if first:
        w_both, *refs = refs
    rows, sems = refs
    blocks = outs[0].shape[0] // KV_BLOCK
    copies = [
        pltpu.make_async_copy(
            x_ref.at[pl.ds(start + i * KV_BLOCK, KV_BLOCK)],
            rows.at[part * blocks + i],
            sems.at[part * blocks + i],
        )
        for part, start in enumerate(starts)
        for i in range(blocks)
    ]
    for copy in copies:
        copy.start()
    if first:
        for i in range(2):
            turned = jnp.transpose(w_ref[i].astype(F32) * gain_ref[0:1, :]).astype(BF)
            w_both[:, i * HEAD_DIM : (i + 1) * HEAD_DIM] = turned
    for part, out in enumerate(outs):
        for i in range(blocks):
            copies[part * blocks + i].wait()

            x = rows[part * blocks + i].astype(F32)
            x = x - jnp.mean(x, axis=-1, keepdims=True)
            variance = jnp.mean(x * x, axis=-1, keepdims=True)
            scale = lax.rsqrt(variance + 1e-05)
            x = x.astype(BF)
            for line in range(0, KV_BLOCK, 128):
                kv = jnp.dot(x[line : line + 128], w_both[...], preferred_element_type=F32)
                at = i * KV_BLOCK + line
                out[at : at + 128, :] = (kv * scale[line : line + 128]).astype(BF)


def grid_kv(grid_latent, starts, count, gains=None, w=None, w_both=None):
    d = grid_latent.shape[1]
    blocks = len(starts) * count // KV_BLOCK
    first = w_both is None
    weight_shape = sds((d, 128))
    out_shape = [sds((count, 128))] * len(starts) + ([weight_shape] if first else [])
    return pl.pallas_call(
        functools.partial(grid_kv_kernel, starts, first),
        in_specs=[hbm()] + [whole()] * (2 if first else 1),
        out_specs=[whole()] * len(out_shape),
        out_shape=out_shape,
        scratch_shapes=[
            pltpu.VMEM((blocks, KV_BLOCK, d), BF),
            pltpu.SemaphoreType.DMA((blocks,)),
        ],
        compiler_params=vm(56),
        cost_estimate=cost(2 * blocks * KV_BLOCK * d * 128, blocks * KV_BLOCK * d * 2),
        name="grid_kv",
    )(grid_latent, *((gains, w) if first else (w_both,)))


COUNT_STEP = 64
TILES = KEYS // 128


def edge_count_kernel(place_ref, src_ref, degree_ref, out_ref, by_node, high_key, low_key):
    step = pl.program_id(0)

    @pl.when(step == 0)
    def _():
        shape = src_ref.shape
        local = src_ref[...] - (place_ref[0] * place_ref[2] - EDGE)
        used = lax.broadcasted_iota(jnp.int32, shape, 0) < degree_ref[...]
        by_node[...] = jnp.transpose(jnp.where(used, local, -1))
        for t in range(8):
            local_rows = by_node[pl.ds(t, NODES_HERE // 8, stride=8), :]
            cols = slice(t * K_MAX, (t + 1) * K_MAX)
            high_key[:, cols] = jnp.where(local_rows < 0, -1, (local_rows >> 7) * 8 + t)
            low_key[:, cols] = local_rows & 127

    row_high = lax.broadcasted_iota(jnp.int32, (TILES * 8, 256), 0)
    row_low = lax.broadcasted_iota(jnp.int32, (128, 256), 0)

    def counts(group):
        left = jnp.where(row_high == high_key[pl.ds(group, 1), :], 1.0, 0.0).astype(BF)
        right = jnp.where(row_low == low_key[pl.ds(group, 1), :], 1.0, 0.0).astype(BF)
        return lax.dot_general(left, right, NT, preferred_element_type=F32)

    def pair(i, carry):
        group = step * (COUNT_STEP // 8) + 2 * i
        first = counts(group)
        second = counts(group + 1)
        rows = pl.ds(pl.multiple_of(i * 16, 16), 16)
        for t in range(TILES):
            both = jnp.concatenate([first[t * 8 : t * 8 + 8], second[t * 8 : t * 8 + 8]], axis=0)
            out_ref[rows, t * 128 : (t + 1) * 128] = both.astype(BF)
        return carry

    lax.fori_loop(0, COUNT_STEP // 16, pair, 0, unroll=COUNT_STEP // 16)


def edge_counts(place, sources, degrees):
    return pl.pallas_call(
        edge_count_kernel,
        grid=(NODES_HERE // COUNT_STEP,),
        in_specs=[
            smem(),
            pl.BlockSpec(sources.shape, lambda i: (0, 0)),
            pl.BlockSpec(degrees.shape, lambda i: (0, 0)),
        ],
        out_specs=pl.BlockSpec((COUNT_STEP, KEYS), lambda i: (i, 0)),
        out_shape=sds((NODES_HERE, KEYS)),
        scratch_shapes=[
            pltpu.VMEM((NODES_HERE, K_MAX), jnp.int32),
            pltpu.VMEM((NODES_HERE // 8, 8 * K_MAX), jnp.int32),
            pltpu.VMEM((NODES_HERE // 8, 8 * K_MAX), jnp.int32),
        ],
        compiler_params=vm(),
        cost_estimate=cost(4e9, 10e6),
        name="edge_counts",
    )(place, sources, degrees)


def block_places(head):
    z, core = head // 2, head % 2
    side = 2 * core - 1
    places = []
    for g in range(4):
        from_z = z if g < 2 else z + side
        from_core = core if g % 2 == 0 else 1 - core
        step = 2 - 4 * from_core
        places += [2 * ((from_z + step * k + 16) & 7) + from_core for k in range(4)]
    return places


def row_positions(places):
    lane = lax.broadcasted_iota(jnp.int32, (1, NODES_HERE), 1)
    pos = jnp.zeros((1, NODES_HERE), jnp.int32)
    for i, place in enumerate(places):
        pos = jnp.where(lane // BLOCK == i, place * BLOCK + lane % BLOCK, pos)
    return pos


def node_query_kernel(place_ref, r0, r1, r2, r3, gain_ref, w_ref, order_ref, q_ref, mine_ref, order_col, rows):
    head = place_ref[1]
    places = block_places(head)
    for g, r in enumerate((r0, r1, r2, r3)):
        rows[g * GROUP : (g + 1) * GROUP, :] = r[...]
        normed = normed_rows(r[...].astype(F32), gain_ref[1:2, :])
        q = lax.dot_general(normed, w_ref[...], NT, preferred_element_type=F32).astype(BF)
        for k in range(4):
            start = pl.multiple_of(places[g * 4 + k] * BLOCK, BLOCK)
            q_ref[pl.ds(start, BLOCK), :] = q[k * BLOCK : (k + 1) * BLOCK, :]
    local = order_ref[...] - place_ref[0] * NODES_HERE
    order_col[...] = jnp.transpose(jnp.broadcast_to(local, (8, NODES_HERE)))
    wanted = order_col[pl.ds(pl.multiple_of(head * BLOCK, BLOCK), BLOCK), 0:1]
    pick = jnp.where(row_positions(places) == wanted, 1.0, 0.0).astype(BF)
    mine_ref[...] = jnp.dot(pick, rows[...], preferred_element_type=F32).astype(BF)


def node_queries(place, pieces, gains, wq_t, order):
    d = wq_t.shape[1]
    return pl.pallas_call(
        node_query_kernel,
        in_specs=[smem()] + [whole()] * 7,
        out_specs=[whole()] * 2,
        out_shape=[sds((NODES_HERE, HEAD_DIM)), sds((BLOCK, d))],
        scratch_shapes=[pltpu.VMEM((NODES_HERE, 8), jnp.int32), pltpu.VMEM((NODES_HERE, d), BF)],
        compiler_params=vm(),
        cost_estimate=cost(1e8, 2e6),
        name="node_queries",
    )(place, *pieces, gains, wq_t, order)


T_STEP = 256
CHUNK = 512


def edge_attention_kernel(
    place_ref, q_all, kv0, kv1, kv2, kv3, kv4, count_ref, order_ref,
    o0, o1, o2, o3, scores, heads, pick, order_col,
):
    step = pl.program_id(0)
    q = q_all[pl.ds(pl.multiple_of(step * T_STEP, T_STEP), T_STEP), :] * SCALE
    chunks = []
    for kv in (kv0, kv1, kv2, kv3, kv4):
        for start in range(0, kv.shape[0], CHUNK):
            chunks.append((kv, start))
    top = None
    for i, (kv, start) in enumerate(chunks):
        keys = kv[start : start + CHUNK, :][:, :HEAD_DIM]
        s = lax.dot_general(q, keys, NT, preferred_element_type=F32)
        cols = slice(i * CHUNK, (i + 1) * CHUNK)
        s = jnp.where(count_ref[:, cols].astype(F32) > 0.0, s, -jnp.inf)
        scores[:, cols] = s
        part = jnp.maximum(
            jnp.maximum(s[:, 0:128], s[:, 128:256]), jnp.maximum(s[:, 256:384], s[:, 384:512])
        )
        top = part if top is None else jnp.maximum(top, part)
    top = jnp.max(top, axis=-1, keepdims=True)
    total = jnp.zeros((T_STEP, 128), F32)
    out = jnp.zeros((T_STEP, 128), F32)
    for i, (kv, start) in enumerate(chunks):
        cols = slice(i * CHUNK, (i + 1) * CHUNK)
        e = jnp.exp(scores[:, cols] - top) * count_ref[:, cols].astype(F32)
        total += (e[:, 0:128] + e[:, 128:256]) + (e[:, 256:384] + e[:, 384:512])
        out += jnp.dot(e.astype(BF), kv[start : start + CHUNK, :], preferred_element_type=F32)
    total = jnp.sum(total, axis=-1, keepdims=True)
    rows = pl.ds(pl.multiple_of(step * T_STEP, T_STEP), T_STEP)
    heads[rows, :] = (out / total).astype(BF)

    @pl.when(step == pl.num_programs(0) - 1)
    def _():
        local = order_ref[...] - place_ref[0] * NODES_HERE
        order_col[...] = jnp.transpose(jnp.broadcast_to(local, (8, NODES_HERE)))
        places = block_places(place_ref[1])
        node = lax.broadcasted_iota(jnp.int32, (BLOCK, NODES_HERE), 1)
        for g, o in enumerate((o0, o1, o2, o3)):
            for k in range(4):
                start = pl.multiple_of(places[g * 4 + k] * BLOCK, BLOCK)
                wanted = order_col[pl.ds(start, BLOCK), 0:1]
                pick[k * BLOCK : (k + 1) * BLOCK, :] = jnp.where(node == wanted, 1.0, 0.0).astype(BF)
            taken = jnp.dot(pick[...], heads[...], preferred_element_type=F32)
            o[...] = taken[:, HEAD_DIM:].astype(BF)


def edge_attention(place, queries, kv_parts, counts, order):
    def full(x):
        return pl.BlockSpec(x.shape, lambda i: (0,) * x.ndim)

    return pl.pallas_call(
        edge_attention_kernel,
        grid=(NODES_HERE // T_STEP,),
        in_specs=[smem(), full(queries)]
        + [full(kv) for kv in kv_parts]
        + [pl.BlockSpec((T_STEP, KEYS), lambda i: (i, 0)), full(order)],
        out_specs=[pl.BlockSpec((GROUP, HEAD_DIM), lambda i: (0, 0))] * 4,
        out_shape=[sds((GROUP, HEAD_DIM))] * 4,
        scratch_shapes=[
            pltpu.VMEM((T_STEP, KEYS), F32),
            pltpu.VMEM((NODES_HERE, 128), BF),
            pltpu.VMEM((GROUP, NODES_HERE), BF),
            pltpu.VMEM((NODES_HERE, 8), jnp.int32),
        ],
        compiler_params=vm(40),
        cost_estimate=cost(2e9, 12e6),
        name="edge_attention",
    )(place, queries, *kv_parts, counts, order)


def head_sum_kernel(h0, h1, h2, h3, w0, w1, w2, w3, p0, p1, p2, p3):
    heads = jnp.concatenate([h0[...], h1[...], h2[...], h3[...]], axis=1)
    rows = jnp.concatenate([w0[...], w1[...], w2[...], w3[...]], axis=0)
    total = jnp.dot(heads, rows, preferred_element_type=F32).astype(BF)
    for k, p in enumerate((p0, p1, p2, p3)):
        p[...] = total[k * BLOCK : (k + 1) * BLOCK]


def head_sum(heads, shards, row_block):
    d = shards[0].shape[1]
    full = pl.BlockSpec((GROUP, HEAD_DIM), lambda i: (0, 0))
    return pl.pallas_call(
        head_sum_kernel,
        grid=(1,),
        in_specs=[full] * 4 + [pl.BlockSpec((HEAD_DIM, d), lambda i: (row_block, 0))] * 4,
        out_specs=[pl.BlockSpec((BLOCK, d), lambda i: (0, 0))] * 4,
        out_shape=[sds((BLOCK, d))] * 4,
        compiler_params=vm(),
        cost_estimate=cost(7e7, 1e6),
        name="head_sum",
    )(*heads, *shards)


def close_sum_kernel(gain_row, r_ref, p0, p1, p2, p3, gain_ref, stream_ref, normed_ref):
    total = (p0[...].astype(F32) + p1[...].astype(F32)) + (p2[...].astype(F32) + p3[...].astype(F32))
    stream = (r_ref[...].astype(F32) + total).astype(BF)
    stream_ref[...] = stream
    normed_ref[...] = normed_rows(stream.astype(F32), gain_ref[gain_row : gain_row + 1, :])


def close_sum(residual, parts, gains, gain_row):
    shape = residual.shape
    return pl.pallas_call(
        functools.partial(close_sum_kernel, gain_row),
        in_specs=[whole()] * 6,
        out_specs=[whole()] * 2,
        out_shape=[sds(shape), sds(shape)],
        compiler_params=vm(),
        cost_estimate=cost(1e6, 4e5),
        name="close_sum",
    )(residual, *parts, gains)


def final_sum_kernel(r_ref, p0, p1, stream_ref):
    total = p0[...].astype(F32) + p1[...].astype(F32)
    stream_ref[...] = (r_ref[...].astype(F32) + total).astype(BF)


def final_sum(residual, parts):
    return pl.pallas_call(
        final_sum_kernel,
        in_specs=[whole()] * 3,
        out_specs=whole(),
        out_shape=sds(residual.shape),
        compiler_params=vm(),
        cost_estimate=cost(1e6, 4e5),
        name="final_sum",
    )(residual, *parts)


def qkv_kernel(b0, b1, b2, b3, w0, w1, w2, w3, p0, p1, p2, p3):
    rows = jnp.concatenate([b0[...], b1[...], b2[...], b3[...]], axis=0)
    for w, out in ((w0, p0), (w1, p1), (w2, p2), (w3, p3)):
        all_cols = lax.dot_general(rows, w[...], NT, preferred_element_type=F32).astype(BF)
        out[:, :128] = all_cols[:, HEAD_DIM:]
        out[:, 128:] = all_cols[:, :HEAD_DIM]


def qkv(blocks, shards, layer):
    d = blocks[0].shape[1]
    return pl.pallas_call(
        qkv_kernel,
        grid=(1,),
        in_specs=[pl.BlockSpec((BLOCK, d), lambda i: (0, 0))] * 4
        + [pl.BlockSpec((3 * HEAD_DIM, d), lambda i: (layer, 0))] * 4,
        out_specs=[pl.BlockSpec((GROUP, 3 * HEAD_DIM), lambda i: (0, 0))] * 4,
        out_shape=[sds((GROUP, 3 * HEAD_DIM))] * 4,
        compiler_params=vm(),
        cost_estimate=cost(3e8, 2.5e6),
        name="qkv",
    )(*blocks, *shards)


def window_kernel(place_ref, a0, a1, a2, a3, kv_ref, low_ref, high_ref, out_ref):
    kv = kv_ref[...]
    low = low_ref[...]
    high = high_ref[...]
    has_low = place_ref[0] > 0
    has_high = place_ref[0] < place_ref[3] - 1
    places = block_places(place_ref[1])
    col = row_positions(places)
    line = lax.broadcasted_iota(jnp.int32, (GROUP, 1), 0)
    for g, a in enumerate((a0, a1, a2, a3)):
        q = a[:, 128:] * SCALE
        row = jnp.zeros((GROUP, 1), jnp.int32)
        for k in range(4):
            row = jnp.where(line // BLOCK == k, places[g * 4 + k] * BLOCK + line % BLOCK, row)
        s_own = lax.dot_general(q, kv[:, :HEAD_DIM], NT, preferred_element_type=F32)
        s_low = lax.dot_general(q, low[:, :HEAD_DIM], NT, preferred_element_type=F32)
        s_high = lax.dot_general(q, high[:, :HEAD_DIM], NT, preferred_element_type=F32)
        after = col >= row
        in_low = jnp.logical_and(after, has_low)
        in_high = jnp.logical_and(jnp.logical_not(after), has_high)
        s_far = jnp.where(in_low, s_low, jnp.where(in_high, s_high, -jnp.inf))
        top = jnp.maximum(
            jnp.max(s_own, axis=-1, keepdims=True), jnp.max(s_far, axis=-1, keepdims=True)
        )
        e_own = jnp.exp(s_own - top)
        e_far = jnp.exp(s_far - top)
        total = jnp.sum(e_own + e_far, axis=-1, keepdims=True)
        e_low = jnp.where(in_low, e_far, 0.0).astype(BF)
        e_high = jnp.where(in_high, e_far, 0.0).astype(BF)
        out = jnp.dot(e_own.astype(BF), kv, preferred_element_type=F32)
        out += jnp.dot(e_low, low, preferred_element_type=F32)
        out += jnp.dot(e_high, high, preferred_element_type=F32)
        heads = (out / total)[:, HEAD_DIM:].astype(BF)
        for k in range(4):
            out_ref[places[g * 4 + k]] = heads[k * BLOCK : (k + 1) * BLOCK]


def window_attention(place, pieces, kv, low, high):
    return pl.pallas_call(
        window_kernel,
        in_specs=[smem()] + [whole()] * 7,
        out_specs=whole(),
        out_shape=sds((NODES_HERE // BLOCK, BLOCK, HEAD_DIM)),
        compiler_params=vm(),
        cost_estimate=cost(4e8, 1e6),
        name="window_attention",
    )(place, *pieces, kv, low, high)


def one_layer_kernel(w_ref, out_ref):
    out_ref[...] = w_ref[:, 0].reshape(out_ref.shape)


def one_layer(wo_all, layer):
    count, _, rows, d = wo_all.shape
    return pl.pallas_call(
        one_layer_kernel,
        grid=(4,),
        in_specs=[pl.BlockSpec((count // 4, 1, rows, d), lambda i: (i, layer, 0, 0))],
        out_specs=pl.BlockSpec((count // 4 * rows, d), lambda i: (i, 0)),
        out_shape=sds((count * rows, d)),
        compiler_params=vm(),
        cost_estimate=cost(1e5, 2 * count * rows * d * 2),
        name="one_layer",
    )(wo_all)


def heads_to_stream_kernel(gain_row, heads_ref, wo_ref, r_ref, gain_ref, stream_ref, normed_ref):
    count = heads_ref.shape[0]
    heads = jnp.concatenate([heads_ref[h] for h in range(count)], axis=1)
    total = jnp.dot(heads, wo_ref[...], preferred_element_type=F32)
    stream = (r_ref[...].astype(F32) + total).astype(BF)
    stream_ref[...] = stream
    normed_ref[...] = normed_rows(stream.astype(F32), gain_ref[gain_row : gain_row + 1, :])


def heads_to_stream(heads, wo, residual, gains, gain_row):
    return pl.pallas_call(
        functools.partial(heads_to_stream_kernel, gain_row),
        in_specs=[whole()] * 4,
        out_specs=[whole()] * 2,
        out_shape=[sds(residual.shape)] * 2,
        compiler_params=vm(),
        cost_estimate=cost(7e7, 2.5e6),
        name="heads_to_stream",
    )(heads, wo, residual, gains)


def pack_kernel(layer, up_ref, down_ref, out_ref, sems):
    rows = down_ref.shape[1]
    copies = [
        pltpu.make_async_copy(
            up_ref.at[layer, q * rows : (q + 1) * rows],
            out_ref.at[:rows, q * rows : (q + 1) * rows],
            sems.at[q],
        )
        for q in range(4)
    ]
    copies.append(pltpu.make_async_copy(down_ref.at[layer], out_ref.at[rows:, :], sems.at[4]))
    for copy in copies:
        copy.start()
    for copy in copies:
        copy.wait()


def pack(w_up, w_down, layer):
    d, hidden = w_up.shape[1:]
    return pl.pallas_call(
        functools.partial(pack_kernel, layer),
        in_specs=[hbm(), hbm()],
        out_specs=whole(),
        out_shape=sds((2 * hidden, d)),
        scratch_shapes=[pltpu.SemaphoreType.DMA((5,))],
        compiler_params=vm(),
        cost_estimate=cost(1e5, 2e6),
        name="pack",
    )(w_up, w_down)


def feed_forward_kernel(b0, b1, b2, b3, w0, w1, w2, w3, p0, p1, p2, p3):
    rows = jnp.concatenate([b0[...], b1[...], b2[...], b3[...]], axis=0)
    total = None
    for w in (w0, w1, w2, w3):
        hidden = w.shape[0] // 2
        up = None
        for q in range(4):
            cols = slice(q * hidden, (q + 1) * hidden)
            part = jnp.dot(rows[:, cols], w[:hidden, cols], preferred_element_type=F32)
            up = part if up is None else up + part
        part = jnp.dot(jax.nn.gelu(up).astype(BF), w[hidden:, :], preferred_element_type=F32)
        total = part if total is None else total + part
    total = total.astype(BF)
    for k, p in enumerate((p0, p1, p2, p3)):
        p[...] = total[k * BLOCK : (k + 1) * BLOCK]


def feed_forward(blocks, shards):
    d = blocks[0].shape[1]
    return pl.pallas_call(
        feed_forward_kernel,
        in_specs=[whole()] * 8,
        out_specs=[whole()] * 4,
        out_shape=[sds((BLOCK, d))] * 4,
        compiler_params=vm(),
        cost_estimate=cost(5e8, 5e6),
        name="feed_forward",
    )(*blocks, *shards)


def pair_feed_forward_kernel(mine_ref, other_ref, w_ref, own_ref, send_ref, total, held, sems):
    count = held.shape[0]
    hidden = held.shape[1] * 16

    def copy(i):
        return pltpu.make_async_copy(w_ref.at[:, i], held.at[i], sems.at[i])

    for i in range(count):
        copy(i).start()
    rows = jnp.concatenate([mine_ref[...], other_ref[...]], axis=0)
    total[...] = jnp.zeros_like(total)

    def shard(i, carry):
        copy(i).wait()
        up = None
        for q in range(4):
            cols = slice(q * 256, (q + 1) * 256)
            weight = held[i, :, :16, cols].reshape(256, hidden)
            part = jnp.dot(rows[:, cols], weight, preferred_element_type=F32)
            up = part if up is None else up + part
        weight = held[i, :, 16:, :].reshape(hidden, rows.shape[1])
        total[...] += jnp.dot(jax.nn.gelu(up).astype(BF), weight, preferred_element_type=F32)
        return carry

    lax.fori_loop(0, count, shard, 0)
    own_ref[...] = total[:BLOCK, :].astype(BF)
    send_ref[...] = total[BLOCK:, :].astype(BF)


def pair_feed_forward(mine, other, weights):
    d = mine.shape[1]
    bands, count = weights.shape[:2]
    return pl.pallas_call(
        pair_feed_forward_kernel,
        in_specs=[whole(), whole(), hbm()],
        out_specs=[whole()] * 2,
        out_shape=[sds((BLOCK, d))] * 2,
        scratch_shapes=[
            pltpu.VMEM((2 * BLOCK, d), F32),
            pltpu.VMEM((count, bands, 32, d), BF),
            pltpu.SemaphoreType.DMA((count,)),
        ],
        compiler_params=vm(50),
        cost_estimate=cost(5e8, 9e6),
        name="pair_feed_forward",
    )(mine, other, weights)


def sixteenth_kernel(layer, place_ref, up_ref, down_ref, out_ref, sems):
    band = place_ref[0]
    copies = [
        pltpu.make_async_copy(
            up_ref.at[layer, q, band], out_ref.at[:16, q * 256 : (q + 1) * 256], sems.at[q]
        )
        for q in range(4)
    ]
    rows = pl.ds(pl.multiple_of(band * 16, 16), 16)
    copies.append(pltpu.make_async_copy(down_ref.at[layer, rows], out_ref.at[16:, :], sems.at[4]))
    for copy in copies:
        copy.start()
    for copy in copies:
        copy.wait()


def sixteenth(place, w_up, w_down, layer):
    d, hidden = w_up.shape[1:]
    return pl.pallas_call(
        functools.partial(sixteenth_kernel, layer),
        in_specs=[smem(), hbm(), hbm()],
        out_specs=whole(),
        out_shape=sds((32, d)),
        scratch_shapes=[pltpu.SemaphoreType.DMA((5,))],
        compiler_params=vm(63),
        cost_estimate=cost(1e5, 2e5),
        name="sixteenth",
    )(place, w_up.reshape(-1, 4, 16, 16, hidden), w_down)


def one_parity_kernel(place_ref, all_ref, out_ref, sems):
    core = place_ref[1] % 2
    copies = [
        pltpu.make_async_copy(all_ref.at[2 * i + core], out_ref.at[i], sems.at[i])
        for i in range(out_ref.shape[0])
    ]
    for copy in copies:
        copy.start()
    for copy in copies:
        copy.wait()


def one_parity(place, over_head):
    count, rows, d = over_head.shape
    return pl.pallas_call(
        one_parity_kernel,
        in_specs=[smem(), pl.BlockSpec(memory_space=pl.ANY)],
        out_specs=pl.BlockSpec(memory_space=pl.ANY),
        out_shape=sds((count // 2, rows, d)),
        scratch_shapes=[pltpu.SemaphoreType.DMA((count // 2,))],
        compiler_params=vm(),
        cost_estimate=cost(1e5, count * rows * d * 2),
        name="one_parity",
    )(place, over_head)


def shards(
    grid_latent,
    node_latent,
    src_index,
    in_degree,
    node_order,
    norm_gains,
    enc_wq,
    enc_wkv,
    enc_wo,
    proc_wqkv,
    proc_wo,
    w_up,
    w_down,
):
    d = grid_latent.shape[1]
    band = lax.axis_index("band")
    head = lax.axis_index("head")
    place = jnp.stack([band, head, grid_latent.shape[0], lax.axis_size("band")]).astype(jnp.int32)
    order = node_order[None, :]

    barrier = lax.optimization_barrier
    wo_all = lax.all_gather(proc_wo, "head")
    qkv_t = jnp.swapaxes(proc_wqkv, 2, 3).reshape(-1, d)

    wkv_t = jnp.swapaxes(enc_wkv, 1, 2)
    grid_rows = grid_latent.shape[0]
    edge_low, edge_high, w_both = grid_kv(
        grid_latent, (0, grid_rows - EDGE), EDGE, gains=norm_gains, w=wkv_t
    )
    node_latent, w_up, w_down, grid_latent, enc_wo, edge_low, edge_high = barrier(
        (node_latent, w_up, w_down, grid_latent, enc_wo, edge_low, edge_high)
    )
    node_blocks = gather_group(node_latent)
    from_low = up_band(edge_high)
    from_high = down_band(edge_low)
    middle = grid_kv(grid_latent, (EDGE,), grid_rows - 2 * EDGE, w_both=w_both)[0]
    late_part = sixteenth(place, w_up, w_down, 1)
    tall = jnp.concatenate([qkv_t, enc_wo], axis=0)
    node_blocks, middle, late_part, tall = barrier((node_blocks, middle, late_part, tall))
    node_group = stack(node_blocks, d)
    node_pieces = exchange([node_group] * 4)
    sources, _ = barrier((src_index.T, node_group))
    counts = edge_counts(place, sources, in_degree[None, :])
    node_pieces, counts, from_low, from_high, tall = barrier((node_pieces, counts, from_low, from_high, tall))

    tall_third, tall_other = outward(tall), swap(tall)
    queries, residual = node_queries(place, node_pieces, norm_gains, enc_wq.T, order)
    kv_parts = [from_low, edge_low, middle, edge_high, from_high]
    enc_heads = edge_attention(place, queries, kv_parts, counts, order)
    enc_heads, tall_third, tall_other, late_part, wo_all = barrier(
        (enc_heads, tall_third, tall_other, late_part, wo_all)
    )
    late_weights = lax.all_gather(late_part, "head")
    tall_shards = [tall, tall_other, tall_third, swap(tall_third)]
    sums = head_sum(give_back(enc_heads), tall_shards, qkv_t.shape[0] // HEAD_DIM)
    stream, normed = close_sum(residual, scatter_group(sums), norm_gains, 2)

    for layer in range(LAYERS):
        blocks = gather_group(normed)
        if layer == 0:
            w_up, w_down, _ = barrier((w_up, w_down, normed))
            blocks, first = barrier((blocks, pack(w_up, w_down, 0)))
        pieces = exchange(qkv(blocks, tall_shards, layer))
        kv = stack(pieces, 2 * HEAD_DIM)
        low = up_band(kv)
        high = down_band(kv)
        wo_all, _ = barrier((wo_all, kv))
        wo = one_layer(wo_all, layer)
        low, high, wo = barrier((low, high, wo))
        if layer == 0:
            first, late_weights, _ = barrier((first, late_weights, kv))
            first_third, first_other = outward(first), swap(first)
            late_weights = one_parity(place, late_weights)
            low, high, late_weights, first_third, first_other = barrier(
                (low, high, late_weights, first_third, first_other)
            )
            late_weights = lax.all_gather(late_weights, "band")
        win_heads = window_attention(place, pieces, kv, low, high)
        if layer == 0:
            first_shards = [first, first_other, first_third, swap(first_third)]
        win_heads = lax.all_to_all(win_heads, "head", 0, 0)
        stream, normed = heads_to_stream(win_heads, wo, stream, norm_gains, 3 + 2 * layer)
        if layer == 0:
            parts = scatter_group(feed_forward(gather_group(normed), first_shards))
            stream, normed = close_sum(stream, parts, norm_gains, 4 + 2 * layer)
        else:
            own, other = pair_feed_forward(normed, swap(normed), late_weights)
            stream = final_sum(stream, [own, swap(other)])
    return stream


def solution(mesh):
    in_specs = (
        P("band", None),
        P(("band", "head"), None),
        P("band", None),
        P("band"),
        P("band"),
        P(),
        P(None, "head"),
        P(None, None, "head"),
        P("head", None),
        P(None, None, None, "head"),
        P(None, "head", None),
        P(None, None, "head"),
        P(None, "head", None),
    )
    out_specs = P(("band", "head"), None)
    return jax.shard_map(shards, mesh=mesh, in_specs=in_specs, out_specs=out_specs, check_vma=False)
```

```python
import functools
import math

import jax
import jax.numpy as jnp
from jax import lax
from jax.experimental import pallas as pl
from jax.experimental.pallas import tpu as pltpu
from jax.sharding import PartitionSpec as P

HEAD_DIM = 64
K_MAX = 32
HALF_WIN = 512
LAYERS = 2
EDGE = 1536
KV_BLOCK = 512
BLOCK = 32
GROUP = 128
NODES_HERE = 512
KEYS = 7168
SCALE = 1.0 / math.sqrt(HEAD_DIM)
BF = jnp.bfloat16
F32 = jnp.float32
NT = (((1,), (1,)), ((), ()))


def vm(limit_mib=20):
    return pltpu.CompilerParams(vmem_limit_bytes=limit_mib * 1024 * 1024)


def cost(flops, nbytes):
    return pl.CostEstimate(flops=int(flops), bytes_accessed=int(nbytes), transcendentals=0)


def whole():
    return pl.BlockSpec(memory_space=pltpu.VMEM)


def hbm():
    return pl.BlockSpec(memory_space=pltpu.HBM)


def smem():
    return pl.BlockSpec(memory_space=pltpu.SMEM)


def sds(shape, dtype=BF):
    return jax.ShapeDtypeStruct(shape, dtype)


def swap(x):
    return lax.ppermute(x, "head", [(i, i ^ 1) for i in range(16)])


def shift_z(x, k):
    steps = (k, -k)
    return lax.ppermute(x, "head", [(i, ((i // 2 + steps[i % 2]) % 8) * 2 + i % 2) for i in range(16)])


def outward_pairs():
    return [(2 * z + c, 2 * ((z + (1 if c else -1)) % 8) + c) for z in range(8) for c in range(2)]


def outward(x):
    return lax.ppermute(x, "head", outward_pairs())


def inward(x):
    return lax.ppermute(x, "head", [(t, s) for s, t in outward_pairs()])


def crossed(x):
    pairs = [(2 * z, 2 * ((z - 1) % 8) + 1) for z in range(8)]
    return lax.ppermute(x, "head", pairs + [(t, s) for s, t in pairs])


def up_band(x):
    return lax.ppermute(x, "band", [(i, i + 1) for i in range(15)])


def down_band(x):
    return lax.ppermute(x, "band", [(i + 1, i) for i in range(15)])


def gather_group(x):
    behind = shift_z(x, 2)
    ahead = shift_z(x, -2)
    far = shift_z(x, 4)
    return [x, ahead, far, behind]


def scatter_group(parts):
    return [parts[0], shift_z(parts[1], 2), shift_z(parts[2], 4), shift_z(parts[3], -2)]


def four_shards(x):
    third = outward(x)
    return [x, swap(x), third, swap(third)]


def exchange(pieces):
    return [pieces[0], swap(pieces[1]), inward(pieces[2]), crossed(pieces[3])]


def give_back(pieces):
    return [pieces[0], swap(pieces[1]), outward(pieces[2]), crossed(pieces[3])]


def stack_kernel(b0, b1, b2, b3, out_ref):
    rows, cols = b0.shape[0], out_ref.shape[1]
    for k, b in enumerate((b0, b1, b2, b3)):
        out_ref[k * rows : (k + 1) * rows, :] = b[:, :cols]


def stack(blocks, cols):
    rows = blocks[0].shape[0]
    return pl.pallas_call(
        stack_kernel,
        in_specs=[whole()] * 4,
        out_specs=whole(),
        out_shape=sds((4 * rows, cols)),
        compiler_params=vm(),
        cost_estimate=cost(1e5, 4 * rows * cols * 4),
        name="stack",
    )(*blocks)


def normed_rows(values, gain):
    mean = jnp.mean(values, axis=-1, keepdims=True)
    centred = values - mean
    variance = jnp.mean(centred * centred, axis=-1, keepdims=True)
    return (centred * lax.rsqrt(variance + 1e-05) * gain).astype(BF)


def grid_kv_kernel(starts, first, x_ref, *refs):
    if first:
        gain_ref, w_ref, *refs = refs
    else:
        w_both, *refs = refs
    outs, refs = refs[: len(starts)], refs[len(starts) :]
    if first:
        w_both, *refs = refs
    rows, sems = refs
    blocks = outs[0].shape[0] // KV_BLOCK
    copies = [
        pltpu.make_async_copy(
            x_ref.at[pl.ds(start + i * KV_BLOCK, KV_BLOCK)],
            rows.at[part * blocks + i],
            sems.at[part * blocks + i],
        )
        for part, start in enumerate(starts)
        for i in range(blocks)
    ]
    for copy in copies:
        copy.start()
    if first:
        for i in range(2):
            turned = jnp.transpose(w_ref[i].astype(F32) * gain_ref[0:1, :]).astype(BF)
            w_both[:, i * HEAD_DIM : (i + 1) * HEAD_DIM] = turned
    for part, out in enumerate(outs):
        for i in range(blocks):
            copies[part * blocks + i].wait()

            x = rows[part * blocks + i].astype(F32)
            x = x - jnp.mean(x, axis=-1, keepdims=True)
            variance = jnp.mean(x * x, axis=-1, keepdims=True)
            scale = lax.rsqrt(variance + 1e-05)
            x = x.astype(BF)
            for line in range(0, KV_BLOCK, 128):
                kv = jnp.dot(x[line : line + 128], w_both[...], preferred_element_type=F32)
                at = i * KV_BLOCK + line
                out[at : at + 128, :] = (kv * scale[line : line + 128]).astype(BF)


def grid_kv(grid_latent, starts, count, gains=None, w=None, w_both=None):
    d = grid_latent.shape[1]
    blocks = len(starts) * count // KV_BLOCK
    first = w_both is None
    weight_shape = sds((d, 128))
    out_shape = [sds((count, 128))] * len(starts) + ([weight_shape] if first else [])
    return pl.pallas_call(
        functools.partial(grid_kv_kernel, starts, first),
        in_specs=[hbm()] + [whole()] * (2 if first else 1),
        out_specs=[whole()] * len(out_shape),
        out_shape=out_shape,
        scratch_shapes=[
            pltpu.VMEM((blocks, KV_BLOCK, d), BF),
            pltpu.SemaphoreType.DMA((blocks,)),
        ],
        compiler_params=vm(56),
        cost_estimate=cost(2 * blocks * KV_BLOCK * d * 128, blocks * KV_BLOCK * d * 2),
        name="grid_kv",
    )(grid_latent, *((gains, w) if first else (w_both,)))


COUNT_STEP = 64
TILES = KEYS // 128


def edge_count_kernel(place_ref, src_ref, degree_ref, out_ref, by_node, high_key, low_key):
    step = pl.program_id(0)

    @pl.when(step == 0)
    def _():
        shape = src_ref.shape
        local = src_ref[...] - (place_ref[0] * place_ref[2] - EDGE)
        used = lax.broadcasted_iota(jnp.int32, shape, 0) < degree_ref[...]
        by_node[...] = jnp.transpose(jnp.where(used, local, -1))
        for t in range(8):
            local_rows = by_node[pl.ds(t, NODES_HERE // 8, stride=8), :]
            cols = slice(t * K_MAX, (t + 1) * K_MAX)
            high_key[:, cols] = jnp.where(local_rows < 0, -1, (local_rows >> 7) * 8 + t)
            low_key[:, cols] = local_rows & 127

    row_high = lax.broadcasted_iota(jnp.int32, (TILES * 8, 256), 0)
    row_low = lax.broadcasted_iota(jnp.int32, (128, 256), 0)

    def counts(group):
        left = jnp.where(row_high == high_key[pl.ds(group, 1), :], 1.0, 0.0).astype(BF)
        right = jnp.where(row_low == low_key[pl.ds(group, 1), :], 1.0, 0.0).astype(BF)
        return lax.dot_general(left, right, NT, preferred_element_type=F32)

    def pair(i, carry):
        group = step * (COUNT_STEP // 8) + 2 * i
        first = counts(group)
        second = counts(group + 1)
        rows = pl.ds(pl.multiple_of(i * 16, 16), 16)
        for t in range(TILES):
            both = jnp.concatenate([first[t * 8 : t * 8 + 8], second[t * 8 : t * 8 + 8]], axis=0)
            out_ref[rows, t * 128 : (t + 1) * 128] = both.astype(BF)
        return carry

    lax.fori_loop(0, COUNT_STEP // 16, pair, 0, unroll=COUNT_STEP // 16)


def edge_counts(place, sources, degrees):
    return pl.pallas_call(
        edge_count_kernel,
        grid=(NODES_HERE // COUNT_STEP,),
        in_specs=[
            smem(),
            pl.BlockSpec(sources.shape, lambda i: (0, 0)),
            pl.BlockSpec(degrees.shape, lambda i: (0, 0)),
        ],
        out_specs=pl.BlockSpec((COUNT_STEP, KEYS), lambda i: (i, 0)),
        out_shape=sds((NODES_HERE, KEYS)),
        scratch_shapes=[
            pltpu.VMEM((NODES_HERE, K_MAX), jnp.int32),
            pltpu.VMEM((NODES_HERE // 8, 8 * K_MAX), jnp.int32),
            pltpu.VMEM((NODES_HERE // 8, 8 * K_MAX), jnp.int32),
        ],
        compiler_params=vm(),
        cost_estimate=cost(4e9, 10e6),
        name="edge_counts",
    )(place, sources, degrees)


def block_places(head):
    z, core = head // 2, head % 2
    side = 2 * core - 1
    places = []
    for g in range(4):
        from_z = z if g < 2 else z + side
        from_core = core if g % 2 == 0 else 1 - core
        step = 2 - 4 * from_core
        places += [2 * ((from_z + step * k + 16) & 7) + from_core for k in range(4)]
    return places


def row_positions(places):
    lane = lax.broadcasted_iota(jnp.int32, (1, NODES_HERE), 1)
    pos = jnp.zeros((1, NODES_HERE), jnp.int32)
    for i, place in enumerate(places):
        pos = jnp.where(lane // BLOCK == i, place * BLOCK + lane % BLOCK, pos)
    return pos


def node_query_kernel(place_ref, r0, r1, r2, r3, gain_ref, w_ref, order_ref, q_ref, mine_ref, order_col, rows):
    head = place_ref[1]
    places = block_places(head)
    for g, r in enumerate((r0, r1, r2, r3)):
        rows[g * GROUP : (g + 1) * GROUP, :] = r[...]
        normed = normed_rows(r[...].astype(F32), gain_ref[1:2, :])
        q = lax.dot_general(normed, w_ref[...], NT, preferred_element_type=F32).astype(BF)
        for k in range(4):
            start = pl.multiple_of(places[g * 4 + k] * BLOCK, BLOCK)
            q_ref[pl.ds(start, BLOCK), :] = q[k * BLOCK : (k + 1) * BLOCK, :]
    local = order_ref[...] - place_ref[0] * NODES_HERE
    order_col[...] = jnp.transpose(jnp.broadcast_to(local, (8, NODES_HERE)))
    wanted = order_col[pl.ds(pl.multiple_of(head * BLOCK, BLOCK), BLOCK), 0:1]
    pick = jnp.where(row_positions(places) == wanted, 1.0, 0.0).astype(BF)
    mine_ref[...] = jnp.dot(pick, rows[...], preferred_element_type=F32).astype(BF)


def node_queries(place, pieces, gains, wq_t, order):
    d = wq_t.shape[1]
    return pl.pallas_call(
        node_query_kernel,
        in_specs=[smem()] + [whole()] * 7,
        out_specs=[whole()] * 2,
        out_shape=[sds((NODES_HERE, HEAD_DIM)), sds((BLOCK, d))],
        scratch_shapes=[pltpu.VMEM((NODES_HERE, 8), jnp.int32), pltpu.VMEM((NODES_HERE, d), BF)],
        compiler_params=vm(),
        cost_estimate=cost(1e8, 2e6),
        name="node_queries",
    )(place, *pieces, gains, wq_t, order)


T_STEP = 256
CHUNK = 512


def edge_attention_kernel(
    place_ref, q_all, kv0, kv1, kv2, kv3, kv4, count_ref, order_ref,
    o0, o1, o2, o3, scores, heads, pick, order_col,
):
    step = pl.program_id(0)
    q = q_all[pl.ds(pl.multiple_of(step * T_STEP, T_STEP), T_STEP), :] * SCALE
    chunks = []
    for kv in (kv0, kv1, kv2, kv3, kv4):
        for start in range(0, kv.shape[0], CHUNK):
            chunks.append((kv, start))
    top = None
    for i, (kv, start) in enumerate(chunks):
        keys = kv[start : start + CHUNK, :][:, :HEAD_DIM]
        s = lax.dot_general(q, keys, NT, preferred_element_type=F32)
        cols = slice(i * CHUNK, (i + 1) * CHUNK)
        s = jnp.where(count_ref[:, cols].astype(F32) > 0.0, s, -jnp.inf)
        scores[:, cols] = s
        part = jnp.maximum(
            jnp.maximum(s[:, 0:128], s[:, 128:256]), jnp.maximum(s[:, 256:384], s[:, 384:512])
        )
        top = part if top is None else jnp.maximum(top, part)
    top = jnp.max(top, axis=-1, keepdims=True)
    total = jnp.zeros((T_STEP, 128), F32)
    out = jnp.zeros((T_STEP, 128), F32)
    for i, (kv, start) in enumerate(chunks):
        cols = slice(i * CHUNK, (i + 1) * CHUNK)
        e = jnp.exp(scores[:, cols] - top) * count_ref[:, cols].astype(F32)
        total += (e[:, 0:128] + e[:, 128:256]) + (e[:, 256:384] + e[:, 384:512])
        out += jnp.dot(e.astype(BF), kv[start : start + CHUNK, :], preferred_element_type=F32)
    total = jnp.sum(total, axis=-1, keepdims=True)
    rows = pl.ds(pl.multiple_of(step * T_STEP, T_STEP), T_STEP)
    heads[rows, :] = (out / total).astype(BF)

    @pl.when(step == pl.num_programs(0) - 1)
    def _():
        local = order_ref[...] - place_ref[0] * NODES_HERE
        order_col[...] = jnp.transpose(jnp.broadcast_to(local, (8, NODES_HERE)))
        places = block_places(place_ref[1])
        node = lax.broadcasted_iota(jnp.int32, (BLOCK, NODES_HERE), 1)
        for g, o in enumerate((o0, o1, o2, o3)):
            for k in range(4):
                start = pl.multiple_of(places[g * 4 + k] * BLOCK, BLOCK)
                wanted = order_col[pl.ds(start, BLOCK), 0:1]
                pick[k * BLOCK : (k + 1) * BLOCK, :] = jnp.where(node == wanted, 1.0, 0.0).astype(BF)
            taken = jnp.dot(pick[...], heads[...], preferred_element_type=F32)
            o[...] = taken[:, HEAD_DIM:].astype(BF)


def edge_attention(place, queries, kv_parts, counts, order):
    def full(x):
        return pl.BlockSpec(x.shape, lambda i: (0,) * x.ndim)

    return pl.pallas_call(
        edge_attention_kernel,
        grid=(NODES_HERE // T_STEP,),
        in_specs=[smem(), full(queries)]
        + [full(kv) for kv in kv_parts]
        + [pl.BlockSpec((T_STEP, KEYS), lambda i: (i, 0)), full(order)],
        out_specs=[pl.BlockSpec((GROUP, HEAD_DIM), lambda i: (0, 0))] * 4,
        out_shape=[sds((GROUP, HEAD_DIM))] * 4,
        scratch_shapes=[
            pltpu.VMEM((T_STEP, KEYS), F32),
            pltpu.VMEM((NODES_HERE, 128), BF),
            pltpu.VMEM((GROUP, NODES_HERE), BF),
            pltpu.VMEM((NODES_HERE, 8), jnp.int32),
        ],
        compiler_params=vm(40),
        cost_estimate=cost(2e9, 12e6),
        name="edge_attention",
    )(place, queries, *kv_parts, counts, order)


def head_sum_kernel(h0, h1, h2, h3, w0, w1, w2, w3, p0, p1, p2, p3):
    heads = jnp.concatenate([h0[...], h1[...], h2[...], h3[...]], axis=1)
    rows = jnp.concatenate([w0[...], w1[...], w2[...], w3[...]], axis=0)
    total = jnp.dot(heads, rows, preferred_element_type=F32).astype(BF)
    for k, p in enumerate((p0, p1, p2, p3)):
        p[...] = total[k * BLOCK : (k + 1) * BLOCK]


def head_sum(heads, shards, row_block):
    d = shards[0].shape[1]
    full = pl.BlockSpec((GROUP, HEAD_DIM), lambda i: (0, 0))
    return pl.pallas_call(
        head_sum_kernel,
        grid=(1,),
        in_specs=[full] * 4 + [pl.BlockSpec((HEAD_DIM, d), lambda i: (row_block, 0))] * 4,
        out_specs=[pl.BlockSpec((BLOCK, d), lambda i: (0, 0))] * 4,
        out_shape=[sds((BLOCK, d))] * 4,
        compiler_params=vm(),
        cost_estimate=cost(7e7, 1e6),
        name="head_sum",
    )(*heads, *shards)


def close_sum_kernel(gain_row, r_ref, p0, p1, p2, p3, gain_ref, stream_ref, normed_ref):
    total = (p0[...].astype(F32) + p1[...].astype(F32)) + (p2[...].astype(F32) + p3[...].astype(F32))
    stream = (r_ref[...].astype(F32) + total).astype(BF)
    stream_ref[...] = stream
    normed_ref[...] = normed_rows(stream.astype(F32), gain_ref[gain_row : gain_row + 1, :])


def close_sum(residual, parts, gains, gain_row):
    shape = residual.shape
    return pl.pallas_call(
        functools.partial(close_sum_kernel, gain_row),
        in_specs=[whole()] * 6,
        out_specs=[whole()] * 2,
        out_shape=[sds(shape), sds(shape)],
        compiler_params=vm(),
        cost_estimate=cost(1e6, 4e5),
        name="close_sum",
    )(residual, *parts, gains)


def final_sum_kernel(r_ref, p0, p1, stream_ref):
    total = p0[...].astype(F32) + p1[...].astype(F32)
    stream_ref[...] = (r_ref[...].astype(F32) + total).astype(BF)


def final_sum(residual, parts):
    return pl.pallas_call(
        final_sum_kernel,
        in_specs=[whole()] * 3,
        out_specs=whole(),
        out_shape=sds(residual.shape),
        compiler_params=vm(),
        cost_estimate=cost(1e6, 4e5),
        name="final_sum",
    )(residual, *parts)


def qkv_kernel(b0, b1, b2, b3, w0, w1, w2, w3, p0, p1, p2, p3):
    rows = jnp.concatenate([b0[...], b1[...], b2[...], b3[...]], axis=0)
    for w, out in ((w0, p0), (w1, p1), (w2, p2), (w3, p3)):
        all_cols = lax.dot_general(rows, w[...], NT, preferred_element_type=F32).astype(BF)
        out[:, :128] = all_cols[:, HEAD_DIM:]
        out[:, 128:] = all_cols[:, :HEAD_DIM]


def qkv(blocks, shards, layer):
    d = blocks[0].shape[1]
    return pl.pallas_call(
        qkv_kernel,
        grid=(1,),
        in_specs=[pl.BlockSpec((BLOCK, d), lambda i: (0, 0))] * 4
        + [pl.BlockSpec((3 * HEAD_DIM, d), lambda i: (layer, 0))] * 4,
        out_specs=[pl.BlockSpec((GROUP, 3 * HEAD_DIM), lambda i: (0, 0))] * 4,
        out_shape=[sds((GROUP, 3 * HEAD_DIM))] * 4,
        compiler_params=vm(),
        cost_estimate=cost(3e8, 2.5e6),
        name="qkv",
    )(*blocks, *shards)


def window_kernel(place_ref, a0, a1, a2, a3, kv_ref, low_ref, high_ref, out_ref):
    kv = kv_ref[...]
    low = low_ref[...]
    high = high_ref[...]
    has_low = place_ref[0] > 0
    has_high = place_ref[0] < place_ref[3] - 1
    places = block_places(place_ref[1])
    col = row_positions(places)
    line = lax.broadcasted_iota(jnp.int32, (GROUP, 1), 0)
    for g, a in enumerate((a0, a1, a2, a3)):
        q = a[:, 128:] * SCALE
        row = jnp.zeros((GROUP, 1), jnp.int32)
        for k in range(4):
            row = jnp.where(line // BLOCK == k, places[g * 4 + k] * BLOCK + line % BLOCK, row)
        s_own = lax.dot_general(q, kv[:, :HEAD_DIM], NT, preferred_element_type=F32)
        s_low = lax.dot_general(q, low[:, :HEAD_DIM], NT, preferred_element_type=F32)
        s_high = lax.dot_general(q, high[:, :HEAD_DIM], NT, preferred_element_type=F32)
        after = col >= row
        in_low = jnp.logical_and(after, has_low)
        in_high = jnp.logical_and(jnp.logical_not(after), has_high)
        s_far = jnp.where(in_low, s_low, jnp.where(in_high, s_high, -jnp.inf))
        top = jnp.maximum(
            jnp.max(s_own, axis=-1, keepdims=True), jnp.max(s_far, axis=-1, keepdims=True)
        )
        e_own = jnp.exp(s_own - top)
        e_far = jnp.exp(s_far - top)
        total = jnp.sum(e_own + e_far, axis=-1, keepdims=True)
        e_low = jnp.where(in_low, e_far, 0.0).astype(BF)
        e_high = jnp.where(in_high, e_far, 0.0).astype(BF)
        out = jnp.dot(e_own.astype(BF), kv, preferred_element_type=F32)
        out += jnp.dot(e_low, low, preferred_element_type=F32)
        out += jnp.dot(e_high, high, preferred_element_type=F32)
        heads = (out / total)[:, HEAD_DIM:].astype(BF)
        for k in range(4):
            out_ref[places[g * 4 + k]] = heads[k * BLOCK : (k + 1) * BLOCK]


def window_attention(place, pieces, kv, low, high):
    return pl.pallas_call(
        window_kernel,
        in_specs=[smem()] + [whole()] * 7,
        out_specs=whole(),
        out_shape=sds((NODES_HERE // BLOCK, BLOCK, HEAD_DIM)),
        compiler_params=vm(),
        cost_estimate=cost(4e8, 1e6),
        name="window_attention",
    )(place, *pieces, kv, low, high)


def one_layer_kernel(w_ref, out_ref):
    out_ref[...] = w_ref[:, 0].reshape(out_ref.shape)


def one_layer(wo_all, layer):
    count, _, rows, d = wo_all.shape
    return pl.pallas_call(
        one_layer_kernel,
        grid=(4,),
        in_specs=[pl.BlockSpec((count // 4, 1, rows, d), lambda i: (i, layer, 0, 0))],
        out_specs=pl.BlockSpec((count // 4 * rows, d), lambda i: (i, 0)),
        out_shape=sds((count * rows, d)),
        compiler_params=vm(),
        cost_estimate=cost(1e5, 2 * count * rows * d * 2),
        name="one_layer",
    )(wo_all)


def heads_to_stream_kernel(gain_row, heads_ref, wo_ref, r_ref, gain_ref, stream_ref, normed_ref):
    count = heads_ref.shape[0]
    heads = jnp.concatenate([heads_ref[h] for h in range(count)], axis=1)
    total = jnp.dot(heads, wo_ref[...], preferred_element_type=F32)
    stream = (r_ref[...].astype(F32) + total).astype(BF)
    stream_ref[...] = stream
    normed_ref[...] = normed_rows(stream.astype(F32), gain_ref[gain_row : gain_row + 1, :])


def heads_to_stream(heads, wo, residual, gains, gain_row):
    return pl.pallas_call(
        functools.partial(heads_to_stream_kernel, gain_row),
        in_specs=[whole()] * 4,
        out_specs=[whole()] * 2,
        out_shape=[sds(residual.shape)] * 2,
        compiler_params=vm(),
        cost_estimate=cost(7e7, 2.5e6),
        name="heads_to_stream",
    )(heads, wo, residual, gains)


def pack_kernel(layer, up_ref, down_ref, out_ref, sems):
    rows = down_ref.shape[1]
    copies = [
        pltpu.make_async_copy(
            up_ref.at[layer, q * rows : (q + 1) * rows],
            out_ref.at[:rows, q * rows : (q + 1) * rows],
            sems.at[q],
        )
        for q in range(4)
    ]
    copies.append(pltpu.make_async_copy(down_ref.at[layer], out_ref.at[rows:, :], sems.at[4]))
    for copy in copies:
        copy.start()
    for copy in copies:
        copy.wait()


def pack(w_up, w_down, layer):
    d, hidden = w_up.shape[1:]
    return pl.pallas_call(
        functools.partial(pack_kernel, layer),
        in_specs=[hbm(), hbm()],
        out_specs=whole(),
        out_shape=sds((2 * hidden, d)),
        scratch_shapes=[pltpu.SemaphoreType.DMA((5,))],
        compiler_params=vm(),
        cost_estimate=cost(1e5, 2e6),
        name="pack",
    )(w_up, w_down)


def feed_forward_kernel(b0, b1, b2, b3, w0, w1, w2, w3, p0, p1, p2, p3):
    rows = jnp.concatenate([b0[...], b1[...], b2[...], b3[...]], axis=0)
    total = None
    for w in (w0, w1, w2, w3):
        hidden = w.shape[0] // 2
        up = None
        for q in range(4):
            cols = slice(q * hidden, (q + 1) * hidden)
            part = jnp.dot(rows[:, cols], w[:hidden, cols], preferred_element_type=F32)
            up = part if up is None else up + part
        part = jnp.dot(jax.nn.gelu(up).astype(BF), w[hidden:, :], preferred_element_type=F32)
        total = part if total is None else total + part
    total = total.astype(BF)
    for k, p in enumerate((p0, p1, p2, p3)):
        p[...] = total[k * BLOCK : (k + 1) * BLOCK]


def feed_forward(blocks, shards):
    d = blocks[0].shape[1]
    return pl.pallas_call(
        feed_forward_kernel,
        in_specs=[whole()] * 8,
        out_specs=[whole()] * 4,
        out_shape=[sds((BLOCK, d))] * 4,
        compiler_params=vm(),
        cost_estimate=cost(5e8, 5e6),
        name="feed_forward",
    )(*blocks, *shards)


def pair_feed_forward_kernel(mine_ref, other_ref, w_ref, own_ref, send_ref, total, held, sems):
    count = held.shape[0]
    hidden = held.shape[1] * 16

    def copy(i):
        return pltpu.make_async_copy(w_ref.at[:, i], held.at[i], sems.at[i])

    for i in range(count):
        copy(i).start()
    rows = jnp.concatenate([mine_ref[...], other_ref[...]], axis=0)
    total[...] = jnp.zeros_like(total)

    def shard(i, carry):
        copy(i).wait()
        up = None
        for q in range(4):
            cols = slice(q * 256, (q + 1) * 256)
            weight = held[i, :, :16, cols].reshape(256, hidden)
            part = jnp.dot(rows[:, cols], weight, preferred_element_type=F32)
            up = part if up is None else up + part
        weight = held[i, :, 16:, :].reshape(hidden, rows.shape[1])
        total[...] += jnp.dot(jax.nn.gelu(up).astype(BF), weight, preferred_element_type=F32)
        return carry

    lax.fori_loop(0, count, shard, 0)
    own_ref[...] = total[:BLOCK, :].astype(BF)
    send_ref[...] = total[BLOCK:, :].astype(BF)


def pair_feed_forward(mine, other, weights):
    d = mine.shape[1]
    bands, count = weights.shape[:2]
    return pl.pallas_call(
        pair_feed_forward_kernel,
        in_specs=[whole(), whole(), hbm()],
        out_specs=[whole()] * 2,
        out_shape=[sds((BLOCK, d))] * 2,
        scratch_shapes=[
            pltpu.VMEM((2 * BLOCK, d), F32),
            pltpu.VMEM((count, bands, 32, d), BF),
            pltpu.SemaphoreType.DMA((count,)),
        ],
        compiler_params=vm(50),
        cost_estimate=cost(5e8, 9e6),
        name="pair_feed_forward",
    )(mine, other, weights)


def sixteenth_kernel(layer, place_ref, up_ref, down_ref, out_ref, sems):
    band = place_ref[0]
    copies = [
        pltpu.make_async_copy(
            up_ref.at[layer, q, band], out_ref.at[:16, q * 256 : (q + 1) * 256], sems.at[q]
        )
        for q in range(4)
    ]
    rows = pl.ds(pl.multiple_of(band * 16, 16), 16)
    copies.append(pltpu.make_async_copy(down_ref.at[layer, rows], out_ref.at[16:, :], sems.at[4]))
    for copy in copies:
        copy.start()
    for copy in copies:
        copy.wait()


def sixteenth(place, w_up, w_down, layer):
    d, hidden = w_up.shape[1:]
    return pl.pallas_call(
        functools.partial(sixteenth_kernel, layer),
        in_specs=[smem(), hbm(), hbm()],
        out_specs=whole(),
        out_shape=sds((32, d)),
        scratch_shapes=[pltpu.SemaphoreType.DMA((5,))],
        compiler_params=vm(63),
        cost_estimate=cost(1e5, 2e5),
        name="sixteenth",
    )(place, w_up.reshape(-1, 4, 16, 16, hidden), w_down)


def one_parity_kernel(place_ref, all_ref, out_ref, sems):
    core = place_ref[1] % 2
    copies = [
        pltpu.make_async_copy(all_ref.at[2 * i + core], out_ref.at[i], sems.at[i])
        for i in range(out_ref.shape[0])
    ]
    for copy in copies:
        copy.start()
    for copy in copies:
        copy.wait()


def one_parity(place, over_head):
    count, rows, d = over_head.shape
    return pl.pallas_call(
        one_parity_kernel,
        in_specs=[smem(), pl.BlockSpec(memory_space=pl.ANY)],
        out_specs=pl.BlockSpec(memory_space=pl.ANY),
        out_shape=sds((count // 2, rows, d)),
        scratch_shapes=[pltpu.SemaphoreType.DMA((count // 2,))],
        compiler_params=vm(),
        cost_estimate=cost(1e5, count * rows * d * 2),
        name="one_parity",
    )(place, over_head)


def shards(
    grid_latent,
    node_latent,
    src_index,
    in_degree,
    node_order,
    norm_gains,
    enc_wq,
    enc_wkv,
    enc_wo,
    proc_wqkv,
    proc_wo,
    w_up,
    w_down,
):
    d = grid_latent.shape[1]
    band = lax.axis_index("band")
    head = lax.axis_index("head")
    place = jnp.stack([band, head, grid_latent.shape[0], lax.axis_size("band")]).astype(jnp.int32)
    order = node_order[None, :]

    barrier = lax.optimization_barrier
    wo_all = lax.all_gather(proc_wo, "head")
    qkv_t = jnp.swapaxes(proc_wqkv, 2, 3).reshape(-1, d)

    tall = jnp.concatenate([qkv_t, enc_wo], axis=0)

    node_blocks = gather_group(node_latent)
    wkv_t = jnp.swapaxes(enc_wkv, 1, 2)
    grid_rows = grid_latent.shape[0]
    edge_low, edge_high, w_both = grid_kv(
        grid_latent, (0, grid_rows - EDGE), EDGE, gains=norm_gains, w=wkv_t
    )
    node_blocks, edge_low, edge_high = barrier((node_blocks, edge_low, edge_high))
    node_group = stack(node_blocks, d)
    node_pieces = exchange([node_group] * 4)
    from_low = up_band(edge_high)
    from_high = down_band(edge_low)
    w_up, w_down, grid_latent, _ = barrier((w_up, w_down, grid_latent, node_group))
    late_part = sixteenth(place, w_up, w_down, 1)
    middle = grid_kv(grid_latent, (EDGE,), grid_rows - 2 * EDGE, w_both=w_both)[0]
    sources, middle, late_part = barrier((src_index.T, middle, late_part))
    counts = edge_counts(place, sources, in_degree[None, :])
    node_pieces, counts, from_low, from_high, tall = barrier((node_pieces, counts, from_low, from_high, tall))

    tall_third, tall_other = outward(tall), swap(tall)
    queries, residual = node_queries(place, node_pieces, norm_gains, enc_wq.T, order)
    kv_parts = [from_low, edge_low, middle, edge_high, from_high]
    enc_heads = edge_attention(place, queries, kv_parts, counts, order)
    enc_heads, tall_third, tall_other, late_part, wo_all = barrier(
        (enc_heads, tall_third, tall_other, late_part, wo_all)
    )
    late_weights = lax.all_gather(late_part, "head")
    tall_shards = [tall, tall_other, tall_third, swap(tall_third)]
    sums = head_sum(give_back(enc_heads), tall_shards, qkv_t.shape[0] // HEAD_DIM)
    stream, normed = close_sum(residual, scatter_group(sums), norm_gains, 2)

    for layer in range(LAYERS):
        blocks = gather_group(normed)
        if layer == 0:
            w_up, w_down, _ = barrier((w_up, w_down, normed))
            blocks, first = barrier((blocks, pack(w_up, w_down, 0)))
        pieces = exchange(qkv(blocks, tall_shards, layer))
        kv = stack(pieces, 2 * HEAD_DIM)
        low = up_band(kv)
        high = down_band(kv)
        wo_all, _ = barrier((wo_all, kv))
        wo = one_layer(wo_all, layer)
        low, high, wo = barrier((low, high, wo))
        if layer == 0:
            first, late_weights, _ = barrier((first, late_weights, kv))
            first_third, first_other = outward(first), swap(first)
            late_weights = one_parity(place, late_weights)
            low, high, late_weights, first_third, first_other = barrier(
                (low, high, late_weights, first_third, first_other)
            )
        win_heads = window_attention(place, pieces, kv, low, high)
        if layer == 0:
            win_heads, late_weights = barrier((win_heads, late_weights))
            late_weights = lax.all_gather(late_weights, "band")
            first_shards = [first, first_other, first_third, swap(first_third)]
        win_heads = lax.all_to_all(win_heads, "head", 0, 0)
        stream, normed = heads_to_stream(win_heads, wo, stream, norm_gains, 3 + 2 * layer)
        if layer == 0:
            parts = scatter_group(feed_forward(gather_group(normed), first_shards))
            stream, normed = close_sum(stream, parts, norm_gains, 4 + 2 * layer)
        else:
            own, other = pair_feed_forward(normed, swap(normed), late_weights)
            stream = final_sum(stream, [own, swap(other)])
    return stream


def solution(mesh):
    in_specs = (
        P("band", None),
        P(("band", "head"), None),
        P("band", None),
        P("band"),
        P("band"),
        P(),
        P(None, "head"),
        P(None, None, "head"),
        P("head", None),
        P(None, None, None, "head"),
        P(None, "head", None),
        P(None, None, "head"),
        P(None, "head", None),
    )
    out_specs = P(("band", "head"), None)
    return jax.shard_map(shards, mesh=mesh, in_specs=in_specs, out_specs=out_specs, check_vma=False)
```

```python
import functools
import math

import jax
import jax.numpy as jnp
from jax import lax
from jax.experimental import pallas as pl
from jax.experimental.pallas import tpu as pltpu
from jax.sharding import PartitionSpec as P

HEAD_DIM = 64
K_MAX = 32
HALF_WIN = 512
LAYERS = 2
EDGE = 1536
KV_BLOCK = 512
BLOCK = 32
GROUP = 128
NODES_HERE = 512
KEYS = 7168
SCALE = 1.0 / math.sqrt(HEAD_DIM)
BF = jnp.bfloat16
F32 = jnp.float32
NT = (((1,), (1,)), ((), ()))


def vm(limit_mib=20):
    return pltpu.CompilerParams(vmem_limit_bytes=limit_mib * 1024 * 1024)


def cost(flops, nbytes):
    return pl.CostEstimate(flops=int(flops), bytes_accessed=int(nbytes), transcendentals=0)


def whole():
    return pl.BlockSpec(memory_space=pltpu.VMEM)


def hbm():
    return pl.BlockSpec(memory_space=pltpu.HBM)


def smem():
    return pl.BlockSpec(memory_space=pltpu.SMEM)


def sds(shape, dtype=BF):
    return jax.ShapeDtypeStruct(shape, dtype)


def swap(x):
    return lax.ppermute(x, "head", [(i, i ^ 1) for i in range(16)])


def shift_z(x, k):
    steps = (k, -k)
    return lax.ppermute(x, "head", [(i, ((i // 2 + steps[i % 2]) % 8) * 2 + i % 2) for i in range(16)])


def outward_pairs():
    return [(2 * z + c, 2 * ((z + (1 if c else -1)) % 8) + c) for z in range(8) for c in range(2)]


def outward(x):
    return lax.ppermute(x, "head", outward_pairs())


def inward(x):
    return lax.ppermute(x, "head", [(t, s) for s, t in outward_pairs()])


def crossed(x):
    pairs = [(2 * z, 2 * ((z - 1) % 8) + 1) for z in range(8)]
    return lax.ppermute(x, "head", pairs + [(t, s) for s, t in pairs])


def up_band(x):
    return lax.ppermute(x, "band", [(i, i + 1) for i in range(15)])


def down_band(x):
    return lax.ppermute(x, "band", [(i + 1, i) for i in range(15)])


def gather_group(x):
    behind = shift_z(x, 2)
    ahead = shift_z(x, -2)
    far = shift_z(x, 4)
    return [x, ahead, far, behind]


def scatter_group(parts):
    return [parts[0], shift_z(parts[1], 2), shift_z(parts[2], 4), shift_z(parts[3], -2)]


def four_shards(x):
    third = outward(x)
    return [x, swap(x), third, swap(third)]


def exchange(pieces):
    return [pieces[0], swap(pieces[1]), inward(pieces[2]), crossed(pieces[3])]


def give_back(pieces):
    return [pieces[0], swap(pieces[1]), outward(pieces[2]), crossed(pieces[3])]


def stack_kernel(b0, b1, b2, b3, out_ref):
    rows, cols = b0.shape[0], out_ref.shape[1]
    for k, b in enumerate((b0, b1, b2, b3)):
        out_ref[k * rows : (k + 1) * rows, :] = b[:, :cols]


def stack(blocks, cols):
    rows = blocks[0].shape[0]
    return pl.pallas_call(
        stack_kernel,
        in_specs=[whole()] * 4,
        out_specs=whole(),
        out_shape=sds((4 * rows, cols)),
        compiler_params=vm(),
        cost_estimate=cost(1e5, 4 * rows * cols * 4),
        name="stack",
    )(*blocks)


def normed_rows(values, gain):
    mean = jnp.mean(values, axis=-1, keepdims=True)
    centred = values - mean
    variance = jnp.mean(centred * centred, axis=-1, keepdims=True)
    return (centred * lax.rsqrt(variance + 1e-05) * gain).astype(BF)


def grid_kv_kernel(starts, first, x_ref, *refs):
    if first:
        gain_ref, w_ref, *refs = refs
    else:
        w_both, *refs = refs
    outs, refs = refs[: len(starts)], refs[len(starts) :]
    if first:
        w_both, *refs = refs
    rows, sems = refs
    blocks = outs[0].shape[0] // KV_BLOCK
    copies = [
        pltpu.make_async_copy(
            x_ref.at[pl.ds(start + i * KV_BLOCK, KV_BLOCK)],
            rows.at[part * blocks + i],
            sems.at[part * blocks + i],
        )
        for part, start in enumerate(starts)
        for i in range(blocks)
    ]
    for copy in copies:
        copy.start()
    if first:
        for i in range(2):
            turned = jnp.transpose(w_ref[i].astype(F32) * gain_ref[0:1, :]).astype(BF)
            w_both[:, i * HEAD_DIM : (i + 1) * HEAD_DIM] = turned
    for part, out in enumerate(outs):
        for i in range(blocks):
            copies[part * blocks + i].wait()

            x = rows[part * blocks + i].astype(F32)
            x = x - jnp.mean(x, axis=-1, keepdims=True)
            variance = jnp.mean(x * x, axis=-1, keepdims=True)
            scale = lax.rsqrt(variance + 1e-05)
            x = x.astype(BF)
            for line in range(0, KV_BLOCK, 128):
                kv = jnp.dot(x[line : line + 128], w_both[...], preferred_element_type=F32)
                at = i * KV_BLOCK + line
                out[at : at + 128, :] = (kv * scale[line : line + 128]).astype(BF)


def grid_kv(grid_latent, starts, count, gains=None, w=None, w_both=None):
    d = grid_latent.shape[1]
    blocks = len(starts) * count // KV_BLOCK
    first = w_both is None
    weight_shape = sds((d, 128))
    out_shape = [sds((count, 128))] * len(starts) + ([weight_shape] if first else [])
    return pl.pallas_call(
        functools.partial(grid_kv_kernel, starts, first),
        in_specs=[hbm()] + [whole()] * (2 if first else 1),
        out_specs=[whole()] * len(out_shape),
        out_shape=out_shape,
        scratch_shapes=[
            pltpu.VMEM((blocks, KV_BLOCK, d), BF),
            pltpu.SemaphoreType.DMA((blocks,)),
        ],
        compiler_params=vm(56),
        cost_estimate=cost(2 * blocks * KV_BLOCK * d * 128, blocks * KV_BLOCK * d * 2),
        name="grid_kv",
    )(grid_latent, *((gains, w) if first else (w_both,)))


COUNT_STEP = 64
TILES = KEYS // 128


def edge_count_kernel(place_ref, src_ref, degree_ref, out_ref, by_node, high_key, low_key):
    step = pl.program_id(0)

    @pl.when(step == 0)
    def _():
        shape = src_ref.shape
        local = src_ref[...] - (place_ref[0] * place_ref[2] - EDGE)
        used = lax.broadcasted_iota(jnp.int32, shape, 0) < degree_ref[...]
        by_node[...] = jnp.transpose(jnp.where(used, local, -1))
        for t in range(8):
            local_rows = by_node[pl.ds(t, NODES_HERE // 8, stride=8), :]
            cols = slice(t * K_MAX, (t + 1) * K_MAX)
            high_key[:, cols] = jnp.where(local_rows < 0, -1, (local_rows >> 7) * 8 + t)
            low_key[:, cols] = local_rows & 127

    row_high = lax.broadcasted_iota(jnp.int32, (TILES * 8, 256), 0)
    row_low = lax.broadcasted_iota(jnp.int32, (128, 256), 0)

    def counts(group):
        left = jnp.where(row_high == high_key[pl.ds(group, 1), :], 1.0, 0.0).astype(BF)
        right = jnp.where(row_low == low_key[pl.ds(group, 1), :], 1.0, 0.0).astype(BF)
        return lax.dot_general(left, right, NT, preferred_element_type=F32)

    def pair(i, carry):
        group = step * (COUNT_STEP // 8) + 2 * i
        first = counts(group)
        second = counts(group + 1)
        rows = pl.ds(pl.multiple_of(i * 16, 16), 16)
        for t in range(TILES):
            both = jnp.concatenate([first[t * 8 : t * 8 + 8], second[t * 8 : t * 8 + 8]], axis=0)
            out_ref[rows, t * 128 : (t + 1) * 128] = both.astype(BF)
        return carry

    lax.fori_loop(0, COUNT_STEP // 16, pair, 0, unroll=COUNT_STEP // 16)


def edge_counts(place, sources, degrees):
    return pl.pallas_call(
        edge_count_kernel,
        grid=(NODES_HERE // COUNT_STEP,),
        in_specs=[
            smem(),
            pl.BlockSpec(sources.shape, lambda i: (0, 0)),
            pl.BlockSpec(degrees.shape, lambda i: (0, 0)),
        ],
        out_specs=pl.BlockSpec((COUNT_STEP, KEYS), lambda i: (i, 0)),
        out_shape=sds((NODES_HERE, KEYS)),
        scratch_shapes=[
            pltpu.VMEM((NODES_HERE, K_MAX), jnp.int32),
            pltpu.VMEM((NODES_HERE // 8, 8 * K_MAX), jnp.int32),
            pltpu.VMEM((NODES_HERE // 8, 8 * K_MAX), jnp.int32),
        ],
        compiler_params=vm(),
        cost_estimate=cost(4e9, 10e6),
        name="edge_counts",
    )(place, sources, degrees)


def block_places(head):
    z, core = head // 2, head % 2
    side = 2 * core - 1
    places = []
    for g in range(4):
        from_z = z if g < 2 else z + side
        from_core = core if g % 2 == 0 else 1 - core
        step = 2 - 4 * from_core
        places += [2 * ((from_z + step * k + 16) & 7) + from_core for k in range(4)]
    return places


def row_positions(places):
    lane = lax.broadcasted_iota(jnp.int32, (1, NODES_HERE), 1)
    pos = jnp.zeros((1, NODES_HERE), jnp.int32)
    for i, place in enumerate(places):
        pos = jnp.where(lane // BLOCK == i, place * BLOCK + lane % BLOCK, pos)
    return pos


def node_query_kernel(place_ref, r0, r1, r2, r3, gain_ref, w_ref, order_ref, q_ref, mine_ref, order_col, rows):
    head = place_ref[1]
    places = block_places(head)
    for g, r in enumerate((r0, r1, r2, r3)):
        rows[g * GROUP : (g + 1) * GROUP, :] = r[...]
        normed = normed_rows(r[...].astype(F32), gain_ref[1:2, :])
        q = lax.dot_general(normed, w_ref[...], NT, preferred_element_type=F32).astype(BF)
        for k in range(4):
            start = pl.multiple_of(places[g * 4 + k] * BLOCK, BLOCK)
            q_ref[pl.ds(start, BLOCK), :] = q[k * BLOCK : (k + 1) * BLOCK, :]
    local = order_ref[...] - place_ref[0] * NODES_HERE
    order_col[...] = jnp.transpose(jnp.broadcast_to(local, (8, NODES_HERE)))
    wanted = order_col[pl.ds(pl.multiple_of(head * BLOCK, BLOCK), BLOCK), 0:1]
    pick = jnp.where(row_positions(places) == wanted, 1.0, 0.0).astype(BF)
    mine_ref[...] = jnp.dot(pick, rows[...], preferred_element_type=F32).astype(BF)


def node_queries(place, pieces, gains, wq_t, order):
    d = wq_t.shape[1]
    return pl.pallas_call(
        node_query_kernel,
        in_specs=[smem()] + [whole()] * 7,
        out_specs=[whole()] * 2,
        out_shape=[sds((NODES_HERE, HEAD_DIM)), sds((BLOCK, d))],
        scratch_shapes=[pltpu.VMEM((NODES_HERE, 8), jnp.int32), pltpu.VMEM((NODES_HERE, d), BF)],
        compiler_params=vm(),
        cost_estimate=cost(1e8, 2e6),
        name="node_queries",
    )(place, *pieces, gains, wq_t, order)


T_STEP = 256
CHUNK = 512


def edge_attention_kernel(
    place_ref, q_all, kv0, kv1, kv2, kv3, kv4, count_ref, order_ref,
    o0, o1, o2, o3, scores, heads, pick, order_col,
):
    step = pl.program_id(0)
    q = q_all[pl.ds(pl.multiple_of(step * T_STEP, T_STEP), T_STEP), :] * SCALE
    chunks = []
    for kv in (kv0, kv1, kv2, kv3, kv4):
        for start in range(0, kv.shape[0], CHUNK):
            chunks.append((kv, start))
    top = None
    for i, (kv, start) in enumerate(chunks):
        keys = kv[start : start + CHUNK, :][:, :HEAD_DIM]
        s = lax.dot_general(q, keys, NT, preferred_element_type=F32)
        cols = slice(i * CHUNK, (i + 1) * CHUNK)
        s = jnp.where(count_ref[:, cols].astype(F32) > 0.0, s, -jnp.inf)
        scores[:, cols] = s
        part = jnp.maximum(
            jnp.maximum(s[:, 0:128], s[:, 128:256]), jnp.maximum(s[:, 256:384], s[:, 384:512])
        )
        top = part if top is None else jnp.maximum(top, part)
    top = jnp.max(top, axis=-1, keepdims=True)
    total = jnp.zeros((T_STEP, 128), F32)
    out = jnp.zeros((T_STEP, 128), F32)
    for i, (kv, start) in enumerate(chunks):
        cols = slice(i * CHUNK, (i + 1) * CHUNK)
        e = jnp.exp(scores[:, cols] - top) * count_ref[:, cols].astype(F32)
        total += (e[:, 0:128] + e[:, 128:256]) + (e[:, 256:384] + e[:, 384:512])
        out += jnp.dot(e.astype(BF), kv[start : start + CHUNK, :], preferred_element_type=F32)
    total = jnp.sum(total, axis=-1, keepdims=True)
    rows = pl.ds(pl.multiple_of(step * T_STEP, T_STEP), T_STEP)
    heads[rows, :] = (out / total).astype(BF)

    @pl.when(step == pl.num_programs(0) - 1)
    def _():
        local = order_ref[...] - place_ref[0] * NODES_HERE
        order_col[...] = jnp.transpose(jnp.broadcast_to(local, (8, NODES_HERE)))
        places = block_places(place_ref[1])
        node = lax.broadcasted_iota(jnp.int32, (BLOCK, NODES_HERE), 1)
        for g, o in enumerate((o0, o1, o2, o3)):
            for k in range(4):
                start = pl.multiple_of(places[g * 4 + k] * BLOCK, BLOCK)
                wanted = order_col[pl.ds(start, BLOCK), 0:1]
                pick[k * BLOCK : (k + 1) * BLOCK, :] = jnp.where(node == wanted, 1.0, 0.0).astype(BF)
            taken = jnp.dot(pick[...], heads[...], preferred_element_type=F32)
            o[...] = taken[:, HEAD_DIM:].astype(BF)


def edge_attention(place, queries, kv_parts, counts, order):
    def full(x):
        return pl.BlockSpec(x.shape, lambda i: (0,) * x.ndim)

    return pl.pallas_call(
        edge_attention_kernel,
        grid=(NODES_HERE // T_STEP,),
        in_specs=[smem(), full(queries)]
        + [full(kv) for kv in kv_parts]
        + [pl.BlockSpec((T_STEP, KEYS), lambda i: (i, 0)), full(order)],
        out_specs=[pl.BlockSpec((GROUP, HEAD_DIM), lambda i: (0, 0))] * 4,
        out_shape=[sds((GROUP, HEAD_DIM))] * 4,
        scratch_shapes=[
            pltpu.VMEM((T_STEP, KEYS), F32),
            pltpu.VMEM((NODES_HERE, 128), BF),
            pltpu.VMEM((GROUP, NODES_HERE), BF),
            pltpu.VMEM((NODES_HERE, 8), jnp.int32),
        ],
        compiler_params=vm(40),
        cost_estimate=cost(2e9, 12e6),
        name="edge_attention",
    )(place, queries, *kv_parts, counts, order)


def head_sum_kernel(h0, h1, h2, h3, w0, w1, w2, w3, p0, p1, p2, p3):
    heads = jnp.concatenate([h0[...], h1[...], h2[...], h3[...]], axis=1)
    rows = jnp.concatenate([w0[...], w1[...], w2[...], w3[...]], axis=0)
    total = jnp.dot(heads, rows, preferred_element_type=F32).astype(BF)
    for k, p in enumerate((p0, p1, p2, p3)):
        p[...] = total[k * BLOCK : (k + 1) * BLOCK]


def head_sum(heads, shards, row_block):
    d = shards[0].shape[1]
    full = pl.BlockSpec((GROUP, HEAD_DIM), lambda i: (0, 0))
    return pl.pallas_call(
        head_sum_kernel,
        grid=(1,),
        in_specs=[full] * 4 + [pl.BlockSpec((HEAD_DIM, d), lambda i: (row_block, 0))] * 4,
        out_specs=[pl.BlockSpec((BLOCK, d), lambda i: (0, 0))] * 4,
        out_shape=[sds((BLOCK, d))] * 4,
        compiler_params=vm(),
        cost_estimate=cost(7e7, 1e6),
        name="head_sum",
    )(*heads, *shards)


def close_sum_kernel(gain_row, r_ref, p0, p1, p2, p3, gain_ref, stream_ref, normed_ref):
    total = (p0[...].astype(F32) + p1[...].astype(F32)) + (p2[...].astype(F32) + p3[...].astype(F32))
    stream = (r_ref[...].astype(F32) + total).astype(BF)
    stream_ref[...] = stream
    normed_ref[...] = normed_rows(stream.astype(F32), gain_ref[gain_row : gain_row + 1, :])


def close_sum(residual, parts, gains, gain_row):
    shape = residual.shape
    return pl.pallas_call(
        functools.partial(close_sum_kernel, gain_row),
        in_specs=[whole()] * 6,
        out_specs=[whole()] * 2,
        out_shape=[sds(shape), sds(shape)],
        compiler_params=vm(),
        cost_estimate=cost(1e6, 4e5),
        name="close_sum",
    )(residual, *parts, gains)


def final_sum_kernel(r_ref, p0, p1, stream_ref):
    total = p0[...].astype(F32) + p1[...].astype(F32)
    stream_ref[...] = (r_ref[...].astype(F32) + total).astype(BF)


def final_sum(residual, parts):
    return pl.pallas_call(
        final_sum_kernel,
        in_specs=[whole()] * 3,
        out_specs=whole(),
        out_shape=sds(residual.shape),
        compiler_params=vm(),
        cost_estimate=cost(1e6, 4e5),
        name="final_sum",
    )(residual, *parts)


def qkv_kernel(b0, b1, b2, b3, w0, w1, w2, w3, p0, p1, p2, p3):
    rows = jnp.concatenate([b0[...], b1[...], b2[...], b3[...]], axis=0)
    for w, out in ((w0, p0), (w1, p1), (w2, p2), (w3, p3)):
        all_cols = lax.dot_general(rows, w[...], NT, preferred_element_type=F32).astype(BF)
        out[:, :128] = all_cols[:, HEAD_DIM:]
        out[:, 128:] = all_cols[:, :HEAD_DIM]


def qkv(blocks, shards, layer):
    d = blocks[0].shape[1]
    return pl.pallas_call(
        qkv_kernel,
        grid=(1,),
        in_specs=[pl.BlockSpec((BLOCK, d), lambda i: (0, 0))] * 4
        + [pl.BlockSpec((3 * HEAD_DIM, d), lambda i: (layer, 0))] * 4,
        out_specs=[pl.BlockSpec((GROUP, 3 * HEAD_DIM), lambda i: (0, 0))] * 4,
        out_shape=[sds((GROUP, 3 * HEAD_DIM))] * 4,
        compiler_params=vm(),
        cost_estimate=cost(3e8, 2.5e6),
        name="qkv",
    )(*blocks, *shards)


def window_kernel(place_ref, a0, a1, a2, a3, kv_ref, low_ref, high_ref, out_ref):
    kv = kv_ref[...]
    low = low_ref[...]
    high = high_ref[...]
    has_low = place_ref[0] > 0
    has_high = place_ref[0] < place_ref[3] - 1
    places = block_places(place_ref[1])
    col = row_positions(places)
    line = lax.broadcasted_iota(jnp.int32, (GROUP, 1), 0)
    for g, a in enumerate((a0, a1, a2, a3)):
        q = a[:, 128:] * SCALE
        row = jnp.zeros((GROUP, 1), jnp.int32)
        for k in range(4):
            row = jnp.where(line // BLOCK == k, places[g * 4 + k] * BLOCK + line % BLOCK, row)
        s_own = lax.dot_general(q, kv[:, :HEAD_DIM], NT, preferred_element_type=F32)
        s_low = lax.dot_general(q, low[:, :HEAD_DIM], NT, preferred_element_type=F32)
        s_high = lax.dot_general(q, high[:, :HEAD_DIM], NT, preferred_element_type=F32)
        after = col >= row
        in_low = jnp.logical_and(after, has_low)
        in_high = jnp.logical_and(jnp.logical_not(after), has_high)
        s_far = jnp.where(in_low, s_low, jnp.where(in_high, s_high, -jnp.inf))
        top = jnp.maximum(
            jnp.max(s_own, axis=-1, keepdims=True), jnp.max(s_far, axis=-1, keepdims=True)
        )
        e_own = jnp.exp(s_own - top)
        e_far = jnp.exp(s_far - top)
        total = jnp.sum(e_own + e_far, axis=-1, keepdims=True)
        e_low = jnp.where(in_low, e_far, 0.0).astype(BF)
        e_high = jnp.where(in_high, e_far, 0.0).astype(BF)
        out = jnp.dot(e_own.astype(BF), kv, preferred_element_type=F32)
        out += jnp.dot(e_low, low, preferred_element_type=F32)
        out += jnp.dot(e_high, high, preferred_element_type=F32)
        heads = (out / total)[:, HEAD_DIM:].astype(BF)
        for k in range(4):
            out_ref[places[g * 4 + k]] = heads[k * BLOCK : (k + 1) * BLOCK]


def window_attention(place, pieces, kv, low, high):
    return pl.pallas_call(
        window_kernel,
        in_specs=[smem()] + [whole()] * 7,
        out_specs=whole(),
        out_shape=sds((NODES_HERE // BLOCK, BLOCK, HEAD_DIM)),
        compiler_params=vm(),
        cost_estimate=cost(4e8, 1e6),
        name="window_attention",
    )(place, *pieces, kv, low, high)


def one_layer_kernel(w_ref, out_ref):
    out_ref[...] = w_ref[:, 0].reshape(out_ref.shape)


def one_layer(wo_all, layer):
    count, _, rows, d = wo_all.shape
    return pl.pallas_call(
        one_layer_kernel,
        grid=(4,),
        in_specs=[pl.BlockSpec((count // 4, 1, rows, d), lambda i: (i, layer, 0, 0))],
        out_specs=pl.BlockSpec((count // 4 * rows, d), lambda i: (i, 0)),
        out_shape=sds((count * rows, d)),
        compiler_params=vm(),
        cost_estimate=cost(1e5, 2 * count * rows * d * 2),
        name="one_layer",
    )(wo_all)


def heads_to_stream_kernel(gain_row, heads_ref, wo_ref, r_ref, gain_ref, stream_ref, normed_ref):
    count = heads_ref.shape[0]
    heads = jnp.concatenate([heads_ref[h] for h in range(count)], axis=1)
    total = jnp.dot(heads, wo_ref[...], preferred_element_type=F32)
    stream = (r_ref[...].astype(F32) + total).astype(BF)
    stream_ref[...] = stream
    normed_ref[...] = normed_rows(stream.astype(F32), gain_ref[gain_row : gain_row + 1, :])


def heads_to_stream(heads, wo, residual, gains, gain_row):
    return pl.pallas_call(
        functools.partial(heads_to_stream_kernel, gain_row),
        in_specs=[whole()] * 4,
        out_specs=[whole()] * 2,
        out_shape=[sds(residual.shape)] * 2,
        compiler_params=vm(),
        cost_estimate=cost(7e7, 2.5e6),
        name="heads_to_stream",
    )(heads, wo, residual, gains)


def pack_kernel(layer, up_ref, down_ref, out_ref, sems):
    rows = down_ref.shape[1]
    copies = [
        pltpu.make_async_copy(
            up_ref.at[layer, q * rows : (q + 1) * rows],
            out_ref.at[:rows, q * rows : (q + 1) * rows],
            sems.at[q],
        )
        for q in range(4)
    ]
    copies.append(pltpu.make_async_copy(down_ref.at[layer], out_ref.at[rows:, :], sems.at[4]))
    for copy in copies:
        copy.start()
    for copy in copies:
        copy.wait()


def pack(w_up, w_down, layer):
    d, hidden = w_up.shape[1:]
    return pl.pallas_call(
        functools.partial(pack_kernel, layer),
        in_specs=[hbm(), hbm()],
        out_specs=whole(),
        out_shape=sds((2 * hidden, d)),
        scratch_shapes=[pltpu.SemaphoreType.DMA((5,))],
        compiler_params=vm(),
        cost_estimate=cost(1e5, 2e6),
        name="pack",
    )(w_up, w_down)


def feed_forward_kernel(b0, b1, b2, b3, w0, w1, w2, w3, p0, p1, p2, p3):
    rows = jnp.concatenate([b0[...], b1[...], b2[...], b3[...]], axis=0)
    total = None
    for w in (w0, w1, w2, w3):
        hidden = w.shape[0] // 2
        up = None
        for q in range(4):
            cols = slice(q * hidden, (q + 1) * hidden)
            part = jnp.dot(rows[:, cols], w[:hidden, cols], preferred_element_type=F32)
            up = part if up is None else up + part
        part = jnp.dot(jax.nn.gelu(up).astype(BF), w[hidden:, :], preferred_element_type=F32)
        total = part if total is None else total + part
    total = total.astype(BF)
    for k, p in enumerate((p0, p1, p2, p3)):
        p[...] = total[k * BLOCK : (k + 1) * BLOCK]


def feed_forward(blocks, shards):
    d = blocks[0].shape[1]
    return pl.pallas_call(
        feed_forward_kernel,
        in_specs=[whole()] * 8,
        out_specs=[whole()] * 4,
        out_shape=[sds((BLOCK, d))] * 4,
        compiler_params=vm(),
        cost_estimate=cost(5e8, 5e6),
        name="feed_forward",
    )(*blocks, *shards)


def pair_feed_forward_kernel(mine_ref, other_ref, w_ref, own_ref, send_ref, total, held, sems):
    count = held.shape[0]
    hidden = held.shape[1] * 16

    def copy(i):
        return pltpu.make_async_copy(w_ref.at[:, i], held.at[i], sems.at[i])

    for i in range(count):
        copy(i).start()
    rows = jnp.concatenate([mine_ref[...], other_ref[...]], axis=0)
    total[...] = jnp.zeros_like(total)

    def shard(i, carry):
        copy(i).wait()
        up = None
        for q in range(4):
            cols = slice(q * 256, (q + 1) * 256)
            weight = held[i, :, :16, cols].reshape(256, hidden)
            part = jnp.dot(rows[:, cols], weight, preferred_element_type=F32)
            up = part if up is None else up + part
        weight = held[i, :, 16:, :].reshape(hidden, rows.shape[1])
        total[...] += jnp.dot(jax.nn.gelu(up).astype(BF), weight, preferred_element_type=F32)
        return carry

    lax.fori_loop(0, count, shard, 0)
    own_ref[...] = total[:BLOCK, :].astype(BF)
    send_ref[...] = total[BLOCK:, :].astype(BF)


def pair_feed_forward(mine, other, weights):
    d = mine.shape[1]
    bands, count = weights.shape[:2]
    return pl.pallas_call(
        pair_feed_forward_kernel,
        in_specs=[whole(), whole(), hbm()],
        out_specs=[whole()] * 2,
        out_shape=[sds((BLOCK, d))] * 2,
        scratch_shapes=[
            pltpu.VMEM((2 * BLOCK, d), F32),
            pltpu.VMEM((count, bands, 32, d), BF),
            pltpu.SemaphoreType.DMA((count,)),
        ],
        compiler_params=vm(50),
        cost_estimate=cost(5e8, 9e6),
        name="pair_feed_forward",
    )(mine, other, weights)


def sixteenth_kernel(layer, place_ref, up_ref, down_ref, out_ref, sems):
    band = place_ref[0]
    copies = [
        pltpu.make_async_copy(
            up_ref.at[layer, q, band], out_ref.at[:16, q * 256 : (q + 1) * 256], sems.at[q]
        )
        for q in range(4)
    ]
    rows = pl.ds(pl.multiple_of(band * 16, 16), 16)
    copies.append(pltpu.make_async_copy(down_ref.at[layer, rows], out_ref.at[16:, :], sems.at[4]))
    for copy in copies:
        copy.start()
    for copy in copies:
        copy.wait()


def sixteenth(place, w_up, w_down, layer):
    d, hidden = w_up.shape[1:]
    return pl.pallas_call(
        functools.partial(sixteenth_kernel, layer),
        in_specs=[smem(), hbm(), hbm()],
        out_specs=whole(),
        out_shape=sds((32, d)),
        scratch_shapes=[pltpu.SemaphoreType.DMA((5,))],
        compiler_params=vm(63),
        cost_estimate=cost(1e5, 2e5),
        name="sixteenth",
    )(place, w_up.reshape(-1, 4, 16, 16, hidden), w_down)


def one_parity_kernel(place_ref, all_ref, out_ref):
    out_ref[...] = all_ref[...]


def one_parity(place, over_head):
    count, rows, d = over_head.shape
    block = (count // 8, 1, rows, d)
    grid_spec = pltpu.PrefetchScalarGridSpec(
        num_scalar_prefetch=1,
        grid=(4,),
        in_specs=[pl.BlockSpec(block, lambda i, place: (i, place[1] & 1, 0, 0))],
        out_specs=pl.BlockSpec(block, lambda i, place: (i, 0, 0, 0)),
    )
    return pl.pallas_call(
        one_parity_kernel,
        grid_spec=grid_spec,
        out_shape=sds((count // 2, 1, rows, d)),
        compiler_params=vm(),
        cost_estimate=cost(1e5, count * rows * d * 2),
        name="one_parity",
    )(place, over_head.reshape(count // 2, 2, rows, d)).reshape(count // 2, rows, d)


def shards(
    grid_latent,
    node_latent,
    src_index,
    in_degree,
    node_order,
    norm_gains,
    enc_wq,
    enc_wkv,
    enc_wo,
    proc_wqkv,
    proc_wo,
    w_up,
    w_down,
):
    d = grid_latent.shape[1]
    band = lax.axis_index("band")
    head = lax.axis_index("head")
    place = jnp.stack([band, head, grid_latent.shape[0], lax.axis_size("band")]).astype(jnp.int32)
    order = node_order[None, :]

    barrier = lax.optimization_barrier
    wo_all = lax.all_gather(proc_wo, "head")
    qkv_t = jnp.swapaxes(proc_wqkv, 2, 3).reshape(-1, d)

    tall = jnp.concatenate([qkv_t, enc_wo], axis=0)

    node_blocks = gather_group(node_latent)
    wkv_t = jnp.swapaxes(enc_wkv, 1, 2)
    grid_rows = grid_latent.shape[0]
    edge_low, edge_high, w_both = grid_kv(
        grid_latent, (0, grid_rows - EDGE), EDGE, gains=norm_gains, w=wkv_t
    )
    node_blocks, edge_low, edge_high = barrier((node_blocks, edge_low, edge_high))
    node_group = stack(node_blocks, d)
    node_pieces = exchange([node_group] * 4)
    from_low = up_band(edge_high)
    from_high = down_band(edge_low)
    w_up, w_down, grid_latent, _ = barrier((w_up, w_down, grid_latent, node_group))
    late_part = sixteenth(place, w_up, w_down, 1)
    middle = grid_kv(grid_latent, (EDGE,), grid_rows - 2 * EDGE, w_both=w_both)[0]
    sources, middle, late_part = barrier((src_index.T, middle, late_part))
    counts = edge_counts(place, sources, in_degree[None, :])
    node_pieces, counts, from_low, from_high, tall = barrier((node_pieces, counts, from_low, from_high, tall))

    tall_third, tall_other = outward(tall), swap(tall)
    queries, residual = node_queries(place, node_pieces, norm_gains, enc_wq.T, order)
    kv_parts = [from_low, edge_low, middle, edge_high, from_high]
    enc_heads = edge_attention(place, queries, kv_parts, counts, order)
    enc_heads, tall_third, tall_other, late_part, wo_all = barrier(
        (enc_heads, tall_third, tall_other, late_part, wo_all)
    )
    late_weights = lax.all_gather(late_part, "head")
    tall_shards = [tall, tall_other, tall_third, swap(tall_third)]
    sums = head_sum(give_back(enc_heads), tall_shards, qkv_t.shape[0] // HEAD_DIM)
    stream, normed = close_sum(residual, scatter_group(sums), norm_gains, 2)

    for layer in range(LAYERS):
        blocks = gather_group(normed)
        if layer == 0:
            w_up, w_down, _ = barrier((w_up, w_down, normed))
            blocks, first = barrier((blocks, pack(w_up, w_down, 0)))
        pieces = exchange(qkv(blocks, tall_shards, layer))
        kv = stack(pieces, 2 * HEAD_DIM)
        low = up_band(kv)
        high = down_band(kv)
        wo_all, _ = barrier((wo_all, kv))
        wo = one_layer(wo_all, layer)
        low, high, wo = barrier((low, high, wo))
        if layer == 0:
            first, late_weights, _ = barrier((first, late_weights, kv))
            first_third, first_other = outward(first), swap(first)
            late_weights = one_parity(place, late_weights)
            low, high, late_weights, first_third, first_other = barrier(
                (low, high, late_weights, first_third, first_other)
            )
            late_weights = lax.all_gather(late_weights, "band")
        win_heads = window_attention(place, pieces, kv, low, high)
        if layer == 0:
            first_shards = [first, first_other, first_third, swap(first_third)]
        win_heads = lax.all_to_all(win_heads, "head", 0, 0)
        stream, normed = heads_to_stream(win_heads, wo, stream, norm_gains, 3 + 2 * layer)
        if layer == 0:
            parts = scatter_group(feed_forward(gather_group(normed), first_shards))
            stream, normed = close_sum(stream, parts, norm_gains, 4 + 2 * layer)
        else:
            own, other = pair_feed_forward(normed, swap(normed), late_weights)
            stream = final_sum(stream, [own, swap(other)])
    return stream


def solution(mesh):
    in_specs = (
        P("band", None),
        P(("band", "head"), None),
        P("band", None),
        P("band"),
        P("band"),
        P(),
        P(None, "head"),
        P(None, None, "head"),
        P("head", None),
        P(None, None, None, "head"),
        P(None, "head", None),
        P(None, None, "head"),
        P(None, "head", None),
    )
    out_specs = P(("band", "head"), None)
    return jax.shard_map(shards, mesh=mesh, in_specs=in_specs, out_specs=out_specs, check_vma=False)
```

```python
import functools
import math

import jax
import jax.numpy as jnp
from jax import lax
from jax.experimental import pallas as pl
from jax.experimental.pallas import tpu as pltpu
from jax.sharding import PartitionSpec as P

HEAD_DIM = 64
K_MAX = 32
HALF_WIN = 512
LAYERS = 2
EDGE = 1536
KV_BLOCK = 512
BLOCK = 32
GROUP = 128
NODES_HERE = 512
KEYS = 7168
SCALE = 1.0 / math.sqrt(HEAD_DIM)
BF = jnp.bfloat16
F32 = jnp.float32
NT = (((1,), (1,)), ((), ()))


def vm(limit_mib=20):
    return pltpu.CompilerParams(vmem_limit_bytes=limit_mib * 1024 * 1024)


def cost(flops, nbytes):
    return pl.CostEstimate(flops=int(flops), bytes_accessed=int(nbytes), transcendentals=0)


def whole():
    return pl.BlockSpec(memory_space=pltpu.VMEM)


def hbm():
    return pl.BlockSpec(memory_space=pltpu.HBM)


def smem():
    return pl.BlockSpec(memory_space=pltpu.SMEM)


def sds(shape, dtype=BF):
    return jax.ShapeDtypeStruct(shape, dtype)


def swap(x):
    return lax.ppermute(x, "head", [(i, i ^ 1) for i in range(16)])


def shift_z(x, k):
    steps = (k, -k)
    return lax.ppermute(x, "head", [(i, ((i // 2 + steps[i % 2]) % 8) * 2 + i % 2) for i in range(16)])


def outward_pairs():
    return [(2 * z + c, 2 * ((z + (1 if c else -1)) % 8) + c) for z in range(8) for c in range(2)]


def outward(x):
    return lax.ppermute(x, "head", outward_pairs())


def inward(x):
    return lax.ppermute(x, "head", [(t, s) for s, t in outward_pairs()])


def crossed(x):
    pairs = [(2 * z, 2 * ((z - 1) % 8) + 1) for z in range(8)]
    return lax.ppermute(x, "head", pairs + [(t, s) for s, t in pairs])


def up_band(x):
    return lax.ppermute(x, "band", [(i, i + 1) for i in range(15)])


def down_band(x):
    return lax.ppermute(x, "band", [(i + 1, i) for i in range(15)])


def gather_group(x):
    behind = shift_z(x, 2)
    ahead = shift_z(x, -2)
    far = shift_z(x, 4)
    return [x, ahead, far, behind]


def scatter_group(parts):
    return [parts[0], shift_z(parts[1], 2), shift_z(parts[2], 4), shift_z(parts[3], -2)]


def four_shards(x):
    third = outward(x)
    return [x, swap(x), third, swap(third)]


def exchange(pieces):
    return [pieces[0], swap(pieces[1]), inward(pieces[2]), crossed(pieces[3])]


def give_back(pieces):
    return [pieces[0], swap(pieces[1]), outward(pieces[2]), crossed(pieces[3])]


def stack_kernel(b0, b1, b2, b3, out_ref):
    rows, cols = b0.shape[0], out_ref.shape[1]
    for k, b in enumerate((b0, b1, b2, b3)):
        out_ref[k * rows : (k + 1) * rows, :] = b[:, :cols]


def stack(blocks, cols):
    rows = blocks[0].shape[0]
    return pl.pallas_call(
        stack_kernel,
        in_specs=[whole()] * 4,
        out_specs=whole(),
        out_shape=sds((4 * rows, cols)),
        compiler_params=vm(),
        cost_estimate=cost(1e5, 4 * rows * cols * 4),
        name="stack",
    )(*blocks)


def normed_rows(values, gain):
    mean = jnp.mean(values, axis=-1, keepdims=True)
    centred = values - mean
    variance = jnp.mean(centred * centred, axis=-1, keepdims=True)
    return (centred * lax.rsqrt(variance + 1e-05) * gain).astype(BF)


def grid_kv_kernel(starts, first, x_ref, *refs):
    if first:
        gain_ref, w_ref, *refs = refs
    else:
        w_both, *refs = refs
    outs, refs = refs[: len(starts)], refs[len(starts) :]
    if first:
        w_both, *refs = refs
    rows, sems = refs
    blocks = outs[0].shape[0] // KV_BLOCK
    copies = [
        pltpu.make_async_copy(
            x_ref.at[pl.ds(start + i * KV_BLOCK, KV_BLOCK)],
            rows.at[part * blocks + i],
            sems.at[part * blocks + i],
        )
        for part, start in enumerate(starts)
        for i in range(blocks)
    ]
    for copy in copies:
        copy.start()
    if first:
        for i in range(2):
            turned = jnp.transpose(w_ref[i].astype(F32) * gain_ref[0:1, :]).astype(BF)
            w_both[:, i * HEAD_DIM : (i + 1) * HEAD_DIM] = turned
    for part, out in enumerate(outs):
        for i in range(blocks):
            copies[part * blocks + i].wait()

            x = rows[part * blocks + i].astype(F32)
            x = x - jnp.mean(x, axis=-1, keepdims=True)
            variance = jnp.mean(x * x, axis=-1, keepdims=True)
            scale = lax.rsqrt(variance + 1e-05)
            x = x.astype(BF)
            for line in range(0, KV_BLOCK, 128):
                kv = jnp.dot(x[line : line + 128], w_both[...], preferred_element_type=F32)
                at = i * KV_BLOCK + line
                out[at : at + 128, :] = (kv * scale[line : line + 128]).astype(BF)


def grid_kv(grid_latent, starts, count, gains=None, w=None, w_both=None):
    d = grid_latent.shape[1]
    blocks = len(starts) * count // KV_BLOCK
    first = w_both is None
    weight_shape = sds((d, 128))
    out_shape = [sds((count, 128))] * len(starts) + ([weight_shape] if first else [])
    return pl.pallas_call(
        functools.partial(grid_kv_kernel, starts, first),
        in_specs=[hbm()] + [whole()] * (2 if first else 1),
        out_specs=[whole()] * len(out_shape),
        out_shape=out_shape,
        scratch_shapes=[
            pltpu.VMEM((blocks, KV_BLOCK, d), BF),
            pltpu.SemaphoreType.DMA((blocks,)),
        ],
        compiler_params=vm(56),
        cost_estimate=cost(2 * blocks * KV_BLOCK * d * 128, blocks * KV_BLOCK * d * 2),
        name="grid_kv",
    )(grid_latent, *((gains, w) if first else (w_both,)))


COUNT_STEP = 64
TILES = KEYS // 128


def edge_count_kernel(place_ref, src_ref, degree_ref, out_ref, by_node, high_key, low_key):
    step = pl.program_id(0)

    @pl.when(step == 0)
    def _():
        shape = src_ref.shape
        local = src_ref[...] - (place_ref[0] * place_ref[2] - EDGE)
        used = lax.broadcasted_iota(jnp.int32, shape, 0) < degree_ref[...]
        by_node[...] = jnp.transpose(jnp.where(used, local, -1))
        for t in range(8):
            local_rows = by_node[pl.ds(t, NODES_HERE // 8, stride=8), :]
            cols = slice(t * K_MAX, (t + 1) * K_MAX)
            high_key[:, cols] = jnp.where(local_rows < 0, -1, (local_rows >> 7) * 8 + t)
            low_key[:, cols] = local_rows & 127

    row_high = lax.broadcasted_iota(jnp.int32, (TILES * 8, 256), 0)
    row_low = lax.broadcasted_iota(jnp.int32, (128, 256), 0)

    def counts(group):
        left = jnp.where(row_high == high_key[pl.ds(group, 1), :], 1.0, 0.0).astype(BF)
        right = jnp.where(row_low == low_key[pl.ds(group, 1), :], 1.0, 0.0).astype(BF)
        return lax.dot_general(left, right, NT, preferred_element_type=F32)

    def pair(i, carry):
        group = step * (COUNT_STEP // 8) + 2 * i
        first = counts(group)
        second = counts(group + 1)
        rows = pl.ds(pl.multiple_of(i * 16, 16), 16)
        for t in range(TILES):
            both = jnp.concatenate([first[t * 8 : t * 8 + 8], second[t * 8 : t * 8 + 8]], axis=0)
            out_ref[rows, t * 128 : (t + 1) * 128] = both.astype(BF)
        return carry

    lax.fori_loop(0, COUNT_STEP // 16, pair, 0, unroll=COUNT_STEP // 16)


def edge_counts(place, sources, degrees):
    return pl.pallas_call(
        edge_count_kernel,
        grid=(NODES_HERE // COUNT_STEP,),
        in_specs=[
            smem(),
            pl.BlockSpec(sources.shape, lambda i: (0, 0)),
            pl.BlockSpec(degrees.shape, lambda i: (0, 0)),
        ],
        out_specs=pl.BlockSpec((COUNT_STEP, KEYS), lambda i: (i, 0)),
        out_shape=sds((NODES_HERE, KEYS)),
        scratch_shapes=[
            pltpu.VMEM((NODES_HERE, K_MAX), jnp.int32),
            pltpu.VMEM((NODES_HERE // 8, 8 * K_MAX), jnp.int32),
            pltpu.VMEM((NODES_HERE // 8, 8 * K_MAX), jnp.int32),
        ],
        compiler_params=vm(),
        cost_estimate=cost(4e9, 10e6),
        name="edge_counts",
    )(place, sources, degrees)


def block_places(head):
    z, core = head // 2, head % 2
    side = 2 * core - 1
    places = []
    for g in range(4):
        from_z = z if g < 2 else z + side
        from_core = core if g % 2 == 0 else 1 - core
        step = 2 - 4 * from_core
        places += [2 * ((from_z + step * k + 16) & 7) + from_core for k in range(4)]
    return places


def row_positions(places):
    lane = lax.broadcasted_iota(jnp.int32, (1, NODES_HERE), 1)
    pos = jnp.zeros((1, NODES_HERE), jnp.int32)
    for i, place in enumerate(places):
        pos = jnp.where(lane // BLOCK == i, place * BLOCK + lane % BLOCK, pos)
    return pos


def node_query_kernel(place_ref, r0, r1, r2, r3, gain_ref, w_ref, order_ref, q_ref, mine_ref, order_col, rows):
    head = place_ref[1]
    places = block_places(head)
    for g, r in enumerate((r0, r1, r2, r3)):
        rows[g * GROUP : (g + 1) * GROUP, :] = r[...]
        normed = normed_rows(r[...].astype(F32), gain_ref[1:2, :])
        q = lax.dot_general(normed, w_ref[...], NT, preferred_element_type=F32).astype(BF)
        for k in range(4):
            start = pl.multiple_of(places[g * 4 + k] * BLOCK, BLOCK)
            q_ref[pl.ds(start, BLOCK), :] = q[k * BLOCK : (k + 1) * BLOCK, :]
    local = order_ref[...] - place_ref[0] * NODES_HERE
    order_col[...] = jnp.transpose(jnp.broadcast_to(local, (8, NODES_HERE)))
    wanted = order_col[pl.ds(pl.multiple_of(head * BLOCK, BLOCK), BLOCK), 0:1]
    pick = jnp.where(row_positions(places) == wanted, 1.0, 0.0).astype(BF)
    mine_ref[...] = jnp.dot(pick, rows[...], preferred_element_type=F32).astype(BF)


def node_queries(place, pieces, gains, wq_t, order):
    d = wq_t.shape[1]
    return pl.pallas_call(
        node_query_kernel,
        in_specs=[smem()] + [whole()] * 7,
        out_specs=[whole()] * 2,
        out_shape=[sds((NODES_HERE, HEAD_DIM)), sds((BLOCK, d))],
        scratch_shapes=[pltpu.VMEM((NODES_HERE, 8), jnp.int32), pltpu.VMEM((NODES_HERE, d), BF)],
        compiler_params=vm(),
        cost_estimate=cost(1e8, 2e6),
        name="node_queries",
    )(place, *pieces, gains, wq_t, order)


T_STEP = 256
CHUNK = 512


def edge_attention_kernel(
    place_ref, q_all, kv0, kv1, kv2, kv3, kv4, count_ref, order_ref,
    o0, o1, o2, o3, scores, heads, pick, order_col,
):
    step = pl.program_id(0)
    q = q_all[pl.ds(pl.multiple_of(step * T_STEP, T_STEP), T_STEP), :] * SCALE
    chunks = []
    for kv in (kv0, kv1, kv2, kv3, kv4):
        for start in range(0, kv.shape[0], CHUNK):
            chunks.append((kv, start))
    top = None
    for i, (kv, start) in enumerate(chunks):
        keys = kv[start : start + CHUNK, :][:, :HEAD_DIM]
        s = lax.dot_general(q, keys, NT, preferred_element_type=F32)
        cols = slice(i * CHUNK, (i + 1) * CHUNK)
        s = jnp.where(count_ref[:, cols].astype(F32) > 0.0, s, -jnp.inf)
        scores[:, cols] = s
        part = jnp.maximum(
            jnp.maximum(s[:, 0:128], s[:, 128:256]), jnp.maximum(s[:, 256:384], s[:, 384:512])
        )
        top = part if top is None else jnp.maximum(top, part)
    top = jnp.max(top, axis=-1, keepdims=True)
    total = jnp.zeros((T_STEP, 128), F32)
    out = jnp.zeros((T_STEP, 128), F32)
    for i, (kv, start) in enumerate(chunks):
        cols = slice(i * CHUNK, (i + 1) * CHUNK)
        e = jnp.exp(scores[:, cols] - top) * count_ref[:, cols].astype(F32)
        total += (e[:, 0:128] + e[:, 128:256]) + (e[:, 256:384] + e[:, 384:512])
        out += jnp.dot(e.astype(BF), kv[start : start + CHUNK, :], preferred_element_type=F32)
    total = jnp.sum(total, axis=-1, keepdims=True)
    rows = pl.ds(pl.multiple_of(step * T_STEP, T_STEP), T_STEP)
    heads[rows, :] = (out / total).astype(BF)

    @pl.when(step == pl.num_programs(0) - 1)
    def _():
        local = order_ref[...] - place_ref[0] * NODES_HERE
        order_col[...] = jnp.transpose(jnp.broadcast_to(local, (8, NODES_HERE)))
        places = block_places(place_ref[1])
        node = lax.broadcasted_iota(jnp.int32, (BLOCK, NODES_HERE), 1)
        for g, o in enumerate((o0, o1, o2, o3)):
            for k in range(4):
                start = pl.multiple_of(places[g * 4 + k] * BLOCK, BLOCK)
                wanted = order_col[pl.ds(start, BLOCK), 0:1]
                pick[k * BLOCK : (k + 1) * BLOCK, :] = jnp.where(node == wanted, 1.0, 0.0).astype(BF)
            taken = jnp.dot(pick[...], heads[...], preferred_element_type=F32)
            o[...] = taken[:, HEAD_DIM:].astype(BF)


def edge_attention(place, queries, kv_parts, counts, order):
    def full(x):
        return pl.BlockSpec(x.shape, lambda i: (0,) * x.ndim)

    return pl.pallas_call(
        edge_attention_kernel,
        grid=(NODES_HERE // T_STEP,),
        in_specs=[smem(), full(queries)]
        + [full(kv) for kv in kv_parts]
        + [pl.BlockSpec((T_STEP, KEYS), lambda i: (i, 0)), full(order)],
        out_specs=[pl.BlockSpec((GROUP, HEAD_DIM), lambda i: (0, 0))] * 4,
        out_shape=[sds((GROUP, HEAD_DIM))] * 4,
        scratch_shapes=[
            pltpu.VMEM((T_STEP, KEYS), F32),
            pltpu.VMEM((NODES_HERE, 128), BF),
            pltpu.VMEM((GROUP, NODES_HERE), BF),
            pltpu.VMEM((NODES_HERE, 8), jnp.int32),
        ],
        compiler_params=vm(40),
        cost_estimate=cost(2e9, 12e6),
        name="edge_attention",
    )(place, queries, *kv_parts, counts, order)


def head_sum_kernel(h0, h1, h2, h3, w0, w1, w2, w3, p0, p1, p2, p3):
    heads = jnp.concatenate([h0[...], h1[...], h2[...], h3[...]], axis=1)
    rows = jnp.concatenate([w0[...], w1[...], w2[...], w3[...]], axis=0)
    total = jnp.dot(heads, rows, preferred_element_type=F32).astype(BF)
    for k, p in enumerate((p0, p1, p2, p3)):
        p[...] = total[k * BLOCK : (k + 1) * BLOCK]


def head_sum(heads, shards, row_block):
    d = shards[0].shape[1]
    full = pl.BlockSpec((GROUP, HEAD_DIM), lambda i: (0, 0))
    return pl.pallas_call(
        head_sum_kernel,
        grid=(1,),
        in_specs=[full] * 4 + [pl.BlockSpec((HEAD_DIM, d), lambda i: (row_block, 0))] * 4,
        out_specs=[pl.BlockSpec((BLOCK, d), lambda i: (0, 0))] * 4,
        out_shape=[sds((BLOCK, d))] * 4,
        compiler_params=vm(),
        cost_estimate=cost(7e7, 1e6),
        name="head_sum",
    )(*heads, *shards)


def close_sum_kernel(gain_row, r_ref, p0, p1, p2, p3, gain_ref, stream_ref, normed_ref):
    total = (p0[...].astype(F32) + p1[...].astype(F32)) + (p2[...].astype(F32) + p3[...].astype(F32))
    stream = (r_ref[...].astype(F32) + total).astype(BF)
    stream_ref[...] = stream
    normed_ref[...] = normed_rows(stream.astype(F32), gain_ref[gain_row : gain_row + 1, :])


def close_sum(residual, parts, gains, gain_row):
    shape = residual.shape
    return pl.pallas_call(
        functools.partial(close_sum_kernel, gain_row),
        in_specs=[whole()] * 6,
        out_specs=[whole()] * 2,
        out_shape=[sds(shape), sds(shape)],
        compiler_params=vm(),
        cost_estimate=cost(1e6, 4e5),
        name="close_sum",
    )(residual, *parts, gains)


def final_sum_kernel(r_ref, p0, p1, stream_ref):
    total = p0[...].astype(F32) + p1[...].astype(F32)
    stream_ref[...] = (r_ref[...].astype(F32) + total).astype(BF)


def final_sum(residual, parts):
    return pl.pallas_call(
        final_sum_kernel,
        in_specs=[whole()] * 3,
        out_specs=whole(),
        out_shape=sds(residual.shape),
        compiler_params=vm(),
        cost_estimate=cost(1e6, 4e5),
        name="final_sum",
    )(residual, *parts)


def qkv_kernel(b0, b1, b2, b3, w0, w1, w2, w3, p0, p1, p2, p3):
    rows = jnp.concatenate([b0[...], b1[...], b2[...], b3[...]], axis=0)
    for w, out in ((w0, p0), (w1, p1), (w2, p2), (w3, p3)):
        all_cols = lax.dot_general(rows, w[...], NT, preferred_element_type=F32).astype(BF)
        out[:, :128] = all_cols[:, HEAD_DIM:]
        out[:, 128:] = all_cols[:, :HEAD_DIM]


def qkv(blocks, shards, layer):
    d = blocks[0].shape[1]
    return pl.pallas_call(
        qkv_kernel,
        grid=(1,),
        in_specs=[pl.BlockSpec((BLOCK, d), lambda i: (0, 0))] * 4
        + [pl.BlockSpec((3 * HEAD_DIM, d), lambda i: (layer, 0))] * 4,
        out_specs=[pl.BlockSpec((GROUP, 3 * HEAD_DIM), lambda i: (0, 0))] * 4,
        out_shape=[sds((GROUP, 3 * HEAD_DIM))] * 4,
        compiler_params=vm(),
        cost_estimate=cost(3e8, 2.5e6),
        name="qkv",
    )(*blocks, *shards)


def window_kernel(place_ref, a0, a1, a2, a3, kv_ref, low_ref, high_ref, out_ref):
    kv = kv_ref[...]
    low = low_ref[...]
    high = high_ref[...]
    has_low = place_ref[0] > 0
    has_high = place_ref[0] < place_ref[3] - 1
    places = block_places(place_ref[1])
    col = row_positions(places)
    line = lax.broadcasted_iota(jnp.int32, (GROUP, 1), 0)
    for g, a in enumerate((a0, a1, a2, a3)):
        q = a[:, 128:] * SCALE
        row = jnp.zeros((GROUP, 1), jnp.int32)
        for k in range(4):
            row = jnp.where(line // BLOCK == k, places[g * 4 + k] * BLOCK + line % BLOCK, row)
        s_own = lax.dot_general(q, kv[:, :HEAD_DIM], NT, preferred_element_type=F32)
        s_low = lax.dot_general(q, low[:, :HEAD_DIM], NT, preferred_element_type=F32)
        s_high = lax.dot_general(q, high[:, :HEAD_DIM], NT, preferred_element_type=F32)
        after = col >= row
        in_low = jnp.logical_and(after, has_low)
        in_high = jnp.logical_and(jnp.logical_not(after), has_high)
        s_far = jnp.where(in_low, s_low, jnp.where(in_high, s_high, -jnp.inf))
        top = jnp.maximum(
            jnp.max(s_own, axis=-1, keepdims=True), jnp.max(s_far, axis=-1, keepdims=True)
        )
        e_own = jnp.exp(s_own - top)
        e_far = jnp.exp(s_far - top)
        total = jnp.sum(e_own + e_far, axis=-1, keepdims=True)
        e_low = jnp.where(in_low, e_far, 0.0).astype(BF)
        e_high = jnp.where(in_high, e_far, 0.0).astype(BF)
        out = jnp.dot(e_own.astype(BF), kv, preferred_element_type=F32)
        out += jnp.dot(e_low, low, preferred_element_type=F32)
        out += jnp.dot(e_high, high, preferred_element_type=F32)
        heads = (out / total)[:, HEAD_DIM:].astype(BF)
        for k in range(4):
            out_ref[places[g * 4 + k]] = heads[k * BLOCK : (k + 1) * BLOCK]


def window_attention(place, pieces, kv, low, high):
    return pl.pallas_call(
        window_kernel,
        in_specs=[smem()] + [whole()] * 7,
        out_specs=whole(),
        out_shape=sds((NODES_HERE // BLOCK, BLOCK, HEAD_DIM)),
        compiler_params=vm(),
        cost_estimate=cost(4e8, 1e6),
        name="window_attention",
    )(place, *pieces, kv, low, high)


def one_layer_kernel(w_ref, out_ref):
    out_ref[...] = w_ref[:, 0].reshape(out_ref.shape)


def one_layer(wo_all, layer):
    count, _, rows, d = wo_all.shape
    return pl.pallas_call(
        one_layer_kernel,
        grid=(4,),
        in_specs=[pl.BlockSpec((count // 4, 1, rows, d), lambda i: (i, layer, 0, 0))],
        out_specs=pl.BlockSpec((count // 4 * rows, d), lambda i: (i, 0)),
        out_shape=sds((count * rows, d)),
        compiler_params=vm(),
        cost_estimate=cost(1e5, 2 * count * rows * d * 2),
        name="one_layer",
    )(wo_all)


def heads_to_stream_kernel(gain_row, heads_ref, wo_ref, r_ref, gain_ref, stream_ref, normed_ref):
    count = heads_ref.shape[0]
    heads = jnp.concatenate([heads_ref[h] for h in range(count)], axis=1)
    total = jnp.dot(heads, wo_ref[...], preferred_element_type=F32)
    stream = (r_ref[...].astype(F32) + total).astype(BF)
    stream_ref[...] = stream
    normed_ref[...] = normed_rows(stream.astype(F32), gain_ref[gain_row : gain_row + 1, :])


def heads_to_stream(heads, wo, residual, gains, gain_row):
    return pl.pallas_call(
        functools.partial(heads_to_stream_kernel, gain_row),
        in_specs=[whole()] * 4,
        out_specs=[whole()] * 2,
        out_shape=[sds(residual.shape)] * 2,
        compiler_params=vm(),
        cost_estimate=cost(7e7, 2.5e6),
        name="heads_to_stream",
    )(heads, wo, residual, gains)


def pack_kernel(layer, up_ref, down_ref, out_ref, sems):
    rows = down_ref.shape[1]
    copies = [
        pltpu.make_async_copy(
            up_ref.at[layer, q * rows : (q + 1) * rows],
            out_ref.at[:rows, q * rows : (q + 1) * rows],
            sems.at[q],
        )
        for q in range(4)
    ]
    copies.append(pltpu.make_async_copy(down_ref.at[layer], out_ref.at[rows:, :], sems.at[4]))
    for copy in copies:
        copy.start()
    for copy in copies:
        copy.wait()


def pack(w_up, w_down, layer):
    d, hidden = w_up.shape[1:]
    return pl.pallas_call(
        functools.partial(pack_kernel, layer),
        in_specs=[hbm(), hbm()],
        out_specs=whole(),
        out_shape=sds((2 * hidden, d)),
        scratch_shapes=[pltpu.SemaphoreType.DMA((5,))],
        compiler_params=vm(),
        cost_estimate=cost(1e5, 2e6),
        name="pack",
    )(w_up, w_down)


def feed_forward_kernel(b0, b1, b2, b3, w0, w1, w2, w3, p0, p1, p2, p3):
    rows = jnp.concatenate([b0[...], b1[...], b2[...], b3[...]], axis=0)
    total = None
    for w in (w0, w1, w2, w3):
        hidden = w.shape[0] // 2
        up = None
        for q in range(4):
            cols = slice(q * hidden, (q + 1) * hidden)
            part = jnp.dot(rows[:, cols], w[:hidden, cols], preferred_element_type=F32)
            up = part if up is None else up + part
        part = jnp.dot(jax.nn.gelu(up).astype(BF), w[hidden:, :], preferred_element_type=F32)
        total = part if total is None else total + part
    total = total.astype(BF)
    for k, p in enumerate((p0, p1, p2, p3)):
        p[...] = total[k * BLOCK : (k + 1) * BLOCK]


def feed_forward(blocks, shards):
    d = blocks[0].shape[1]
    return pl.pallas_call(
        feed_forward_kernel,
        in_specs=[whole()] * 8,
        out_specs=[whole()] * 4,
        out_shape=[sds((BLOCK, d))] * 4,
        compiler_params=vm(),
        cost_estimate=cost(5e8, 5e6),
        name="feed_forward",
    )(*blocks, *shards)


def pair_feed_forward_kernel(mine_ref, other_ref, w_ref, own_ref, send_ref, total, held, sems):
    count = held.shape[0]
    hidden = held.shape[1] * 16

    def copy(i):
        return pltpu.make_async_copy(w_ref.at[:, i], held.at[i], sems.at[i])

    for i in range(count):
        copy(i).start()
    rows = jnp.concatenate([mine_ref[...], other_ref[...]], axis=0)
    total[...] = jnp.zeros_like(total)

    def shard(i, carry):
        copy(i).wait()
        up = None
        for q in range(4):
            cols = slice(q * 256, (q + 1) * 256)
            weight = held[i, :, :16, cols].reshape(256, hidden)
            part = jnp.dot(rows[:, cols], weight, preferred_element_type=F32)
            up = part if up is None else up + part
        weight = held[i, :, 16:, :].reshape(hidden, rows.shape[1])
        total[...] += jnp.dot(jax.nn.gelu(up).astype(BF), weight, preferred_element_type=F32)
        return carry

    lax.fori_loop(0, count, shard, 0)
    own_ref[...] = total[:BLOCK, :].astype(BF)
    send_ref[...] = total[BLOCK:, :].astype(BF)


def pair_feed_forward(mine, other, weights):
    d = mine.shape[1]
    bands, count = weights.shape[:2]
    return pl.pallas_call(
        pair_feed_forward_kernel,
        in_specs=[whole(), whole(), hbm()],
        out_specs=[whole()] * 2,
        out_shape=[sds((BLOCK, d))] * 2,
        scratch_shapes=[
            pltpu.VMEM((2 * BLOCK, d), F32),
            pltpu.VMEM((count, bands, 32, d), BF),
            pltpu.SemaphoreType.DMA((count,)),
        ],
        compiler_params=vm(50),
        cost_estimate=cost(5e8, 9e6),
        name="pair_feed_forward",
    )(mine, other, weights)


def sixteenth_kernel(layer, place_ref, up_ref, down_ref, out_ref, sems):
    band = place_ref[0]
    copies = [
        pltpu.make_async_copy(
            up_ref.at[layer, q, band], out_ref.at[:16, q * 256 : (q + 1) * 256], sems.at[q]
        )
        for q in range(4)
    ]
    rows = pl.ds(pl.multiple_of(band * 16, 16), 16)
    copies.append(pltpu.make_async_copy(down_ref.at[layer, rows], out_ref.at[16:, :], sems.at[4]))
    for copy in copies:
        copy.start()
    for copy in copies:
        copy.wait()


def sixteenth(place, w_up, w_down, layer):
    d, hidden = w_up.shape[1:]
    return pl.pallas_call(
        functools.partial(sixteenth_kernel, layer),
        in_specs=[smem(), hbm(), hbm()],
        out_specs=whole(),
        out_shape=sds((32, d)),
        scratch_shapes=[pltpu.SemaphoreType.DMA((5,))],
        compiler_params=vm(63),
        cost_estimate=cost(1e5, 2e5),
        name="sixteenth",
    )(place, w_up.reshape(-1, 4, 16, 16, hidden), w_down)


def one_parity_kernel(place_ref, all_ref, out_ref, sems):
    core = place_ref[1] % 2
    copies = [
        pltpu.make_async_copy(all_ref.at[2 * i + core], out_ref.at[i], sems.at[i])
        for i in range(out_ref.shape[0])
    ]
    for copy in copies:
        copy.start()
    for copy in copies:
        copy.wait()


def one_parity(place, over_head):
    count, rows, d = over_head.shape
    return pl.pallas_call(
        one_parity_kernel,
        in_specs=[smem(), pl.BlockSpec(memory_space=pl.ANY)],
        out_specs=pl.BlockSpec(memory_space=pl.ANY),
        out_shape=sds((count // 2, rows, d)),
        scratch_shapes=[pltpu.SemaphoreType.DMA((count // 2,))],
        compiler_params=vm(),
        cost_estimate=cost(1e5, count * rows * d * 2),
        name="one_parity",
    )(place, over_head)


def shards(
    grid_latent,
    node_latent,
    src_index,
    in_degree,
    node_order,
    norm_gains,
    enc_wq,
    enc_wkv,
    enc_wo,
    proc_wqkv,
    proc_wo,
    w_up,
    w_down,
):
    d = grid_latent.shape[1]
    band = lax.axis_index("band")
    head = lax.axis_index("head")
    place = jnp.stack([band, head, grid_latent.shape[0], lax.axis_size("band")]).astype(jnp.int32)
    order = node_order[None, :]

    barrier = lax.optimization_barrier
    wo_all = lax.all_gather(proc_wo, "head")
    qkv_t = jnp.swapaxes(proc_wqkv, 2, 3).reshape(-1, d)

    tall = jnp.concatenate([qkv_t, enc_wo], axis=0)

    node_blocks = gather_group(node_latent)
    wkv_t = jnp.swapaxes(enc_wkv, 1, 2)
    grid_rows = grid_latent.shape[0]
    edge_low, edge_high, w_both = grid_kv(
        grid_latent, (0, grid_rows - EDGE), EDGE, gains=norm_gains, w=wkv_t
    )
    node_blocks, edge_low, edge_high = barrier((node_blocks, edge_low, edge_high))
    node_group = stack(node_blocks, d)
    node_pieces = exchange([node_group] * 4)
    from_low = up_band(edge_high)
    from_high = down_band(edge_low)
    w_up, w_down, grid_latent, _ = barrier((w_up, w_down, grid_latent, node_group))
    late_part = sixteenth(place, w_up, w_down, 1)
    middle = grid_kv(grid_latent, (EDGE,), grid_rows - 2 * EDGE, w_both=w_both)[0]
    sources, middle, late_part = barrier((src_index.T, middle, late_part))
    counts = edge_counts(place, sources, in_degree[None, :])
    node_pieces, counts, from_low, from_high, tall = barrier((node_pieces, counts, from_low, from_high, tall))

    tall_third, tall_other = outward(tall), swap(tall)
    queries, residual = node_queries(place, node_pieces, norm_gains, enc_wq.T, order)
    kv_parts = [from_low, edge_low, middle, edge_high, from_high]
    enc_heads = edge_attention(place, queries, kv_parts, counts, order)
    enc_heads, tall_third, tall_other, late_part, wo_all = barrier(
        (enc_heads, tall_third, tall_other, late_part, wo_all)
    )
    late_weights = lax.all_gather(late_part, "head")
    tall_shards = [tall, tall_other, tall_third, swap(tall_third)]
    sums = head_sum(give_back(enc_heads), tall_shards, qkv_t.shape[0] // HEAD_DIM)
    stream, normed = close_sum(residual, scatter_group(sums), norm_gains, 2)

    for layer in range(LAYERS):
        blocks = gather_group(normed)
        if layer == 0:
            w_up, w_down, _ = barrier((w_up, w_down, normed))
            blocks, first = barrier((blocks, pack(w_up, w_down, 0)))
        pieces = exchange(qkv(blocks, tall_shards, layer))
        kv = stack(pieces, 2 * HEAD_DIM)
        low = up_band(kv)
        high = down_band(kv)
        wo_all, _ = barrier((wo_all, kv))
        wo = one_layer(wo_all, layer)
        low, high, wo = barrier((low, high, wo))
        if layer == 0:
            first, late_weights, _ = barrier((first, late_weights, kv))
            first_third, first_other = outward(first), swap(first)
            low, high, first_third, first_other = barrier((low, high, first_third, first_other))
        win_heads = window_attention(place, pieces, kv, low, high)
        if layer == 0:
            win_heads, late_weights = barrier((win_heads, late_weights))
            late_weights = lax.all_gather(one_parity(place, late_weights), "band")
            first_shards = [first, first_other, first_third, swap(first_third)]
        win_heads = lax.all_to_all(win_heads, "head", 0, 0)
        stream, normed = heads_to_stream(win_heads, wo, stream, norm_gains, 3 + 2 * layer)
        if layer == 0:
            parts = scatter_group(feed_forward(gather_group(normed), first_shards))
            stream, normed = close_sum(stream, parts, norm_gains, 4 + 2 * layer)
        else:
            own, other = pair_feed_forward(normed, swap(normed), late_weights)
            stream = final_sum(stream, [own, swap(other)])
    return stream


def solution(mesh):
    in_specs = (
        P("band", None),
        P(("band", "head"), None),
        P("band", None),
        P("band"),
        P("band"),
        P(),
        P(None, "head"),
        P(None, None, "head"),
        P("head", None),
        P(None, None, None, "head"),
        P(None, "head", None),
        P(None, None, "head"),
        P(None, "head", None),
    )
    out_specs = P(("band", "head"), None)
    return jax.shard_map(shards, mesh=mesh, in_specs=in_specs, out_specs=out_specs, check_vma=False)
```
